32 devices in a mesh: shard: 4 (over z), context: 4 (over y, x), tensor: 2 (over core).
Axes of the slice: x: 2, y: 2, z: 4, core: 2. Of those that a mesh axis runs over, the one named last changes fastest.
Arguments:
- hidden_in: bfloat16 [4, 1024, 2560], P('shard', 'context'), may hold values from -6 to 6
- out_grad: bfloat16 [4, 1024, 2560], P('shard', 'context'), may hold values from -6 to 6
- prefix_len: int32 [4], P('shard'), may hold values from 102 to 512
- qkv_weight: float32 [2560, 3840], P(('shard', 'context'), 'tensor'), may hold values from -0.15625 to 0.15625
- qkv_m: float32 [2560, 3840], P(('shard', 'context'), 'tensor'), may hold values from -7.6293945e-05 to 7.6293945e-05
- qkv_v: float32 [2560, 3840], P(('shard', 'context'), 'tensor'), may hold values from 7.3678363e-10 to 2.9471345e-09
- out_weight: float32 [2560, 2560], P(('shard', 'context'), 'tensor'), may hold values from -0.5 to 0.5
- out_m: float32 [2560, 2560], P(('shard', 'context'), 'tensor'), may hold values from -7.6293945e-05 to 7.6293945e-05
- out_v: float32 [2560, 2560], P(('shard', 'context'), 'tensor'), may hold values from 7.3678363e-10 to 2.9471345e-09
- gate_up_weight: float32 [2560, 2, 7168], P(('shard', 'context'), None, 'tensor'), may hold values from -0.125 to 0.125
- gate_up_m: float32 [2560, 2, 7168], P(('shard', 'context'), None, 'tensor'), may hold values from -7.6293945e-05 to 7.6293945e-05
- gate_up_v: float32 [2560, 2, 7168], P(('shard', 'context'), None, 'tensor'), may hold values from 7.3678363e-10 to 2.9471345e-09
- down_weight: float32 [2560, 7168], P(('shard', 'context'), 'tensor'), may hold values from -0.0625 to 0.0625
- down_m: float32 [2560, 7168], P(('shard', 'context'), 'tensor'), may hold values from -7.6293945e-05 to 7.6293945e-05
- down_v: float32 [2560, 7168], P(('shard', 'context'), 'tensor'), may hold values from 7.3678363e-10 to 2.9471345e-09
- gains: float32 [2, 2560], P(None, ('shard', 'context')), may hold values from 0.3 to 1.95
- gains_m: float32 [2, 2560], P(None, ('shard', 'context')), may hold values from -0.00024414062 to 0.00024414062
- gains_v: float32 [2, 2560], P(None, ('shard', 'context')), may hold values from 6.6310526e-09 to 2.652421e-08
Outputs:
- hidden_out: bfloat16 [4, 1024, 2560], P('shard', 'context')
- hidden_grad: bfloat16 [4, 1024, 2560], P('shard', 'context')
- grad_norm: float32 [], replicated
- qkv_m_new: float32 [2560, 3840], P(('shard', 'context'), 'tensor')
- qkv_v_new: float32 [2560, 3840], P(('shard', 'context'), 'tensor')
- qkv_new: float32 [2560, 3840], P(('shard', 'context'), 'tensor')
- out_m_new: float32 [2560, 2560], P(('shard', 'context'), 'tensor')
- out_v_new: float32 [2560, 2560], P(('shard', 'context'), 'tensor')
- out_new: float32 [2560, 2560], P(('shard', 'context'), 'tensor')
- gate_up_m_new: float32 [2560, 2, 7168], P(('shard', 'context'), None, 'tensor')
- gate_up_v_new: float32 [2560, 2, 7168], P(('shard', 'context'), None, 'tensor')
- gate_up_new: float32 [2560, 2, 7168], P(('shard', 'context'), None, 'tensor')
- down_m_new: float32 [2560, 7168], P(('shard', 'context'), 'tensor')
- down_v_new: float32 [2560, 7168], P(('shard', 'context'), 'tensor')
- down_new: float32 [2560, 7168], P(('shard', 'context'), 'tensor')
- gains_m_new: float32 [2, 2560], P(None, ('shard', 'context'))
- gains_v_new: float32 [2, 2560], P(None, ('shard', 'context'))
- gains_new: float32 [2, 2560], P(None, ('shard', 'context'))
The draws below stay inside these ranges and needn't reach their ends.
Inputs may be any that keep to these rules, and one draw needn't show every extreme that they name: `prefix_len`: each sequence's bidirectional prefix holds 102 to 512 positions.
All inputs are finite; a program needn't handle non-finite values.
Results may differ from the reference program's by a relative error of at most 0.019.
The reference program's roundings to bfloat16 on the way count: a program that leaves them out, or rounds other values in their place, can miss the bound.
Values may be sent and summed in bfloat16 or wider, within the bound.
A program may use at most 320 MiB of HBM per device.

```python
import math
import jax
import jax.numpy as jnp
from jax import lax

D = 2560
H = 32
KV = 8
HD = 80
FF = 7168
LEN = 1024
STEP = 8
QKV_COLS = 3840
PARAMS = 71434240
SEQS = 4


def draw_gains(key, part):
    start, finish = (0.45, 1.5)
    along = jnp.arange(D, dtype=jnp.float32) / float(max(D - 1, 1))
    ramp = start + (finish - start) * along
    rough = 1.0 + 0.1 * jax.random.uniform(key, (2, D), jnp.float32, -1.0, 1.0)
    return (ramp[None, :] * rough).astype(jnp.float32)


def set_ends(array, key, low, largest):
    dims = array.shape
    place = [jax.random.randint(jax.random.fold_in(key, axis), (), 0, dims[axis]) for axis in range(len(dims))]
    array = array.at[tuple(place)].set(low)
    longest = dims.index(max(dims))
    place[longest] = (place[longest] + 1) % dims[longest]
    return array.at[tuple(place)].set(largest)


def steps_of(rng, shape, pieces, smallest, largest):
    def one(position, parts):
        steps = jax.random.uniform(jax.random.fold_in(jax.random.fold_in(rng, 6), position), (parts,), jnp.float32, smallest / len(pieces), largest / len(pieces))
        return jnp.repeat(jnp.exp(steps), shape[position] // parts).reshape((-1,) + (1,) * (len(shape) - position - 1))

    loudness = one(*pieces[0])
    for cut in pieces[1:]:
        loudness = loudness * one(*cut)
    return loudness


def noise(rng, shape, width, limit, pieces=(), kind=jnp.bfloat16):
    loudness = steps_of(rng, shape, pieces, -0.22, 0.18) if pieces else 1.0
    values = jax.random.normal(rng, shape, jnp.float32) * width * loudness
    return jnp.minimum(jnp.maximum(values, -limit), limit).astype(kind)


def setup_inputs(seed: int = 0) -> dict:
    arg_keys = jax.random.split(jax.random.key(seed), 19)
    hidden_in = noise(arg_keys[0], (SEQS, LEN, D), 1.0, 6.0, ((0, 4), (1, 4)))
    out_grad = noise(arg_keys[1], (SEQS, LEN, D), 1.0, 6.0, ((0, 4), (1, 4)))
    prefix_len = set_ends(jax.random.randint(arg_keys[2], (SEQS,), LEN // 10, LEN // 2 + 1), jax.random.fold_in(arg_keys[2], 1), LEN // 10, (LEN // 2 + 1) - 1).astype(jnp.int32)
    qkv_weight = noise(arg_keys[3], (D, QKV_COLS), (D // 2) ** -0.5, 0.15625, ((0, 16), (1, 2)), jnp.float32)
    qkv_m = noise(arg_keys[4], (D, QKV_COLS), ((81 * PARAMS) ** -0.5), 7.62939453125e-05, ((0, 16), (1, 2)), jnp.float32)
    qkv_v = jnp.clip(jnp.exp(math.log(2.947134536412932e-09) - 1.3862944 * jax.random.uniform(arg_keys[5], (D, QKV_COLS), jnp.float32) ** steps_of(arg_keys[5], (D, QKV_COLS), ((0, 16), (1, 2)), -0.2, 0.2)), 7.36783634103233e-10, 2.947134536412932e-09)
    out_weight = noise(arg_keys[6], (D, H * HD), (H * HD // 16) ** -0.5, 0.5, ((0, 16), (1, 2)), jnp.float32)
    out_m = noise(arg_keys[7], (D, H * HD), ((81 * PARAMS) ** -0.5), 7.62939453125e-05, ((0, 16), (1, 2)), jnp.float32)
    out_v = jnp.clip(jnp.exp(math.log(2.947134536412932e-09) - 1.3862944 * jax.random.uniform(arg_keys[8], (D, H * HD), jnp.float32) ** steps_of(arg_keys[8], (D, H * HD), ((0, 16), (1, 2)), -0.2, 0.2)), 7.36783634103233e-10, 2.947134536412932e-09)
    gate_up_weight = noise(arg_keys[9], (D, 2, FF), D ** -0.5, 0.125, ((0, 16), (2, 2)), jnp.float32)
    gate_up_m = noise(arg_keys[10], (D, 2, FF), ((81 * PARAMS) ** -0.5), 7.62939453125e-05, ((0, 16), (2, 2)), jnp.float32)
    gate_up_v = jnp.clip(jnp.exp(math.log(2.947134536412932e-09) - 1.3862944 * jax.random.uniform(arg_keys[11], (D, 2, FF), jnp.float32) ** steps_of(arg_keys[11], (D, 2, FF), ((0, 16), (2, 2)), -0.2, 0.2)), 7.36783634103233e-10, 2.947134536412932e-09)
    down_weight = noise(arg_keys[12], (D, FF), FF ** -0.5, 0.0625, ((0, 16), (1, 2)), jnp.float32)
    down_m = noise(arg_keys[13], (D, FF), ((81 * PARAMS) ** -0.5), 7.62939453125e-05, ((0, 16), (1, 2)), jnp.float32)
    down_v = jnp.clip(jnp.exp(math.log(2.947134536412932e-09) - 1.3862944 * jax.random.uniform(arg_keys[14], (D, FF), jnp.float32) ** steps_of(arg_keys[14], (D, FF), ((0, 16), (1, 2)), -0.2, 0.2)), 7.36783634103233e-10, 2.947134536412932e-09)
    gains = draw_gains(jax.random.fold_in(arg_keys[18], 71), 0)
    gains_m = noise(arg_keys[16], (2, D), ((9 * PARAMS) ** -0.5), 0.00024414062, ((1, 16),), jnp.float32)
    gains_v = jnp.clip(jnp.exp(math.log(2.6524210383627178e-08) - 1.3862944 * jax.random.uniform(arg_keys[17], (2, D), jnp.float32) ** steps_of(arg_keys[17], (2, D), ((1, 16),), -0.2, 0.2)), 6.6310525959067945e-09, 2.6524210383627178e-08)
    return dict(hidden_in=hidden_in, out_grad=out_grad, prefix_len=prefix_len, qkv_weight=qkv_weight, qkv_m=qkv_m, qkv_v=qkv_v, out_weight=out_weight, out_m=out_m, out_v=out_v, gate_up_weight=gate_up_weight, gate_up_m=gate_up_m, gate_up_v=gate_up_v, down_weight=down_weight, down_m=down_m, down_v=down_v, gains=gains, gains_m=gains_m, gains_v=gains_v)


@jax.custom_vjp
def low(v):
    return lax.optimization_barrier(v.astype(jnp.bfloat16)).astype(jnp.float32)

@jax.custom_vjp
def low_back(v):
    return v

def low_keep(v):
    return (low(v), None)

def low_pass(kept, grad):
    return (grad,)

def back_keep(v):
    return (v, None)

def back_low(kept, grad):
    return (low(grad),)
low.defvjp(low_keep, low_pass)
low_back.defvjp(back_keep, back_low)
norm_epsilon = 1e-05
rope_theta = 1000000.0
masked_score = -1e+30
clip_limit = 1.0
beta_first = 0.9
beta_second = 0.95
adam_epsilon = 1e-08
weight_decay = 0.1
highest = lax.Precision.HIGHEST

def rms_scale(values):
    return values * lax.rsqrt(lax.optimization_barrier(jnp.mean(values * values, axis=-1, keepdims=True)) + norm_epsilon)

def rope_tables(positions):
    half = HD // 2
    exponent = jnp.arange(half, dtype=jnp.float32) * (2.0 / HD)
    frequency = rope_theta ** (-exponent)
    angles = positions.astype(jnp.float32)[:, None] * frequency[None, :]
    angles = jnp.concatenate([angles, angles], axis=-1)
    return (jnp.cos(angles), jnp.sin(angles))

def rotate(values, cosine, sine):
    half = values.shape[-1] // 2
    turned = jnp.concatenate([-values[..., half:], values[..., :half]], axis=-1)
    return values * cosine + turned * sine

def adam_step(weight, first, second, grad, factor, rate, decay):
    grad = grad * factor
    first_new = beta_first * first + (1.0 - beta_first) * grad
    second_new = beta_second * second + (1.0 - beta_second) * grad * grad
    corrected = first_new / (1.0 - beta_first ** STEP) / (jnp.sqrt(second_new / (1.0 - beta_second ** STEP)) + adam_epsilon)
    return (first_new, second_new, weight - rate * (corrected + decay * weight))

def forward(inputs, qkv_w, out_w, gate_up_w, down_w, gain_rows, prefix):
    batch = inputs.shape[0]
    group = H // KV
    normed_one = low(rms_scale(inputs) * low(gain_rows[0]))
    joined = low_back(jnp.einsum('bld,dc->blc', normed_one, low(qkv_w), precision=highest))
    joined = joined.reshape(batch, LEN, KV, group + 2, HD)
    positions = jnp.arange(LEN, dtype=jnp.int32)
    cosine, sine = rope_tables(positions)
    query = low(rotate(joined[:, :, :, :group], cosine[None, :, None, None], sine[None, :, None, None]))
    key = low(rotate(joined[:, :, :, group], cosine[None, :, None], sine[None, :, None]))
    value = low(joined[:, :, :, group + 1])
    allowed = (positions[None, None, :] <= positions[None, :, None]) | (positions[None, None, :] < prefix[:, None, None])

    def head_group(operands):
        query_block, key_block, value_block = operands
        scores = jnp.einsum('bigh,bjh->bgij', query_block, key_block, precision=highest) * HD ** (-0.5)
        scores = low_back(jnp.where(allowed[:, None], scores, masked_score))
        probs = low(jax.nn.softmax(scores, axis=-1))
        return jnp.einsum('bgij,bjh->bigh', probs, value_block, precision=highest)
    mixed = lax.map(jax.checkpoint(head_group), (jnp.moveaxis(query, 2, 0), jnp.moveaxis(key, 2, 0), jnp.moveaxis(value, 2, 0)))
    attended = low(low_back(jnp.moveaxis(mixed, 0, 2).reshape(batch, LEN, H * HD)))
    middle = inputs + low_back(jnp.einsum('blc,dc->bld', attended, low(out_w), precision=highest))
    normed_two = low(rms_scale(middle) * low(gain_rows[1]))
    gate_up = low_back(jnp.einsum('bld,dkf->blkf', normed_two, low(gate_up_w), precision=highest))
    hidden = low(jax.nn.silu(gate_up[:, :, 0]) * gate_up[:, :, 1])
    return middle + low_back(jnp.einsum('blf,df->bld', hidden, low(down_w), precision=highest))

def reference(hidden_in, out_grad, prefix_len, qkv_weight, qkv_m, qkv_v, out_weight, out_m, out_v, gate_up_weight, gate_up_m, gate_up_v, down_weight, down_m, down_v, gains, gains_m, gains_v):
    per_step = 4 if SEQS % 4 == 0 else 2 if SEQS % 2 == 0 else 1
    blocks = SEQS // per_step
    weights = (qkv_weight, out_weight, gate_up_weight, down_weight, gains)
    inputs = hidden_in.astype(jnp.float32).reshape(blocks, per_step, LEN, D)
    cotangent = out_grad.astype(jnp.float32).reshape(blocks, per_step, LEN, D)
    prefixes = prefix_len.astype(jnp.int32).reshape(blocks, per_step)

    def step(totals, operands):
        input_block, cot_block, prefix_block = operands

        def apply(input_rows, qkv_w, out_w, gate_up_w, down_w, gain_rows):
            return forward(input_rows, qkv_w, out_w, gate_up_w, down_w, gain_rows, prefix_block)
        result, pullback = jax.vjp(apply, input_block, *weights)
        grads = pullback(cot_block)
        totals = tuple((total + grad for total, grad in zip(totals, grads[1:])))
        return (totals, (result, grads[0]))
    zeros = tuple((jnp.zeros_like(weight) for weight in weights))
    totals, (results, input_grads) = lax.scan(step, zeros, (inputs, cotangent, prefixes))
    squares = sum((jnp.sum(grad * grad) for grad in totals))
    grad_norm = jnp.sqrt(squares)
    factor = jnp.minimum(1.0, clip_limit / grad_norm)
    qkv_out = adam_step(qkv_weight, qkv_m, qkv_v, totals[0], factor, 2.0 * (D / 2) ** (-0.5), weight_decay)
    out_out = adam_step(out_weight, out_m, out_v, totals[1], factor, 2.0 * (H * HD / 16) ** (-0.5), weight_decay)
    gate_up_out = adam_step(gate_up_weight, gate_up_m, gate_up_v, totals[2], factor, 2.0 * D ** (-0.5), weight_decay)
    down_out = adam_step(down_weight, down_m, down_v, totals[3], factor, 2.0 * FF ** (-0.5), weight_decay)
    gains_out = adam_step(gains, gains_m, gains_v, totals[4], factor, 0.8, 0.0)
    hidden_out = results.reshape(SEQS, LEN, D).astype(jnp.bfloat16)
    hidden_grad = input_grads.reshape(SEQS, LEN, D).astype(jnp.bfloat16)
    return (hidden_out, hidden_grad, grad_norm, qkv_out[0], qkv_out[1], qkv_out[2], out_out[0], out_out[1], out_out[2], gate_up_out[0], gate_up_out[1], gate_up_out[2], down_out[0], down_out[1], down_out[2], gains_out[0], gains_out[1], gains_out[2])
```

```python
import jax
import jax.numpy as jnp
from jax import lax
from jax.sharding import PartitionSpec as P

D = 2560
H = 32
KV = 8
HD = 80
FF = 7168
STEP = 8


norm_epsilon = 1e-05
rope_theta = 1000000.0
masked_score = -1e30
clip_limit = 1.0
beta_first = 0.9
beta_second = 0.95
adam_epsilon = 1e-08
weight_decay = 0.1


def rope_tables(positions):
    half = HD // 2
    exponent = jnp.arange(half, dtype=jnp.float32) * (2.0 / HD)
    frequency = rope_theta ** (-exponent)
    angles = positions.astype(jnp.float32)[:, None] * frequency[None, :]
    angles = jnp.concatenate([angles, angles], axis=-1)
    return (jnp.cos(angles), jnp.sin(angles))


def rotate(values, cosine, sine):
    half = values.shape[-1] // 2
    turned = jnp.concatenate([-values[..., half:], values[..., :half]], axis=-1)
    return values * cosine + turned * sine


def unrotate(values, cosine, sine):
    half = values.shape[-1] // 2
    turned = jnp.concatenate([-values[..., half:], values[..., :half]], axis=-1)
    return values * cosine - turned * sine


def normalize(values):
    factor = lax.rsqrt(jnp.mean(values * values, axis=-1, keepdims=True) + norm_epsilon)
    return (values * factor, factor)


def norm_back(grad_scaled, scaled, factor):
    return factor * (grad_scaled - scaled * jnp.mean(grad_scaled * scaled, axis=-1, keepdims=True))


def adam_step(weight, first, second, grad, factor, rate, decay):
    grad = grad * factor
    first_new = beta_first * first + (1.0 - beta_first) * grad
    second_new = beta_second * second + (1.0 - beta_second) * grad * grad
    corrected = (
        first_new
        / (1.0 - beta_first**STEP)
        / (jnp.sqrt(second_new / (1.0 - beta_second**STEP)) + adam_epsilon)
    )
    return (first_new, second_new, weight - rate * (corrected + decay * weight))


def xor_pairs(axis, k):
    return [(i, i ^ k) for i in range(lax.axis_size(axis))]


def spread(rows, axis):
    blocks = [rows]
    for k in range(1, lax.axis_size(axis)):
        blocks.append(lax.ppermute(rows, axis, xor_pairs(axis, k)))
    other = [lax.ppermute(block, "tensor", [(0, 1), (1, 0)]) for block in blocks]
    return jnp.concatenate(blocks + other, axis=0)


def collect(partial, axis):
    size = lax.axis_size(axis)
    half = partial.shape[0] // 2
    own = half // size
    mate = lax.ppermute(partial[half:].astype(jnp.bfloat16), "tensor", [(0, 1), (1, 0)])
    total = partial[:half] + mate.astype(jnp.float32)
    result = total[:own]
    low = total.astype(jnp.bfloat16)
    for k in range(1, size):
        piece = lax.ppermute(low[k * own : (k + 1) * own], axis, xor_pairs(axis, k))
        result = result + piece.astype(jnp.float32)
    return result


def swap_blocks(blocks, axis):
    me = lax.axis_index(axis)
    result = blocks
    for k in range(1, lax.axis_size(axis)):
        piece = lax.dynamic_index_in_dim(blocks, me ^ k, 0, keepdims=True)
        piece = lax.ppermute(piece, axis, xor_pairs(axis, k))
        result = lax.dynamic_update_slice_in_dim(result, piece, me ^ k, 0)
    return result


def sum_blocks(blocks, axis):
    me = lax.axis_index(axis)
    result = lax.dynamic_index_in_dim(blocks, me, 0, keepdims=False)
    for k in range(1, lax.axis_size(axis)):
        piece = lax.dynamic_index_in_dim(blocks, me ^ k, 0, keepdims=False)
        result = result + lax.ppermute(piece, axis, xor_pairs(axis, k))
    return result


def all_blocks(value, axis):
    me = lax.axis_index(axis)
    result = jnp.zeros((lax.axis_size(axis),) + value.shape, value.dtype)
    result = lax.dynamic_update_slice_in_dim(result, value[None], me, 0)
    for k in range(1, lax.axis_size(axis)):
        piece = lax.ppermute(value, axis, xor_pairs(axis, k))
        result = lax.dynamic_update_slice_in_dim(result, piece[None], me ^ k, 0)
    return result


def sum_over(value, axis):
    result = value
    for k in range(1, lax.axis_size(axis)):
        result = result + lax.ppermute(value, axis, xor_pairs(axis, k))
    return result


def attend(query, key, value, allowed):
    scores = jnp.einsum("ih,jh->ij", query, key, preferred_element_type=jnp.float32) * HD ** (-0.5)
    scores = jnp.where(allowed, scores, masked_score)
    row_max = jnp.max(scores, axis=-1, keepdims=True)
    expanded = jnp.exp(scores - row_max)
    row_total = jnp.sum(expanded, axis=-1, keepdims=True)
    probs = (expanded / row_total).astype(jnp.bfloat16)
    mixed = jnp.einsum("ij,jh->ih", probs, value, preferred_element_type=jnp.float32)
    return mixed, row_max + jnp.log(row_total)


def attend_back(query, key, value, grad, log_total, allowed):
    scores = jnp.einsum("ih,jh->ij", query, key, preferred_element_type=jnp.float32) * HD ** (-0.5)
    scores = jnp.where(allowed, scores, masked_score)
    probs = jnp.exp(scores - log_total)
    grad_value = jnp.einsum("ij,ih->jh", probs.astype(jnp.bfloat16), grad, preferred_element_type=jnp.float32)
    grad_probs = jnp.einsum("ih,jh->ij", grad, value, preferred_element_type=jnp.float32)
    delta = jnp.sum(probs * grad_probs, axis=-1, keepdims=True)
    grad_scores = (probs * (grad_probs - delta)).astype(jnp.bfloat16)
    grad_query = jnp.einsum("ij,jh->ih", grad_scores, key, preferred_element_type=jnp.float32) * HD ** (-0.5)
    grad_key = jnp.einsum("ij,ih->jh", grad_scores, query, preferred_element_type=jnp.float32) * HD ** (-0.5)
    return grad_query, grad_key, grad_value


def body(
    hidden_in,
    out_grad,
    prefix_len,
    qkv_weight,
    qkv_m,
    qkv_v,
    out_weight,
    out_m,
    out_v,
    gate_up_weight,
    gate_up_m,
    gate_up_v,
    down_weight,
    down_m,
    down_v,
    gains,
    gains_m,
    gains_v,
):
    _, local_len, width = hidden_in.shape
    shards, contexts, tensors = (lax.axis_size(a) for a in ("shard", "context", "tensor"))
    context = lax.axis_index("context")
    tensor = lax.axis_index("tensor")
    rows = qkv_weight.shape[0]
    group = H // KV
    head_cols = (group + 2) * HD
    own = local_len // tensors
    ff_block = down_weight.shape[1] // shards
    low = jnp.bfloat16

    def attn_columns(weight):
        blocks = weight.astype(low).reshape(rows, contexts, -1)
        blocks = swap_blocks(jnp.moveaxis(blocks, 1, 0), "context")
        return lax.all_gather(blocks.reshape(contexts * rows, -1), "shard", axis=0, tiled=True)

    def mlp_columns(blocks):
        blocks = swap_blocks(blocks, "shard")
        return lax.all_gather(blocks.reshape(shards * rows, -1), "context", axis=0, tiled=True)

    qkv_full = attn_columns(qkv_weight)
    out_full = attn_columns(out_weight)
    gate_up_full = mlp_columns(
        gate_up_weight.astype(low)
        .reshape(rows, 2, shards, ff_block)
        .transpose(2, 0, 1, 3)
        .reshape(shards, rows, 2 * ff_block)
    )
    down_full = mlp_columns(jnp.moveaxis(down_weight.astype(low).reshape(rows, shards, ff_block), 1, 0))

    def to_mlp_order(values):
        return jnp.swapaxes(values.reshape(-1, shards, contexts, rows), 1, 2).reshape(-1, width)

    def from_mlp_order(values):
        return jnp.swapaxes(values.reshape(-1, contexts, shards, rows), 1, 2).reshape(-1, width)

    gain_blocks = all_blocks(all_blocks(gains.astype(low).astype(jnp.float32), "context"), "shard")
    gain_rows = gain_blocks.reshape(shards * contexts, 2, rows).transpose(1, 0, 2).reshape(2, width)
    gain_attn, gain_mlp = gain_rows[0], gain_rows[1]

    inputs = lax.dynamic_slice_in_dim(hidden_in[0], tensor * own, own, 0).astype(jnp.float32)
    grad_low = lax.dynamic_slice_in_dim(out_grad[0], tensor * own, own, 0)
    cotangent = grad_low.astype(jnp.float32)

    scaled_one, factor_one = normalize(inputs)
    normed_one = spread((scaled_one * gain_attn).astype(low), "context")
    places = jnp.arange(contexts, dtype=jnp.int32) ^ context
    cores = jnp.arange(tensors, dtype=jnp.int32) ^ tensor
    positions = (
        places[None, :, None] * local_len
        + cores[:, None, None] * own
        + jnp.arange(own, dtype=jnp.int32)[None, None, :]
    ).reshape(-1)
    cosine, sine = rope_tables(positions)
    allowed = (positions[None, :] <= positions[:, None]) | (positions[None, :] < prefix_len[0])

    joined = jnp.dot(normed_one, qkv_full, preferred_element_type=jnp.float32)
    parts = [joined[:, i * HD : (i + 1) * HD] for i in range(group + 2)]
    queries = [rotate(part, cosine, sine).astype(low) for part in parts[:group]]
    key = rotate(parts[group], cosine, sine).astype(low)
    value = parts[group + 1].astype(low)

    mixed, log_total = zip(*[attend(query, key, value, allowed) for query in queries])
    attended = jnp.concatenate([part.astype(low) for part in mixed], axis=1)
    branch = collect(jnp.einsum("tc,dc->td", attended, out_full, preferred_element_type=jnp.float32), "context")
    middle = inputs + branch
    scaled_two, factor_two = normalize(middle)
    normed_two = spread(to_mlp_order((scaled_two * gain_mlp).astype(low)), "shard")
    grad_branch_mlp = spread(to_mlp_order(grad_low), "shard")

    gate_up = jnp.dot(normed_two, gate_up_full, preferred_element_type=jnp.float32)
    gate = gate_up[:, :ff_block]
    up_part = gate_up[:, ff_block:]
    sigmoid_gate = jax.nn.sigmoid(gate)
    activated = gate * sigmoid_gate
    hidden = (activated * up_part).astype(low)
    grad_down = jnp.einsum("td,tf->df", grad_branch_mlp, hidden, preferred_element_type=jnp.float32)
    grad_hidden = jnp.dot(grad_branch_mlp, down_full, preferred_element_type=jnp.float32)
    grad_gate = grad_hidden * up_part * sigmoid_gate * (1.0 + gate * (1.0 - sigmoid_gate))
    grad_up = grad_hidden * activated
    grad_rows = jnp.concatenate([grad_gate, grad_up], axis=1).astype(low)
    grad_normed_two = from_mlp_order(
        collect(jnp.einsum("tf,df->td", grad_rows, gate_up_full, preferred_element_type=jnp.float32), "shard")
    )
    grad_gate_up = jnp.einsum("td,tf->df", normed_two, grad_rows, preferred_element_type=jnp.float32)
    mlp_branch = from_mlp_order(
        collect(jnp.einsum("tf,df->td", hidden, down_full, preferred_element_type=jnp.float32), "shard")
    )
    out_own = (middle + mlp_branch).astype(low)

    grad_gain_mlp = jnp.sum(grad_normed_two * scaled_two, axis=0)
    grad_middle = cotangent + norm_back(grad_normed_two * gain_mlp, scaled_two, factor_two)
    grad_branch_attn = spread(grad_middle.astype(low), "context")
    grad_out = jnp.einsum("td,tc->dc", grad_branch_attn, attended, preferred_element_type=jnp.float32)
    grad_attended = jnp.dot(grad_branch_attn, out_full, preferred_element_type=jnp.float32).astype(low)

    grad_queries = []
    grad_key = 0.0
    grad_value = 0.0
    for i in range(group):
        grad_query, key_part, value_part = attend_back(
            queries[i], key, value, grad_attended[:, i * HD : (i + 1) * HD], log_total[i], allowed
        )
        grad_queries.append(unrotate(grad_query, cosine, sine))
        grad_key = grad_key + key_part
        grad_value = grad_value + value_part
    grad_joined = jnp.concatenate(
        grad_queries + [unrotate(grad_key, cosine, sine), grad_value], axis=1
    ).astype(low)
    grad_qkv = jnp.einsum("td,tc->dc", normed_one, grad_joined, preferred_element_type=jnp.float32)
    grad_normed_one = collect(
        jnp.einsum("tc,dc->td", grad_joined, qkv_full, preferred_element_type=jnp.float32), "context"
    )
    grad_gain_attn = jnp.sum(grad_normed_one * scaled_one, axis=0)
    grad_inputs = grad_middle + norm_back(grad_normed_one * gain_attn, scaled_one, factor_one)
    grad_own = grad_inputs.astype(low)

    def both_cores(values):
        other = lax.ppermute(values, "tensor", [(0, 1), (1, 0)])
        return jnp.where(tensor == 0, jnp.concatenate([values, other]), jnp.concatenate([other, values]))[None]

    hidden_out = both_cores(out_own)
    hidden_grad = both_cores(grad_own)

    down_sum = lax.psum_scatter(grad_down.astype(low), "context", scatter_dimension=0, tiled=True)
    gate_up_sum = lax.psum_scatter(grad_gate_up.astype(low), "context", scatter_dimension=0, tiled=True)
    out_sum = lax.psum_scatter(grad_out.astype(low), "shard", scatter_dimension=0, tiled=True)
    qkv_sum = lax.psum_scatter(grad_qkv.astype(low), "shard", scatter_dimension=0, tiled=True)
    gain_sum = sum_over(jnp.stack([grad_gain_attn, grad_gain_mlp]), "tensor")
    gain_sum = jnp.moveaxis(gain_sum.reshape(2, shards, contexts, rows), 0, 2)
    owned_gains = sum_blocks(sum_blocks(gain_sum, "shard"), "context")

    squares = jnp.sum(owned_gains * owned_gains) / tensors
    for total in (down_sum, gate_up_sum, out_sum, qkv_sum):
        total = total.astype(jnp.float32)
        squares = squares + jnp.sum(total * total)
    for axis in ("tensor", "context", "shard"):
        squares = sum_over(squares, axis)
    grad_norm = jnp.sqrt(squares)
    factor = jnp.minimum(1.0, clip_limit / grad_norm)

    def attn_rows(total):
        blocks = swap_blocks(total.reshape(contexts, rows, -1), "context")
        return jnp.moveaxis(blocks, 0, 1).reshape(rows, -1).astype(jnp.float32)

    def mlp_rows(total):
        return swap_blocks(total.reshape(shards, rows, -1), "shard")

    owned_qkv = attn_rows(qkv_sum)
    owned_out = attn_rows(out_sum)
    owned_down = jnp.moveaxis(mlp_rows(down_sum), 0, 1).reshape(rows, -1).astype(jnp.float32)
    owned_gate_up = (
        mlp_rows(gate_up_sum)
        .reshape(shards, rows, 2, ff_block)
        .transpose(1, 2, 0, 3)
        .reshape(rows, 2, shards * ff_block)
        .astype(jnp.float32)
    )
    qkv_out = adam_step(
        qkv_weight, qkv_m, qkv_v, owned_qkv, factor, 2.0 * (D / 2) ** (-0.5), weight_decay
    )
    out_out = adam_step(
        out_weight, out_m, out_v, owned_out, factor, 2.0 * (H * HD / 16) ** (-0.5), weight_decay
    )
    gate_up_out = adam_step(
        gate_up_weight, gate_up_m, gate_up_v, owned_gate_up, factor, 2.0 * D ** (-0.5), weight_decay
    )
    down_out = adam_step(
        down_weight, down_m, down_v, owned_down, factor, 2.0 * FF ** (-0.5), weight_decay
    )
    gains_out = adam_step(gains, gains_m, gains_v, owned_gains, factor, 0.8, 0.0)
    return (
        hidden_out,
        hidden_grad,
        grad_norm,
        *qkv_out,
        *out_out,
        *gate_up_out,
        *down_out,
        *gains_out,
    )


def solution(mesh):
    return jax.shard_map(
        body,
        mesh=mesh,
        in_specs=(
            P("shard", "context", None),
            P("shard", "context", None),
            P("shard"),
            P(("shard", "context"), "tensor"),
            P(("shard", "context"), "tensor"),
            P(("shard", "context"), "tensor"),
            P(("shard", "context"), "tensor"),
            P(("shard", "context"), "tensor"),
            P(("shard", "context"), "tensor"),
            P(("shard", "context"), None, "tensor"),
            P(("shard", "context"), None, "tensor"),
            P(("shard", "context"), None, "tensor"),
            P(("shard", "context"), "tensor"),
            P(("shard", "context"), "tensor"),
            P(("shard", "context"), "tensor"),
            P(None, ("shard", "context")),
            P(None, ("shard", "context")),
            P(None, ("shard", "context")),
        ),
        out_specs=(
            P("shard", "context", None),
            P("shard", "context", None),
            P(),
            P(("shard", "context"), "tensor"),
            P(("shard", "context"), "tensor"),
            P(("shard", "context"), "tensor"),
            P(("shard", "context"), "tensor"),
            P(("shard", "context"), "tensor"),
            P(("shard", "context"), "tensor"),
            P(("shard", "context"), None, "tensor"),
            P(("shard", "context"), None, "tensor"),
            P(("shard", "context"), None, "tensor"),
            P(("shard", "context"), "tensor"),
            P(("shard", "context"), "tensor"),
            P(("shard", "context"), "tensor"),
            P(None, ("shard", "context")),
            P(None, ("shard", "context")),
            P(None, ("shard", "context")),
        ),
        check_vma=False,
    )
```

```python
import functools

import jax
import jax.numpy as jnp
from jax import lax
from jax.experimental import pallas as pl
from jax.experimental.pallas import tpu as pltpu
from jax.sharding import Mesh
from jax.sharding import PartitionSpec as P

D = 2560
H = 32
KV = 8
HD = 80
FF = 7168
STEP = 8


norm_epsilon = 1e-05
rope_theta = 1000000.0
masked_score = -1e30
clip_limit = 1.0
beta_first = 0.9
beta_second = 0.95
adam_epsilon = 1e-08
weight_decay = 0.1

HIGH, LOW, CONTEXT, TENSOR = "high", "low", "context", "tensor"
SHARD = (HIGH, LOW)
AXES = (HIGH, LOW, CONTEXT, TENSOR)
SWAP, STACK, SPREAD, COLLECT = "swap", "stack", "spread", "collect"
MLP_GROUP = (CONTEXT,)
MLP_GATHER = (HIGH, LOW)
MESH = pl.DeviceIdType.MESH
low = jnp.bfloat16
full = jnp.float32


def rope_tables(positions):
    half = HD // 2
    exponent = jnp.arange(half, dtype=full) * (2.0 / HD)
    frequency = rope_theta ** (-exponent)
    angles = positions.astype(full)[:, None] * frequency[None, :]
    angles = jnp.concatenate([angles, angles], axis=-1)
    return (jnp.cos(angles), jnp.sin(angles))


def rotate(values, cosine, sine):
    half = values.shape[-1] // 2
    turned = jnp.concatenate([-values[..., half:], values[..., :half]], axis=-1)
    return values * cosine + turned * sine


def unrotate(values, cosine, sine):
    half = values.shape[-1] // 2
    turned = jnp.concatenate([-values[..., half:], values[..., :half]], axis=-1)
    return values * cosine - turned * sine


def normalize(values):
    factor = lax.rsqrt(jnp.mean(values * values, axis=-1, keepdims=True) + norm_epsilon)
    return (values * factor, factor)


def norm_back(grad_scaled, scaled, factor):
    return factor * (grad_scaled - scaled * jnp.mean(grad_scaled * scaled, axis=-1, keepdims=True))


def adam_step(weight, first, second, grad, factor, rate, decay):
    grad = grad * factor
    first_new = beta_first * first + (1.0 - beta_first) * grad
    second_new = beta_second * second + (1.0 - beta_second) * grad * grad
    corrected = (
        first_new
        / (1.0 - beta_first**STEP)
        / (jnp.sqrt(second_new / (1.0 - beta_second**STEP)) + adam_epsilon)
    )
    return (first_new, second_new, weight - rate * (corrected + decay * weight))


def over(left_dim, right_dim, left, right):
    return lax.dot_general(left, right, (((left_dim,), (right_dim,)), ((), ())), preferred_element_type=full)


rows_by_cols = functools.partial(over, 1, 0)
rows_by_rows = functools.partial(over, 1, 1)
cols_by_cols = functools.partial(over, 0, 0)


class Link:
    def __init__(self, sizes, send, recv):
        self.sizes, self.send, self.recv, self.used = sizes, send, recv, 0
        self.place = tuple(lax.axis_index(axis) for axis in AXES)

    def device(self, offset):
        return {axis: here ^ by for axis, here, by in zip(AXES, self.place, offset)}

    def index(self, group):
        index = 0
        for axis, here in zip(AXES, self.place):
            if axis in group:
                index = index * self.sizes[axis] + here
        return index

    def greet(self, partners):
        barrier = pltpu.get_barrier_semaphore()
        for offset in partners:
            pl.semaphore_signal(barrier, inc=1, device_id=self.device(offset), device_id_type=MESH)
        pl.semaphore_wait(barrier, len(partners))

    def push(self, src, dst, offset):
        copy = pltpu.make_async_remote_copy(
            src_ref=src,
            dst_ref=dst,
            send_sem=self.send.at[self.used],
            recv_sem=self.recv.at[self.used],
            device_id=self.device(offset),
            device_id_type=MESH,
        )
        self.used += 1
        copy.start()
        return copy

    def keep(self, src, dst):
        copy = pltpu.make_async_copy(src, dst, self.send.at[self.used])
        self.used += 1
        copy.start()
        return copy


MATE = (0, 0, 0, 1)


def axis_sizes():
    return {axis: lax.axis_size(axis) for axis in AXES}


def size_of(sizes, group):
    size = 1
    for axis in group:
        size *= sizes[axis]
    return size


def along(sizes, group, k):
    offset = []
    for axis in reversed(AXES):
        by = 0
        if axis in group:
            k, by = divmod(k, sizes[axis])
        offset.append(by)
    return tuple(reversed(offset))


def partners_of(jobs, sizes):
    found = set()
    for job in jobs:
        for group in job[1:]:
            found |= {along(sizes, group, k) for k in range(1, size_of(sizes, group))}
        if job[0] in (SPREAD, COLLECT):
            found.add(MATE)
    return sorted(found)


def bundle_kernel(jobs, sizes, *refs):
    refs = list(refs)
    take = lambda count: [refs.pop(0) for _ in range(count)]
    sources = [take(2 if job[0] == COLLECT else 1) for job in jobs]
    targets = [take(1)[0] for job in jobs]
    extras = [take(2 if job[0] == COLLECT else 0) for job in jobs]
    link = Link(sizes, *refs)
    link.greet(partners_of(jobs, sizes))
    ends, crossing, pieces = [], {}, {}
    for number, (job, source, dst) in enumerate(zip(jobs, sources, targets)):
        src, kind, group = source[-1], job[0], job[-1]
        n, me = size_of(sizes, group), link.index(group)
        if kind == SWAP:
            for k in range(1, n):
                ends.append(link.push(src.at[me ^ k], dst.at[me], along(sizes, group, k)))
            ends.append(link.keep(src.at[me], dst.at[me]))
        elif kind == STACK:
            slot = dst.at[link.index(job[1]), me]
            pieces[number] = [link.push(src, slot, along(sizes, group, k)) for k in range(1, n)]
            pieces[number].append(link.keep(src, slot))
        elif kind == SPREAD:
            pieces[number] = [link.push(src, dst.at[0, k], along(sizes, group, k)) for k in range(1, n)]
            ends.append(link.push(src, dst.at[1, 0], MATE))
            ends.append(link.keep(src, dst.at[0, 0]))
        else:
            mates = extras[number][0]
            order = list(range(1, n)) + [0]
            crossing[number] = {k: link.push(src.at[k], mates.at[k], MATE) for k in order}
    for number, copies in crossing.items():
        near, (mates, got), group = sources[number][0], extras[number], jobs[number][-1]
        pieces[number] = []
        for k in range(1, size_of(sizes, group)):
            copies[k].wait_recv()
            mates[k] = (near[k] + mates[k].astype(full)).astype(low)
            pieces[number].append(link.push(mates.at[k], got.at[k - 1], along(sizes, group, k)))
        copies[0].wait_recv()
        targets[number][...] = near[0] + mates[0].astype(full)
    for number, job in enumerate(jobs):
        dst = targets[number]
        if job[0] == STACK:
            for piece in pieces[number]:
                piece.wait()
            row = dst.at[link.index(job[1])]
            for k in range(1, size_of(sizes, job[1])):
                ends.append(link.push(row, row, along(sizes, job[1], k)))
        elif job[0] == SPREAD:
            for k, piece in enumerate(pieces[number]):
                piece.wait_recv()
                ends.append(link.push(dst.at[0, k + 1], dst.at[1, k + 1], MATE))
            for piece in pieces[number]:
                piece.wait_send()
    for number, copies in crossing.items():
        got = extras[number][1]
        for k, piece in enumerate(pieces[number]):
            piece.wait_recv()
            targets[number][...] += got[k].astype(full)
        for piece in pieces[number] + list(copies.values()):
            piece.wait_send()
    for end in ends:
        end.wait()


def whole_in_vmem():
    return pl.BlockSpec(memory_space=pltpu.VMEM)


def talking(number, mib):
    return pltpu.CompilerParams(collective_id=number, has_side_effects=True, vmem_limit_bytes=mib * 2**20)


def bundle(number, micros, *jobs):
    sizes = axis_sizes()
    anywhere = pl.BlockSpec(memory_space=pl.ANY)
    flat, in_specs, out_specs, shapes, scratch, copies = [], [], [], [], [], 0
    for *job, array in jobs:
        kind, n = job[0], size_of(sizes, job[-1])
        if kind == COLLECT:
            near, far = array
            flat += [near, far]
            in_specs += [whole_in_vmem(), anywhere]
            out_specs.append(whole_in_vmem())
            shapes.append(jax.ShapeDtypeStruct(near.shape[1:], full))
            scratch += [pltpu.VMEM(far.shape, low), pltpu.VMEM((n - 1,) + far.shape[1:], low)]
            copies += 2 * n
            continue
        flat.append(array)
        in_specs.append(anywhere)
        out_specs.append(anywhere)
        shape = array.shape
        if kind == SWAP:
            copies += n
        elif kind == STACK:
            shape = (size_of(sizes, job[1]), n) + shape
            copies += shape[0] + n
        else:
            shape = (2, n) + shape
            copies += 2 * n
        shapes.append(jax.ShapeDtypeStruct(shape, array.dtype))
    return pl.pallas_call(
        functools.partial(bundle_kernel, tuple(tuple(job[:-1]) for job in jobs), sizes),
        out_shape=shapes,
        in_specs=in_specs,
        out_specs=out_specs,
        scratch_shapes=scratch + [pltpu.SemaphoreType.DMA((copies,)), pltpu.SemaphoreType.DMA((copies,))],
        compiler_params=talking(number, 56),
        cost_estimate=pl.CostEstimate(flops=int(micros * 3e8), bytes_accessed=0, transcendentals=0),
    )(*flat)


def halves(products, group):
    n = lax.axis_size(group)
    half = products[0][0].shape[0] // 2

    def part(start):
        total = 0.0
        for left, right in products:
            total = total + rows_by_rows(left[start : start + half], right)
        return total.reshape(n, half // n, -1)

    return part(0), part(half).astype(low)


def total_kernel(sizes, squares_ref, total_ref, held, send, recv):
    link = Link(sizes, send, recv)
    groups = ((TENSOR,), (CONTEXT,), SHARD)
    link.greet([along(sizes, group, k) for group in groups for k in range(1, size_of(sizes, group))])
    total_ref[...] = squares_ref[...]
    slot = 0
    for group in groups:
        n = size_of(sizes, group)
        held[slot] = total_ref[...]
        pushes = [link.push(held.at[slot], held.at[slot + k], along(sizes, group, k)) for k in range(1, n)]
        for push in pushes:
            push.wait()
        for k in range(1, n):
            total_ref[...] += held[slot + k]
        slot += n


def total_over(squares, number):
    sizes = axis_sizes()
    slots = sizes[TENSOR] + sizes[CONTEXT] + size_of(sizes, SHARD)
    tile = jnp.full((8, 128), squares, full)
    total = pl.pallas_call(
        functools.partial(total_kernel, sizes),
        out_shape=jax.ShapeDtypeStruct(tile.shape, tile.dtype),
        in_specs=[whole_in_vmem()],
        out_specs=whole_in_vmem(),
        scratch_shapes=[
            pltpu.VMEM((slots,) + tile.shape, full),
            pltpu.SemaphoreType.DMA((slots,)),
            pltpu.SemaphoreType.DMA((slots,)),
        ],
        compiler_params=talking(number, 16),
    )(tile)
    return total[0, 0]


def fold_kernel(sizes, part_ref, sum_ref, work, mates, outers, inners, send, recv):
    link = Link(sizes, send, recv)
    groups = ((TENSOR,), (CONTEXT,), SHARD)
    link.greet([along(sizes, group, k) for group in groups for k in range(1, size_of(sizes, group))])
    s, c = link.index(SHARD), link.index((CONTEXT,))
    push = link.push(part_ref, mates, MATE)
    push.wait()
    work[...] = part_ref[...] + mates[...]
    shards, contexts = size_of(sizes, SHARD), sizes[CONTEXT]
    pushes = [link.push(work.at[s ^ k], outers.at[k], along(sizes, SHARD, k)) for k in range(1, shards)]
    outers[0] = work[s]
    for push in pushes:
        push.wait()
    for k in range(1, shards):
        outers[0] += outers[k]
    group = (CONTEXT,)
    pushes = [link.push(outers.at[0, c ^ k], inners.at[k], along(sizes, group, k)) for k in range(1, contexts)]
    sum_ref[...] = outers[0, c]
    for push in pushes:
        push.wait()
    for k in range(1, contexts):
        sum_ref[...] += inners[k]


def fold(part, number):
    sizes = axis_sizes()
    slots = sizes[TENSOR] + sizes[CONTEXT] + size_of(sizes, SHARD)
    return pl.pallas_call(
        functools.partial(fold_kernel, sizes),
        out_shape=jax.ShapeDtypeStruct(part.shape[2:], full),
        in_specs=[whole_in_vmem()],
        out_specs=whole_in_vmem(),
        scratch_shapes=[
            pltpu.VMEM(part.shape, full),
            pltpu.VMEM(part.shape, full),
            pltpu.VMEM(part.shape, full),
            pltpu.VMEM(part.shape[1:], full),
            pltpu.SemaphoreType.DMA((slots,)),
            pltpu.SemaphoreType.DMA((slots,)),
        ],
        compiler_params=talking(number, 16),
    )(part)


def adam_kernel(rate, decay, factor_ref, weight_ref, first_ref, second_ref, grad_ref, first_out, second_out, weight_out):
    first, second, weight = adam_step(
        weight_ref[...], first_ref[...], second_ref[...], grad_ref[...], factor_ref[0], rate, decay
    )
    first_out[...] = first
    second_out[...] = second
    weight_out[...] = weight


def adam_paired(weight, first, second, grad, factor, rate, decay):
    rows = weight.shape[0]
    step = 16 if rows % 16 == 0 else 8
    block = pl.BlockSpec((step,) + weight.shape[1:], lambda i: (i, 0, 0))
    return pl.pallas_call(
        functools.partial(adam_kernel, rate, decay),
        grid=(rows // step,),
        out_shape=[jax.ShapeDtypeStruct(weight.shape, weight.dtype)] * 3,
        in_specs=[pl.BlockSpec(memory_space=pltpu.SMEM)] + [block] * 4,
        out_specs=[block] * 3,
        compiler_params=pltpu.CompilerParams(vmem_limit_bytes=48 * 2**20),
    )(factor.reshape(1), weight, first, second, grad)


def attend(query, key, value, allowed):
    scores = rows_by_rows(query, key) * HD ** (-0.5)
    scores = jnp.where(allowed, scores, masked_score)
    row_max = jnp.max(scores, axis=-1, keepdims=True)
    expanded = jnp.exp(scores - row_max)
    row_total = jnp.sum(expanded, axis=-1, keepdims=True)
    probs = (expanded / row_total).astype(low)
    return rows_by_cols(probs, value), row_max + jnp.log(row_total)


def attend_back(query, key, value, grad, log_total, allowed):
    scores = rows_by_rows(query, key) * HD ** (-0.5)
    scores = jnp.where(allowed, scores, masked_score)
    probs = jnp.exp(scores - log_total)
    grad_value = cols_by_cols(probs.astype(low), grad)
    grad_probs = rows_by_rows(grad, value)
    delta = jnp.sum(probs * grad_probs, axis=-1, keepdims=True)
    grad_scores = (probs * (grad_probs - delta)).astype(low)
    grad_query = rows_by_cols(grad_scores, key) * HD ** (-0.5)
    grad_key = cols_by_cols(grad_scores, query) * HD ** (-0.5)
    return grad_query, grad_key, grad_value


def body(
    hidden_in,
    out_grad,
    prefix_len,
    qkv_weight,
    qkv_m,
    qkv_v,
    out_weight,
    out_m,
    out_v,
    gate_up_weight,
    gate_up_m,
    gate_up_v,
    down_weight,
    down_m,
    down_v,
    gains,
    gains_m,
    gains_v,
):
    _, local_len, width = hidden_in.shape
    shards, contexts, tensors = (lax.axis_size(group) for group in (SHARD, CONTEXT, TENSOR))
    context, tensor = lax.axis_index(CONTEXT), lax.axis_index(TENSOR)
    group_size = lax.axis_size(MLP_GROUP)
    rows = qkv_weight.shape[0]
    group = H // KV
    head_cols = (group + 2) * HD
    own = local_len // tensors
    ff_block = down_weight.shape[1] // group_size
    ff_first = ff_block // 2 // 128 * 128 or ff_block // 2
    chunks = ((0, ff_first), (ff_first, ff_block))

    def to_blocks(weight, count):
        return jnp.moveaxis(weight.astype(low).reshape(rows, count, -1), 1, 0)

    def lay(blocks):
        return jnp.moveaxis(blocks, 0, 1).reshape(rows, -1).astype(full)

    attn_part, gain_blocks = bundle(
        0,
        24,
        (
            SWAP,
            (CONTEXT,),
            jnp.concatenate([to_blocks(qkv_weight, contexts), to_blocks(out_weight, contexts)], axis=2),
        ),
        (STACK, SHARD, (CONTEXT,), gains.astype(low).astype(full)),
    )
    attn_full = lax.all_gather(attn_part.reshape(contexts * rows, -1), SHARD, axis=0, tiled=True)
    qkv_full, out_full = attn_full[:, :head_cols], attn_full[:, head_cols:]
    gain_rows = gain_blocks.reshape(shards * contexts, 2, rows).transpose(1, 0, 2).reshape(2, width)
    gain_attn, gain_mlp = gain_rows[0], gain_rows[1]
    inputs = lax.dynamic_slice_in_dim(hidden_in[0], tensor * own, own, 0).astype(full)
    grad_low = lax.dynamic_slice_in_dim(out_grad[0], tensor * own, own, 0)
    cotangent = grad_low.astype(full)
    scaled_one, factor_one = normalize(inputs)

    gate_up_blocks = gate_up_weight.astype(low).reshape(rows, 2, group_size, ff_block).transpose(2, 0, 1, 3)
    down_blocks = to_blocks(down_weight, group_size)

    def chunk_blocks(start, stop):
        pair = gate_up_blocks[:, :, :, start:stop]
        return jnp.concatenate([pair[:, :, 0], pair[:, :, 1], down_blocks[:, :, start:stop]], axis=2)

    def gather_mlp(part):
        return lax.all_gather(part.reshape(group_size * rows, -1), MLP_GATHER, axis=0, tiled=True)

    normed_one, part_one = bundle(
        1,
        60,
        (SPREAD, (CONTEXT,), (scaled_one * gain_attn).astype(low)),
        (SWAP, MLP_GROUP, chunk_blocks(*chunks[0])),
    )
    normed_one = normed_one.reshape(-1, width)
    mlp_full = [gather_mlp(part_one)]

    places = jnp.arange(contexts, dtype=jnp.int32) ^ context
    cores = jnp.arange(tensors, dtype=jnp.int32) ^ tensor
    positions = (
        places[None, :, None] * local_len
        + cores[:, None, None] * own
        + jnp.arange(own, dtype=jnp.int32)[None, None, :]
    ).reshape(-1)
    cosine, sine = rope_tables(positions)
    allowed = (positions[None, :] <= positions[:, None]) | (positions[None, :] < prefix_len[0])

    joined = rows_by_cols(normed_one, qkv_full)
    parts = [joined[:, i * HD : (i + 1) * HD] for i in range(group + 2)]
    queries = [rotate(part, cosine, sine).astype(low) for part in parts[:group]]
    key = rotate(parts[group], cosine, sine).astype(low)
    value = parts[group + 1].astype(low)
    mixed, log_total = zip(*[attend(query, key, value, allowed) for query in queries])
    attended = jnp.concatenate([part.astype(low) for part in mixed], axis=1)
    branch, part_two, grad_branch_mlp = bundle(
        2,
        80,
        (COLLECT, (CONTEXT,), halves([(attended, out_full)], (CONTEXT,))),
        (SWAP, MLP_GROUP, chunk_blocks(*chunks[1])),
        (SPREAD, MLP_GROUP, grad_low),
    )
    grad_branch_mlp = grad_branch_mlp.reshape(-1, width)
    mlp_full.append(gather_mlp(part_two))
    middle = inputs + branch
    scaled_two, factor_two = normalize(middle)
    (normed_two,) = bundle(3, 40, (SPREAD, MLP_GROUP, (scaled_two * gain_mlp).astype(low)))
    normed_two = normed_two.reshape(-1, width)

    sums, back_products, out_products = [], [], []
    for place, (start, stop) in enumerate(chunks):
        size = stop - start
        weights = mlp_full[place]
        pair_weights, down_weights = weights[:, : 2 * size], weights[:, 2 * size :]
        gate_up = rows_by_cols(normed_two, pair_weights)
        gate, up_part = gate_up[:, :size], gate_up[:, size:]
        sigmoid_gate = jax.nn.sigmoid(gate)
        activated = gate * sigmoid_gate
        hidden = (activated * up_part).astype(low)
        grad_hidden = rows_by_cols(grad_branch_mlp, down_weights)
        grad_gate = grad_hidden * up_part * sigmoid_gate * (1.0 + gate * (1.0 - sigmoid_gate))
        grad_up = grad_hidden * activated
        grad_rows = jnp.concatenate([grad_gate, grad_up], axis=1).astype(low)
        grads = jnp.concatenate(
            [cols_by_cols(normed_two, grad_rows).astype(low), cols_by_cols(grad_branch_mlp, hidden).astype(low)],
            axis=1,
        )
        grad_rows, grads = lax.optimization_barrier((grad_rows, grads))
        if sums:
            grads, sums[0] = lax.optimization_barrier((grads, sums[0]))
        else:
            grads, mlp_full[1] = lax.optimization_barrier((grads, mlp_full[1]))
        sums.append(lax.psum_scatter(grads, MLP_GATHER, scatter_dimension=0, tiled=True))
        back_products.append((grad_rows, pair_weights))
        out_products.append((hidden, down_weights))

    grad_normed_two, mlp_branch = bundle(
        4,
        75,
        (COLLECT, MLP_GROUP, halves(back_products, MLP_GROUP)),
        (COLLECT, MLP_GROUP, halves(out_products, MLP_GROUP)),
    )
    out_own = (middle + mlp_branch).astype(low)
    grad_gain_mlp = jnp.sum(grad_normed_two * scaled_two, axis=0)
    grad_middle = cotangent + norm_back(grad_normed_two * gain_mlp, scaled_two, factor_two)
    grad_middle, sums[0] = lax.optimization_barrier((grad_middle, sums[0]))
    (grad_branch_attn,) = bundle(5, 40, (SPREAD, (CONTEXT,), grad_middle.astype(low)))
    grad_branch_attn = grad_branch_attn.reshape(-1, width)
    grad_out = cols_by_cols(grad_branch_attn, attended)
    grad_attended = rows_by_cols(grad_branch_attn, out_full).astype(low)

    grad_queries = []
    grad_key = 0.0
    grad_value = 0.0
    for i in range(group):
        grad_query, key_part, value_part = attend_back(
            queries[i], key, value, grad_attended[:, i * HD : (i + 1) * HD], log_total[i], allowed
        )
        grad_queries.append(unrotate(grad_query, cosine, sine))
        grad_key = grad_key + key_part
        grad_value = grad_value + value_part
    grad_joined = jnp.concatenate(
        grad_queries + [unrotate(grad_key, cosine, sine), grad_value], axis=1
    ).astype(low)
    grad_attn = jnp.concatenate([cols_by_cols(normed_one, grad_joined).astype(low), grad_out.astype(low)], axis=1)
    grad_normed_one, parts_one = bundle(
        6,
        85,
        (COLLECT, (CONTEXT,), halves([(grad_joined, qkv_full)], (CONTEXT,))),
        (SWAP, MLP_GROUP, sums[0].reshape(group_size, rows, -1)),
    )
    grad_attn, sum_two, grad_normed_one = lax.optimization_barrier((grad_attn, sums[1], grad_normed_one))
    attn_sum = lax.psum_scatter(grad_attn, SHARD, scatter_dimension=0, tiled=True)
    grad_gain_attn = jnp.sum(grad_normed_one * scaled_one, axis=0)
    grad_inputs = grad_middle + norm_back(grad_normed_one * gain_attn, scaled_one, factor_one)
    grad_own = grad_inputs.astype(low)

    def both_cores(values):
        other = lax.ppermute(values, TENSOR, [(0, 1), (1, 0)])
        return jnp.where(tensor == 0, jnp.concatenate([values, other]), jnp.concatenate([other, values]))[None]

    hidden_out = both_cores(out_own)
    hidden_grad = both_cores(grad_own)
    gain_part = jnp.stack([grad_gain_attn, grad_gain_mlp]).reshape(2, shards, contexts, rows)
    owned_gains = fold(gain_part.transpose(1, 2, 0, 3), 7)

    sum_two, owned_gains = lax.optimization_barrier((sum_two, owned_gains))
    (parts_two,) = bundle(10, 30, (SWAP, MLP_GROUP, sum_two.reshape(group_size, rows, -1)))
    sizes = [stop - start for start, stop in chunks]
    owned_gate_up = jnp.concatenate(
        [
            parts[:, :, : 2 * size].reshape(group_size, rows, 2, size)
            for parts, size in zip((parts_one, parts_two), sizes)
        ],
        axis=3,
    )
    owned_gate_up = owned_gate_up.transpose(1, 2, 0, 3).reshape(rows, 2, -1).astype(full)
    owned_down = lay(
        jnp.concatenate(
            [parts[:, :, 2 * size :] for parts, size in zip((parts_one, parts_two), sizes)], axis=2
        )
    )
    attn_sum, owned_gate_up, owned_down, owned_gains, hidden_out, hidden_grad = lax.optimization_barrier(
        (attn_sum, owned_gate_up, owned_down, owned_gains, hidden_out, hidden_grad)
    )
    (attn_parts,) = bundle(8, 16, (SWAP, (CONTEXT,), attn_sum.reshape(contexts, rows, -1)))
    owned_qkv = lay(attn_parts[:, :, :head_cols])
    owned_out = lay(attn_parts[:, :, head_cols:])
    squares = jnp.sum(owned_gains * owned_gains) / tensors
    for owned in (owned_qkv, owned_out, owned_gate_up, owned_down):
        squares = squares + jnp.sum(owned * owned)
    grad_norm = jnp.sqrt(total_over(squares, 9))
    factor = jnp.minimum(1.0, clip_limit / grad_norm)

    qkv_out = adam_step(qkv_weight, qkv_m, qkv_v, owned_qkv, factor, 2.0 * (D / 2) ** (-0.5), weight_decay)
    out_out = adam_step(
        out_weight, out_m, out_v, owned_out, factor, 2.0 * (H * HD / 16) ** (-0.5), weight_decay
    )
    gate_up_out = adam_paired(
        gate_up_weight, gate_up_m, gate_up_v, owned_gate_up, factor, 2.0 * D ** (-0.5), weight_decay
    )
    down_out = adam_step(down_weight, down_m, down_v, owned_down, factor, 2.0 * FF ** (-0.5), weight_decay)
    gains_out = adam_step(gains, gains_m, gains_v, owned_gains, factor, 0.8, 0.0)
    return (hidden_out, hidden_grad, grad_norm, *qkv_out, *out_out, *gate_up_out, *down_out, *gains_out)


def solution(mesh):
    shards, contexts, tensors = mesh.devices.shape
    fine = Mesh(mesh.devices.reshape(shards // 2, 2, contexts, tensors), AXES)
    tokens = P(SHARD, CONTEXT, None)
    rows = (HIGH, LOW, CONTEXT)
    flat = P(rows, TENSOR)
    paired = P(rows, None, TENSOR)
    gains = P(None, rows)
    states = (flat,) * 6 + (paired,) * 3 + (flat,) * 3 + (gains,) * 3
    return jax.shard_map(
        body,
        mesh=fine,
        in_specs=(tokens, tokens, P(SHARD)) + states,
        out_specs=(tokens, tokens, P()) + states,
        check_vma=False,
    )
```

```python
import functools

import jax
import jax.numpy as jnp
from jax import lax
from jax.experimental import pallas as pl
from jax.experimental.pallas import tpu as pltpu
from jax.sharding import Mesh
from jax.sharding import PartitionSpec as P

D = 2560
H = 32
KV = 8
HD = 80
FF = 7168
STEP = 8


norm_epsilon = 1e-05
rope_theta = 1000000.0
masked_score = -1e30
clip_limit = 1.0
beta_first = 0.9
beta_second = 0.95
adam_epsilon = 1e-08
weight_decay = 0.1

HIGH, LOW, CONTEXT, TENSOR = "high", "low", "context", "tensor"
SHARD = (HIGH, LOW)
AXES = (HIGH, LOW, CONTEXT, TENSOR)
SWAP, STACK, SPREAD, COLLECT, TOTAL = "swap", "stack", "spread", "collect", "total"
MLP_GROUP = (CONTEXT,)
MLP_GATHER = (HIGH, LOW)
MESH = pl.DeviceIdType.MESH
low = jnp.bfloat16
full = jnp.float32


def rope_tables(positions):
    half = HD // 2
    exponent = jnp.arange(half, dtype=full) * (2.0 / HD)
    frequency = rope_theta ** (-exponent)
    angles = positions.astype(full)[:, None] * frequency[None, :]
    angles = jnp.concatenate([angles, angles], axis=-1)
    return (jnp.cos(angles), jnp.sin(angles))


def rotate(values, cosine, sine):
    half = values.shape[-1] // 2
    turned = jnp.concatenate([-values[..., half:], values[..., :half]], axis=-1)
    return values * cosine + turned * sine


def unrotate(values, cosine, sine):
    half = values.shape[-1] // 2
    turned = jnp.concatenate([-values[..., half:], values[..., :half]], axis=-1)
    return values * cosine - turned * sine


def normalize(values):
    factor = lax.rsqrt(jnp.mean(values * values, axis=-1, keepdims=True) + norm_epsilon)
    return (values * factor, factor)


def norm_back(grad_scaled, scaled, factor):
    return factor * (grad_scaled - scaled * jnp.mean(grad_scaled * scaled, axis=-1, keepdims=True))


def adam_step(weight, first, second, grad, factor, rate, decay):
    grad = grad * factor
    first_new = beta_first * first + (1.0 - beta_first) * grad
    second_new = beta_second * second + (1.0 - beta_second) * grad * grad
    corrected = (
        first_new
        / (1.0 - beta_first**STEP)
        / (jnp.sqrt(second_new / (1.0 - beta_second**STEP)) + adam_epsilon)
    )
    return (first_new, second_new, weight - rate * (corrected + decay * weight))


def over(left_dim, right_dim, left, right):
    return lax.dot_general(left, right, (((left_dim,), (right_dim,)), ((), ())), preferred_element_type=full)


rows_by_cols = functools.partial(over, 1, 0)
rows_by_rows = functools.partial(over, 1, 1)
cols_by_cols = functools.partial(over, 0, 0)


class Link:
    def __init__(self, sizes, send, recv):
        self.sizes, self.send, self.recv, self.used = sizes, send, recv, 0
        self.place = tuple(lax.axis_index(axis) for axis in AXES)

    def device(self, offset):
        return {axis: here ^ by for axis, here, by in zip(AXES, self.place, offset)}

    def index(self, group):
        index = 0
        for axis, here in zip(AXES, self.place):
            if axis in group:
                index = index * self.sizes[axis] + here
        return index

    def greet(self, partners):
        barrier = pltpu.get_barrier_semaphore()
        for offset in partners:
            pl.semaphore_signal(barrier, inc=1, device_id=self.device(offset), device_id_type=MESH)
        pl.semaphore_wait(barrier, len(partners))

    def push(self, src, dst, offset):
        copy = pltpu.make_async_remote_copy(
            src_ref=src,
            dst_ref=dst,
            send_sem=self.send.at[self.used],
            recv_sem=self.recv.at[self.used],
            device_id=self.device(offset),
            device_id_type=MESH,
        )
        self.used += 1
        copy.start()
        return copy

    def keep(self, src, dst):
        copy = pltpu.make_async_copy(src, dst, self.send.at[self.used])
        self.used += 1
        copy.start()
        return copy


MATE = (0, 0, 0, 1)


def axis_sizes():
    return {axis: lax.axis_size(axis) for axis in AXES}


def size_of(sizes, group):
    size = 1
    for axis in group:
        size *= sizes[axis]
    return size


def along(sizes, group, k):
    offset = []
    for axis in reversed(AXES):
        by = 0
        if axis in group:
            k, by = divmod(k, sizes[axis])
        offset.append(by)
    return tuple(reversed(offset))


def partners_of(jobs, sizes):
    found = set()
    for job in jobs:
        for group in job[1:]:
            n = size_of(sizes, group)
            steps = [1 << i for i in range(n.bit_length() - 1)] if job[0] in (SPREAD, COLLECT) else range(1, n)
            found |= {along(sizes, group, k) for k in steps}
        if job[0] in (SPREAD, COLLECT):
            found.add(MATE)
    return sorted(found)


def lanes(width, count):
    tiles, start, runs = width // 128, 0, []
    for i in range(count):
        size = 128 * ((tiles + count - 1 - i) // count)
        runs.append((start, size))
        start += size
    return runs


def turns(n, width):
    bits = [1 << i for i in range(n.bit_length() - 1)]
    return [(pl.ds(*run), bits[i:] + bits[:i]) for i, run in enumerate(lanes(width, len(bits)))]


class Swap:
    copies = staticmethod(lambda sizes, job, n: n)

    def __init__(self, link, job, sources, target, extras):
        (src,), group = sources, job[-1]
        me = link.index(group)
        self.ends = [
            link.push(src.at[me ^ k], target.at[me], along(link.sizes, group, k))
            for k in range(1, size_of(link.sizes, group))
        ]
        self.ends.append(link.keep(src.at[me], target.at[me]))

    def step(self, turn):
        pass

    def finish(self):
        for end in self.ends:
            end.wait()


class Stack:
    copies = staticmethod(lambda sizes, job, n: n + size_of(sizes, job[1]))

    def __init__(self, link, job, sources, target, extras):
        (src,), (_, outer, inner) = sources, job
        slot = target.at[link.index(outer), link.index(inner)]
        self.pieces = [link.push(src, slot, along(link.sizes, inner, k)) for k in range(1, size_of(link.sizes, inner))]
        self.pieces.append(link.keep(src, slot))
        self.link, self.outer, self.target = link, outer, target

    def step(self, turn):
        pass

    def finish(self):
        for piece in self.pieces:
            piece.wait()
        link, row = self.link, self.target.at[self.link.index(self.outer)]
        ends = [
            link.push(row, row, along(link.sizes, self.outer, k)) for k in range(1, size_of(link.sizes, self.outer))
        ]
        for end in ends:
            end.wait()


class Spread:
    copies = staticmethod(lambda sizes, job, n: 2 + 2 * (n - 1) * (n.bit_length() - 1))

    def __init__(self, link, job, sources, target, extras):
        (self.src,), self.group = sources, job[-1]
        self.link, self.target = link, target
        self.routes = turns(size_of(link.sizes, self.group), self.src.shape[1])
        self.held = [[0] for _ in self.routes]
        self.flying = [[] for _ in self.routes]
        self.sent, self.ends = [], []
        self.step(0)
        self.ends.append(link.push(self.src, target.at[1, 0], MATE))
        self.ends.append(link.keep(self.src, target.at[0, 0]))

    def land(self, i):
        run = self.routes[i][0]
        for k, copy in self.flying[i]:
            copy.wait_recv()
            self.held[i].append(k)
            self.ends.append(self.link.push(self.target.at[0, k, :, run], self.target.at[1, k, :, run], MATE))
        self.flying[i] = []

    def step(self, turn):
        for i, (run, bits) in enumerate(self.routes):
            if turn >= len(bits):
                continue
            arrived = self.flying[i]
            for _, copy in arrived:
                copy.wait_recv()
            bit = bits[turn]
            offset = along(self.link.sizes, self.group, bit)
            held = self.held[i] + [k for k, _ in arrived]
            flying = []
            for k in held:
                src = self.src.at[:, run] if k == 0 else self.target.at[0, k, :, run]
                copy = self.link.push(src, self.target.at[0, k ^ bit, :, run], offset)
                flying.append((k ^ bit, copy))
                self.sent.append(copy)
            for k, _ in arrived:
                here, there = self.target.at[0, k, :, run], self.target.at[1, k, :, run]
                self.ends.append(self.link.push(here, there, MATE))
            self.held[i], self.flying[i] = held, flying

    def finish(self):
        for i, _ in enumerate(self.routes):
            self.land(i)
        for copy in self.sent:
            copy.wait_send()
        for end in self.ends:
            end.wait()


class Collect:
    copies = staticmethod(lambda sizes, job, n: n + (n - 1) * (n.bit_length() - 1))

    def __init__(self, link, job, sources, target, extras):
        (self.near, self.far), self.group = sources, job[-1]
        (self.mates, self.got), self.link, self.target = extras, link, target
        n = size_of(link.sizes, self.group)
        self.routes = turns(n, self.near.shape[2])
        self.left = [list(range(n)) for _ in self.routes]
        self.adds = [{k: [] for k in range(n)} for _ in self.routes]
        self.places = [0 for _ in self.routes]
        self.sent = []
        self.crossed = set()
        self.crossing = {k: link.push(self.far.at[k], self.mates.at[k], MATE) for k in reversed(range(n))}

    def value(self, i, k):
        run = self.routes[i][0]
        if k not in self.crossed:
            self.crossing[k].wait_recv()
            self.crossed.add(k)
        total = self.near[k, :, run] + self.mates[k, :, run].astype(full)
        for place, copy in self.adds[i][k]:
            copy.wait_recv()
            total = total + self.got[place, :, run].astype(full)
        return total

    def step(self, turn):
        for i, (run, bits) in enumerate(self.routes):
            if turn >= len(bits):
                continue
            bit = bits[turn]
            offset = along(self.link.sizes, self.group, bit)
            for k in [k for k in self.left[i] if k & bit]:
                self.mates[k, :, run] = self.value(i, k).astype(low)
                place = self.places[i]
                copy = self.link.push(self.mates.at[k, :, run], self.got.at[place, :, run], offset)
                self.adds[i][k ^ bit].append((place, copy))
                self.sent.append(copy)
                self.places[i] += 1
            self.left[i] = [k for k in self.left[i] if not k & bit]

    def finish(self):
        for i, (run, _) in enumerate(self.routes):
            self.target[:, run] = self.value(i, 0)
        for copy in self.sent + list(self.crossing.values()):
            copy.wait_send()


class Total:
    copies = staticmethod(lambda sizes, job, n: sum(size_of(sizes, group) for group in job[1:]))

    def __init__(self, link, job, sources, target, extras):
        (self.src,), (self.held,) = sources, extras
        self.link, self.groups, self.target = link, job[1:], target

    def step(self, turn):
        pass

    def finish(self):
        link, held, slot = self.link, self.held, 0
        self.target[...] = self.src[...]
        for group in self.groups:
            n = size_of(link.sizes, group)
            held[slot] = self.target[...]
            pushes = [
                link.push(held.at[slot], held.at[slot + k], along(link.sizes, group, k)) for k in range(1, n)
            ]
            for push in pushes:
                push.wait()
            for k in range(1, n):
                self.target[...] += held[slot + k]
            slot += n


KINDS = {SWAP: Swap, STACK: Stack, SPREAD: Spread, COLLECT: Collect, TOTAL: Total}
EXTRAS = {COLLECT: 2, TOTAL: 1}


def bundle_kernel(jobs, sizes, *refs):
    refs = list(refs)
    take = lambda count: [refs.pop(0) for _ in range(count)]
    sources = [take(2 if job[0] == COLLECT else 1) for job in jobs]
    targets = [take(1)[0] for job in jobs]
    extras = [take(EXTRAS.get(job[0], 0)) for job in jobs]
    link = Link(sizes, *refs)
    link.greet(partners_of(jobs, sizes))
    running = [KINDS[job[0]](link, job, *rest) for job, *rest in zip(jobs, sources, targets, extras)]
    most = max(size_of(sizes, job[-1]).bit_length() - 1 for job in jobs)
    for turn in range(most):
        for job, work in zip(jobs, running):
            if job[0] == COLLECT or turn:
                work.step(turn)
    for work in reversed(running):
        work.finish()


def whole_in_vmem():
    return pl.BlockSpec(memory_space=pltpu.VMEM)


def talking(number, mib):
    return pltpu.CompilerParams(collective_id=number, has_side_effects=True, vmem_limit_bytes=mib * 2**20)


def bundle(number, micros, *jobs):
    sizes = axis_sizes()
    anywhere = pl.BlockSpec(memory_space=pl.ANY)
    flat, in_specs, out_specs, shapes, scratch, copies = [], [], [], [], [], 0
    for *job, array in jobs:
        kind, n = job[0], size_of(sizes, job[-1])
        copies += KINDS[kind].copies(sizes, job, n)
        if kind == COLLECT:
            near, far = array
            flat += [near, far]
            in_specs += [whole_in_vmem(), anywhere]
            out_specs.append(whole_in_vmem())
            shapes.append(jax.ShapeDtypeStruct(near.shape[1:], full))
            scratch += [pltpu.VMEM(far.shape, low), pltpu.VMEM((n - 1,) + far.shape[1:], low)]
            continue
        flat.append(array)
        if kind == TOTAL:
            in_specs.append(whole_in_vmem())
            out_specs.append(whole_in_vmem())
            shapes.append(jax.ShapeDtypeStruct(array.shape, full))
            scratch.append(pltpu.VMEM((KINDS[kind].copies(sizes, job, n),) + array.shape, full))
            continue
        in_specs.append(anywhere)
        out_specs.append(anywhere)
        shape = array.shape
        if kind == STACK:
            shape = (size_of(sizes, job[1]), n) + shape
        elif kind == SPREAD:
            shape = (2, n) + shape
        shapes.append(jax.ShapeDtypeStruct(shape, array.dtype))
    return pl.pallas_call(
        functools.partial(bundle_kernel, tuple(tuple(job[:-1]) for job in jobs), sizes),
        out_shape=shapes,
        in_specs=in_specs,
        out_specs=out_specs,
        scratch_shapes=scratch + [pltpu.SemaphoreType.DMA((copies,)), pltpu.SemaphoreType.DMA((copies,))],
        compiler_params=talking(number, 56),
        cost_estimate=pl.CostEstimate(flops=int(micros * 8e8), bytes_accessed=0, transcendentals=0),
    )(*flat)


def halves(products, group):
    n = lax.axis_size(group)
    half = products[0][0].shape[0] // 2

    def part(start):
        total = 0.0
        for left, right in products:
            total = total + rows_by_rows(left[start : start + half], right)
        return total.reshape(n, half // n, -1)

    return part(0), part(half).astype(low)


def fold_kernel(sizes, part_ref, sum_ref, work, mates, outers, inners, send, recv):
    link = Link(sizes, send, recv)
    groups = ((TENSOR,), (CONTEXT,), SHARD)
    link.greet([along(sizes, group, k) for group in groups for k in range(1, size_of(sizes, group))])
    s, c = link.index(SHARD), link.index((CONTEXT,))
    push = link.push(part_ref, mates, MATE)
    push.wait()
    work[...] = part_ref[...] + mates[...]
    shards, contexts = size_of(sizes, SHARD), sizes[CONTEXT]
    pushes = [link.push(work.at[s ^ k], outers.at[k], along(sizes, SHARD, k)) for k in range(1, shards)]
    outers[0] = work[s]
    for push in pushes:
        push.wait()
    for k in range(1, shards):
        outers[0] += outers[k]
    group = (CONTEXT,)
    pushes = [link.push(outers.at[0, c ^ k], inners.at[k], along(sizes, group, k)) for k in range(1, contexts)]
    sum_ref[...] = outers[0, c]
    for push in pushes:
        push.wait()
    for k in range(1, contexts):
        sum_ref[...] += inners[k]


def fold(part, number):
    sizes = axis_sizes()
    slots = sizes[TENSOR] + sizes[CONTEXT] + size_of(sizes, SHARD)
    return pl.pallas_call(
        functools.partial(fold_kernel, sizes),
        out_shape=jax.ShapeDtypeStruct(part.shape[2:], full),
        in_specs=[whole_in_vmem()],
        out_specs=whole_in_vmem(),
        scratch_shapes=[
            pltpu.VMEM(part.shape, full),
            pltpu.VMEM(part.shape, full),
            pltpu.VMEM(part.shape, full),
            pltpu.VMEM(part.shape[1:], full),
            pltpu.SemaphoreType.DMA((slots,)),
            pltpu.SemaphoreType.DMA((slots,)),
        ],
        compiler_params=talking(number, 16),
    )(part)


def adam_kernel(rate, decay, factor_ref, weight_ref, first_ref, second_ref, grad_ref, first_out, second_out, weight_out):
    first, second, weight = adam_step(
        weight_ref[...], first_ref[...], second_ref[...], grad_ref[...], factor_ref[0], rate, decay
    )
    first_out[...] = first
    second_out[...] = second
    weight_out[...] = weight


def adam_paired(weight, first, second, grad, factor, rate, decay):
    rows = weight.shape[0]
    step = 16 if rows % 16 == 0 else 8
    block = pl.BlockSpec((step,) + weight.shape[1:], lambda i: (i, 0, 0))
    return pl.pallas_call(
        functools.partial(adam_kernel, rate, decay),
        grid=(rows // step,),
        out_shape=[jax.ShapeDtypeStruct(weight.shape, weight.dtype)] * 3,
        in_specs=[pl.BlockSpec(memory_space=pltpu.SMEM)] + [block] * 4,
        out_specs=[block] * 3,
        compiler_params=pltpu.CompilerParams(vmem_limit_bytes=48 * 2**20),
    )(factor.reshape(1), weight, first, second, grad)


def weight_grads_kernel(pairs, *refs):
    lefts, rights, out = refs[: len(pairs)], refs[len(pairs) : -1], refs[-1]
    start = 0
    for pair, right in zip(pairs, rights):
        size = right.shape[1]
        out[:, start : start + size] = cols_by_cols(lefts[pair][...], right[...]).astype(low)
        start += size


def weight_grads(pairs):
    tokens, width = pairs[0][0].shape
    cols = sum(right.shape[1] for _, right in pairs)
    step = 256
    return pl.pallas_call(
        functools.partial(weight_grads_kernel, tuple(range(len(pairs)))),
        grid=(width // step,),
        out_shape=jax.ShapeDtypeStruct((width, cols), low),
        in_specs=[pl.BlockSpec((tokens, step), lambda i: (0, i))] * len(pairs)
        + [pl.BlockSpec(right.shape, lambda i: (0, 0)) for _, right in pairs],
        out_specs=pl.BlockSpec((step, cols), lambda i: (i, 0)),
        compiler_params=pltpu.CompilerParams(vmem_limit_bytes=48 * 2**20),
        cost_estimate=pl.CostEstimate(flops=2 * tokens * width * cols, bytes_accessed=0, transcendentals=0),
    )(*(left for left, _ in pairs), *(right for _, right in pairs))


def attend(query, key, value, allowed):
    scores = rows_by_rows(query, key) * HD ** (-0.5)
    scores = jnp.where(allowed, scores, masked_score)
    row_max = jnp.max(scores, axis=-1, keepdims=True)
    expanded = jnp.exp(scores - row_max)
    row_total = jnp.sum(expanded, axis=-1, keepdims=True)
    probs = (expanded / row_total).astype(low)
    return rows_by_cols(probs, value), row_max + jnp.log(row_total)


def attend_back(query, key, value, grad, log_total, allowed):
    scores = rows_by_rows(query, key) * HD ** (-0.5)
    scores = jnp.where(allowed, scores, masked_score)
    probs = jnp.exp(scores - log_total)
    grad_value = cols_by_cols(probs.astype(low), grad)
    grad_probs = rows_by_rows(grad, value)
    delta = jnp.sum(probs * grad_probs, axis=-1, keepdims=True)
    grad_scores = (probs * (grad_probs - delta)).astype(low)
    grad_query = rows_by_cols(grad_scores, key) * HD ** (-0.5)
    grad_key = cols_by_cols(grad_scores, query) * HD ** (-0.5)
    return grad_query, grad_key, grad_value


def body(
    hidden_in,
    out_grad,
    prefix_len,
    qkv_weight,
    qkv_m,
    qkv_v,
    out_weight,
    out_m,
    out_v,
    gate_up_weight,
    gate_up_m,
    gate_up_v,
    down_weight,
    down_m,
    down_v,
    gains,
    gains_m,
    gains_v,
):
    _, local_len, width = hidden_in.shape
    shards, contexts, tensors = (lax.axis_size(group) for group in (SHARD, CONTEXT, TENSOR))
    context, tensor = lax.axis_index(CONTEXT), lax.axis_index(TENSOR)
    group_size = lax.axis_size(MLP_GROUP)
    rows = qkv_weight.shape[0]
    group = H // KV
    head_cols = (group + 2) * HD
    own = local_len // tensors
    ff_block = down_weight.shape[1] // group_size
    ff_first = ff_block // 2 // 128 * 128 or ff_block // 2
    chunks = ((0, ff_first), (ff_first, ff_block))

    def to_blocks(weight, count):
        return jnp.moveaxis(weight.astype(low).reshape(rows, count, -1), 1, 0)

    def lay(blocks):
        return jnp.moveaxis(blocks, 0, 1).reshape(rows, -1).astype(full)

    (attn_part,) = bundle(
        0,
        16,
        (
            SWAP,
            (CONTEXT,),
            jnp.concatenate([to_blocks(qkv_weight, contexts), to_blocks(out_weight, contexts)], axis=2),
        ),
    )
    gain_values, attn_part = lax.optimization_barrier((gains.astype(low).astype(full), attn_part))
    (gain_blocks,) = bundle(9, 10, (STACK, SHARD, (CONTEXT,), gain_values))
    attn_full = lax.all_gather(attn_part.reshape(contexts * rows, -1), SHARD, axis=0, tiled=True)
    qkv_full, out_full = attn_full[:, :head_cols], attn_full[:, head_cols:]
    gain_rows = gain_blocks.reshape(shards * contexts, 2, rows).transpose(1, 0, 2).reshape(2, width)
    gain_attn, gain_mlp = gain_rows[0], gain_rows[1]
    inputs = lax.dynamic_slice_in_dim(hidden_in[0], tensor * own, own, 0).astype(full)
    grad_low = lax.dynamic_slice_in_dim(out_grad[0], tensor * own, own, 0)
    cotangent = grad_low.astype(full)
    scaled_one, factor_one = normalize(inputs)

    gate_up_blocks = gate_up_weight.astype(low).reshape(rows, 2, group_size, ff_block).transpose(2, 0, 1, 3)
    down_blocks = to_blocks(down_weight, group_size)

    def chunk_blocks(start, stop):
        pair = gate_up_blocks[:, :, :, start:stop]
        return jnp.concatenate([pair[:, :, 0], pair[:, :, 1], down_blocks[:, :, start:stop]], axis=2)

    def gather_mlp(part):
        return lax.all_gather(part.reshape(group_size * rows, -1), MLP_GATHER, axis=0, tiled=True)

    normed_one, part_one = bundle(
        1,
        60,
        (SPREAD, (CONTEXT,), (scaled_one * gain_attn).astype(low)),
        (SWAP, MLP_GROUP, chunk_blocks(*chunks[0])),
    )
    normed_one = normed_one.reshape(-1, width)
    mlp_full = [gather_mlp(part_one)]

    places = jnp.arange(contexts, dtype=jnp.int32) ^ context
    cores = jnp.arange(tensors, dtype=jnp.int32) ^ tensor
    positions = (
        places[None, :, None] * local_len
        + cores[:, None, None] * own
        + jnp.arange(own, dtype=jnp.int32)[None, None, :]
    ).reshape(-1)
    cosine, sine = rope_tables(positions)
    allowed = (positions[None, :] <= positions[:, None]) | (positions[None, :] < prefix_len[0])

    joined = rows_by_cols(normed_one, qkv_full)
    parts = [joined[:, i * HD : (i + 1) * HD] for i in range(group + 2)]
    queries = [rotate(part, cosine, sine).astype(low) for part in parts[:group]]
    key = rotate(parts[group], cosine, sine).astype(low)
    value = parts[group + 1].astype(low)
    mixed, log_total = zip(*[attend(query, key, value, allowed) for query in queries])
    attended = jnp.concatenate([part.astype(low) for part in mixed], axis=1)
    branch, part_two, grad_branch_mlp = bundle(
        2,
        80,
        (COLLECT, (CONTEXT,), halves([(attended, out_full)], (CONTEXT,))),
        (SWAP, MLP_GROUP, chunk_blocks(*chunks[1])),
        (SPREAD, MLP_GROUP, grad_low),
    )
    grad_branch_mlp = grad_branch_mlp.reshape(-1, width)
    mlp_full.append(gather_mlp(part_two))
    middle = inputs + branch
    scaled_two, factor_two = normalize(middle)
    (normed_two,) = bundle(3, 40, (SPREAD, MLP_GROUP, (scaled_two * gain_mlp).astype(low)))
    normed_two = normed_two.reshape(-1, width)

    sums, back_products, out_products = [], [], []
    for place, (start, stop) in enumerate(chunks):
        size = stop - start
        weights = mlp_full[place]
        pair_weights, down_weights = weights[:, : 2 * size], weights[:, 2 * size :]
        gate_up = rows_by_cols(normed_two, pair_weights)
        gate, up_part = gate_up[:, :size], gate_up[:, size:]
        sigmoid_gate = jax.nn.sigmoid(gate)
        activated = gate * sigmoid_gate
        hidden = (activated * up_part).astype(low)
        grad_hidden = rows_by_cols(grad_branch_mlp, down_weights)
        grad_gate = grad_hidden * up_part * sigmoid_gate * (1.0 + gate * (1.0 - sigmoid_gate))
        grad_up = grad_hidden * activated
        grad_rows = jnp.concatenate([grad_gate, grad_up], axis=1).astype(low)
        grads = weight_grads([(normed_two, grad_rows), (grad_branch_mlp, hidden)])
        grad_rows, grads = lax.optimization_barrier((grad_rows, grads))
        if sums:
            grads, sums[0] = lax.optimization_barrier((grads, sums[0]))
        else:
            grads, mlp_full[1] = lax.optimization_barrier((grads, mlp_full[1]))
        sums.append(lax.psum_scatter(grads, MLP_GATHER, scatter_dimension=0, tiled=True))
        back_products.append((grad_rows, pair_weights))
        out_products.append((hidden, down_weights))

    (grad_normed_two,) = bundle(4, 40, (COLLECT, MLP_GROUP, halves(back_products, MLP_GROUP)))
    grad_gain_mlp = jnp.sum(grad_normed_two * scaled_two, axis=0)
    grad_middle = cotangent + norm_back(grad_normed_two * gain_mlp, scaled_two, factor_two)
    grad_middle, sums[0] = lax.optimization_barrier((grad_middle, sums[0]))
    grad_branch_attn, mlp_branch, parts_one = bundle(
        5,
        80,
        (SPREAD, (CONTEXT,), grad_middle.astype(low)),
        (COLLECT, MLP_GROUP, halves(out_products, MLP_GROUP)),
        (SWAP, MLP_GROUP, sums[0].reshape(group_size, rows, -1)),
    )
    out_own = (middle + mlp_branch).astype(low)
    grad_branch_attn = grad_branch_attn.reshape(-1, width)
    grad_attended = rows_by_cols(grad_branch_attn, out_full).astype(low)

    grad_queries = []
    grad_key = 0.0
    grad_value = 0.0
    for i in range(group):
        grad_query, key_part, value_part = attend_back(
            queries[i], key, value, grad_attended[:, i * HD : (i + 1) * HD], log_total[i], allowed
        )
        grad_queries.append(unrotate(grad_query, cosine, sine))
        grad_key = grad_key + key_part
        grad_value = grad_value + value_part
    grad_joined = jnp.concatenate(
        grad_queries + [unrotate(grad_key, cosine, sine), grad_value], axis=1
    ).astype(low)
    grad_attn = jnp.concatenate(
        [cols_by_cols(normed_one, grad_joined).astype(low), cols_by_cols(grad_branch_attn, attended).astype(low)],
        axis=1,
    )
    grad_attn, sum_two = lax.optimization_barrier((grad_attn, sums[1]))
    attn_sum = lax.psum_scatter(grad_attn, SHARD, scatter_dimension=0, tiled=True)
    (grad_normed_one,) = bundle(6, 40, (COLLECT, (CONTEXT,), halves([(grad_joined, qkv_full)], (CONTEXT,))))
    grad_gain_attn = jnp.sum(grad_normed_one * scaled_one, axis=0)
    grad_inputs = grad_middle + norm_back(grad_normed_one * gain_attn, scaled_one, factor_one)
    grad_own = grad_inputs.astype(low)

    def both_cores(values):
        other = lax.ppermute(values, TENSOR, [(0, 1), (1, 0)])
        return jnp.where(tensor == 0, jnp.concatenate([values, other]), jnp.concatenate([other, values]))[None]

    hidden_out = both_cores(out_own)
    hidden_grad = both_cores(grad_own)
    gain_part = jnp.stack([grad_gain_attn, grad_gain_mlp]).reshape(2, shards, contexts, rows)
    owned_gains = fold(gain_part.transpose(1, 2, 0, 3), 7)

    sum_two, owned_gains = lax.optimization_barrier((sum_two, owned_gains))
    (parts_two,) = bundle(10, 30, (SWAP, MLP_GROUP, sum_two.reshape(group_size, rows, -1)))
    sizes = [stop - start for start, stop in chunks]
    owned_gate_up = jnp.concatenate(
        [
            parts[:, :, : 2 * size].reshape(group_size, rows, 2, size)
            for parts, size in zip((parts_one, parts_two), sizes)
        ],
        axis=3,
    )
    owned_gate_up = owned_gate_up.transpose(1, 2, 0, 3).reshape(rows, 2, -1).astype(full)
    owned_down = lay(
        jnp.concatenate(
            [parts[:, :, 2 * size :] for parts, size in zip((parts_one, parts_two), sizes)], axis=2
        )
    )
    attn_sum, owned_gate_up, owned_down, owned_gains, hidden_out, hidden_grad = lax.optimization_barrier(
        (attn_sum, owned_gate_up, owned_down, owned_gains, hidden_out, hidden_grad)
    )
    squares = jnp.sum(owned_gains * owned_gains) / tensors
    for owned in (attn_sum, sums[0], sum_two):
        owned = owned.astype(full)
        squares = squares + jnp.sum(owned * owned)
    attn_parts, total = bundle(
        8,
        20,
        (SWAP, (CONTEXT,), attn_sum.reshape(contexts, rows, -1)),
        (TOTAL, (TENSOR,), (CONTEXT,), SHARD, jnp.full((8, 128), squares, full)),
    )
    grad_norm = jnp.sqrt(total[0, 0])
    owned_qkv = lay(attn_parts[:, :, :head_cols])
    owned_out = lay(attn_parts[:, :, head_cols:])
    factor = jnp.minimum(1.0, clip_limit / grad_norm)

    qkv_out = adam_step(qkv_weight, qkv_m, qkv_v, owned_qkv, factor, 2.0 * (D / 2) ** (-0.5), weight_decay)
    out_out = adam_step(
        out_weight, out_m, out_v, owned_out, factor, 2.0 * (H * HD / 16) ** (-0.5), weight_decay
    )
    gate_up_out = adam_paired(
        gate_up_weight, gate_up_m, gate_up_v, owned_gate_up, factor, 2.0 * D ** (-0.5), weight_decay
    )
    down_out = adam_step(down_weight, down_m, down_v, owned_down, factor, 2.0 * FF ** (-0.5), weight_decay)
    gains_out = adam_step(gains, gains_m, gains_v, owned_gains, factor, 0.8, 0.0)
    return (hidden_out, hidden_grad, grad_norm, *qkv_out, *out_out, *gate_up_out, *down_out, *gains_out)


def solution(mesh):
    shards, contexts, tensors = mesh.devices.shape
    fine = Mesh(mesh.devices.reshape(shards // 2, 2, contexts, tensors), AXES)
    tokens = P(SHARD, CONTEXT, None)
    rows = (HIGH, LOW, CONTEXT)
    flat = P(rows, TENSOR)
    paired = P(rows, None, TENSOR)
    gains = P(None, rows)
    states = (flat,) * 6 + (paired,) * 3 + (flat,) * 3 + (gains,) * 3
    return jax.shard_map(
        body,
        mesh=fine,
        in_specs=(tokens, tokens, P(SHARD)) + states,
        out_specs=(tokens, tokens, P()) + states,
        check_vma=False,
    )
```

```python
import functools

import jax
import jax.numpy as jnp
from jax import lax
from jax.experimental import pallas as pl
from jax.experimental.pallas import tpu as pltpu
from jax.sharding import Mesh
from jax.sharding import PartitionSpec as P

D = 2560
H = 32
KV = 8
HD = 80
FF = 7168
STEP = 8


norm_epsilon = 1e-05
rope_theta = 1000000.0
masked_score = -1e30
clip_limit = 1.0
beta_first = 0.9
beta_second = 0.95
adam_epsilon = 1e-08
weight_decay = 0.1

HIGH, LOW, CONTEXT, TENSOR = "high", "low", "context", "tensor"
SHARD = (HIGH, LOW)
AXES = (HIGH, LOW, CONTEXT, TENSOR)
SWAP, STACK, SPREAD, COLLECT, TOTAL = "swap", "stack", "spread", "collect", "total"
MLP_GROUP = (CONTEXT,)
MLP_GATHER = (HIGH, LOW)
MESH = pl.DeviceIdType.MESH
low = jnp.bfloat16
full = jnp.float32


def rope_tables(positions):
    half = HD // 2
    exponent = jnp.arange(half, dtype=full) * (2.0 / HD)
    frequency = rope_theta ** (-exponent)
    angles = positions.astype(full)[:, None] * frequency[None, :]
    angles = jnp.concatenate([angles, angles], axis=-1)
    return (jnp.cos(angles), jnp.sin(angles))


def rotate(values, cosine, sine):
    half = values.shape[-1] // 2
    turned = jnp.concatenate([-values[..., half:], values[..., :half]], axis=-1)
    return values * cosine + turned * sine


def unrotate(values, cosine, sine):
    half = values.shape[-1] // 2
    turned = jnp.concatenate([-values[..., half:], values[..., :half]], axis=-1)
    return values * cosine - turned * sine


def normalize(values):
    factor = lax.rsqrt(jnp.mean(values * values, axis=-1, keepdims=True) + norm_epsilon)
    return (values * factor, factor)


def norm_back(grad_scaled, scaled, factor):
    return factor * (grad_scaled - scaled * jnp.mean(grad_scaled * scaled, axis=-1, keepdims=True))


def adam_step(weight, first, second, grad, factor, rate, decay):
    grad = grad * factor
    first_new = beta_first * first + (1.0 - beta_first) * grad
    second_new = beta_second * second + (1.0 - beta_second) * grad * grad
    first_scale, second_scale = 1.0 / (1.0 - beta_first**STEP), 1.0 / (1.0 - beta_second**STEP)
    corrected = first_new * first_scale / (jnp.sqrt(second_new * second_scale) + adam_epsilon)
    return (first_new, second_new, weight - rate * (corrected + decay * weight))


def over(left_dim, right_dim, left, right):
    return lax.dot_general(left, right, (((left_dim,), (right_dim,)), ((), ())), preferred_element_type=full)


rows_by_cols = functools.partial(over, 1, 0)
rows_by_rows = functools.partial(over, 1, 1)
cols_by_cols = functools.partial(over, 0, 0)


class Link:
    def __init__(self, sizes, send, recv):
        self.sizes, self.send, self.recv, self.used = sizes, send, recv, 0
        self.place = tuple(lax.axis_index(axis) for axis in AXES)

    def device(self, offset):
        return {axis: here ^ by for axis, here, by in zip(AXES, self.place, offset)}

    def index(self, group):
        index = 0
        for axis, here in zip(AXES, self.place):
            if axis in group:
                index = index * self.sizes[axis] + here
        return index

    def greet(self, partners):
        barrier = pltpu.get_barrier_semaphore()
        for offset in partners:
            pl.semaphore_signal(barrier, inc=1, device_id=self.device(offset), device_id_type=MESH)
        pl.semaphore_wait(barrier, len(partners))

    def push(self, src, dst, offset):
        copy = pltpu.make_async_remote_copy(
            src_ref=src,
            dst_ref=dst,
            send_sem=self.send.at[self.used],
            recv_sem=self.recv.at[self.used],
            device_id=self.device(offset),
            device_id_type=MESH,
        )
        self.used += 1
        copy.start()
        return copy

    def keep(self, src, dst):
        copy = pltpu.make_async_copy(src, dst, self.send.at[self.used])
        self.used += 1
        copy.start()
        return copy


MATE = (0, 0, 0, 1)


def axis_sizes():
    return {axis: lax.axis_size(axis) for axis in AXES}


def size_of(sizes, group):
    size = 1
    for axis in group:
        size *= sizes[axis]
    return size


def along(sizes, group, k):
    offset = []
    for axis in reversed(AXES):
        by = 0
        if axis in group:
            k, by = divmod(k, sizes[axis])
        offset.append(by)
    return tuple(reversed(offset))


def partners_of(jobs, sizes):
    found = set()
    for job in jobs:
        for group in job[1:]:
            n = size_of(sizes, group)
            steps = [1 << i for i in range(n.bit_length() - 1)] if job[0] in (SPREAD, COLLECT) else range(1, n)
            found |= {along(sizes, group, k) for k in steps}
        if job[0] in (SPREAD, COLLECT):
            found.add(MATE)
    return sorted(found)


def lanes(width, count):
    tiles, start, runs = width // 128, 0, []
    for i in range(count):
        size = 128 * ((tiles + count - 1 - i) // count)
        runs.append((start, size))
        start += size
    return runs


def turns(n, width):
    bits = [1 << i for i in range(n.bit_length() - 1)]
    return [(pl.ds(*run), bits[i:] + bits[:i]) for i, run in enumerate(lanes(width, len(bits)))]


class Swap:
    copies = staticmethod(lambda sizes, job, n: n)

    def __init__(self, link, job, sources, target, extras):
        (src,), group = sources, job[-1]
        me = link.index(group)
        self.ends = [
            link.push(src.at[me ^ k], target.at[me], along(link.sizes, group, k))
            for k in range(1, size_of(link.sizes, group))
        ]
        self.ends.append(link.keep(src.at[me], target.at[me]))

    def step(self, turn):
        pass

    def finish(self):
        for end in self.ends:
            end.wait()


class Stack:
    copies = staticmethod(lambda sizes, job, n: n + size_of(sizes, job[1]))

    def __init__(self, link, job, sources, target, extras):
        (src,), (_, outer, inner) = sources, job
        slot = target.at[link.index(outer), link.index(inner)]
        self.pieces = [link.push(src, slot, along(link.sizes, inner, k)) for k in range(1, size_of(link.sizes, inner))]
        self.pieces.append(link.keep(src, slot))
        self.link, self.outer, self.target = link, outer, target

    def step(self, turn):
        pass

    def finish(self):
        for piece in self.pieces:
            piece.wait()
        link, row = self.link, self.target.at[self.link.index(self.outer)]
        ends = [
            link.push(row, row, along(link.sizes, self.outer, k)) for k in range(1, size_of(link.sizes, self.outer))
        ]
        for end in ends:
            end.wait()


class Spread:
    copies = staticmethod(lambda sizes, job, n: 2 + 2 * (n - 1) * (n.bit_length() - 1))

    def __init__(self, link, job, sources, target, extras):
        (self.src,), self.group = sources, job[-1]
        self.link, self.target = link, target
        self.routes = turns(size_of(link.sizes, self.group), self.src.shape[1])
        self.held = [[0] for _ in self.routes]
        self.flying = [[] for _ in self.routes]
        self.sent, self.ends = [], []
        self.step(0)
        self.ends.append(link.push(self.src, target.at[1, 0], MATE))
        self.ends.append(link.keep(self.src, target.at[0, 0]))

    def land(self, i):
        run = self.routes[i][0]
        for k, copy in self.flying[i]:
            copy.wait_recv()
            self.held[i].append(k)
            self.ends.append(self.link.push(self.target.at[0, k, :, run], self.target.at[1, k, :, run], MATE))
        self.flying[i] = []

    def step(self, turn):
        for i, (run, bits) in enumerate(self.routes):
            if turn >= len(bits):
                continue
            arrived = self.flying[i]
            for _, copy in arrived:
                copy.wait_recv()
            bit = bits[turn]
            offset = along(self.link.sizes, self.group, bit)
            held = self.held[i] + [k for k, _ in arrived]
            flying = []
            for k in held:
                src = self.src.at[:, run] if k == 0 else self.target.at[0, k, :, run]
                copy = self.link.push(src, self.target.at[0, k ^ bit, :, run], offset)
                flying.append((k ^ bit, copy))
                self.sent.append(copy)
            for k, _ in arrived:
                here, there = self.target.at[0, k, :, run], self.target.at[1, k, :, run]
                self.ends.append(self.link.push(here, there, MATE))
            self.held[i], self.flying[i] = held, flying

    def finish(self):
        for i, _ in enumerate(self.routes):
            self.land(i)
        for copy in self.sent:
            copy.wait_send()
        for end in self.ends:
            end.wait()


class Collect:
    copies = staticmethod(lambda sizes, job, n: n + (n - 1) * (n.bit_length() - 1))

    def __init__(self, link, job, sources, target, extras):
        (self.near, self.far), self.group = sources, job[-1]
        (self.mates, self.got), self.link, self.target = extras, link, target
        n = size_of(link.sizes, self.group)
        self.routes = turns(n, self.near.shape[2])
        self.left = [list(range(n)) for _ in self.routes]
        self.adds = [{k: [] for k in range(n)} for _ in self.routes]
        self.places = [0 for _ in self.routes]
        self.sent = []
        self.crossed = set()
        self.crossing = {k: link.push(self.far.at[k], self.mates.at[k], MATE) for k in reversed(range(n))}

    def value(self, i, k):
        run = self.routes[i][0]
        if k not in self.crossed:
            self.crossing[k].wait_recv()
            self.crossed.add(k)
        total = self.near[k, :, run] + self.mates[k, :, run].astype(full)
        for place, copy in self.adds[i][k]:
            copy.wait_recv()
            total = total + self.got[place, :, run].astype(full)
        return total

    def step(self, turn):
        for i, (run, bits) in enumerate(self.routes):
            if turn >= len(bits):
                continue
            bit = bits[turn]
            offset = along(self.link.sizes, self.group, bit)
            for k in [k for k in self.left[i] if k & bit]:
                self.mates[k, :, run] = self.value(i, k).astype(low)
                place = self.places[i]
                copy = self.link.push(self.mates.at[k, :, run], self.got.at[place, :, run], offset)
                self.adds[i][k ^ bit].append((place, copy))
                self.sent.append(copy)
                self.places[i] += 1
            self.left[i] = [k for k in self.left[i] if not k & bit]

    def finish(self):
        for i, (run, _) in enumerate(self.routes):
            self.target[:, run] = self.value(i, 0)
        for copy in self.sent + list(self.crossing.values()):
            copy.wait_send()


class Total:
    copies = staticmethod(lambda sizes, job, n: sum(size_of(sizes, group) for group in job[1:]))

    def __init__(self, link, job, sources, target, extras):
        (tile, array), (self.held,) = sources, extras
        self.link, self.groups, self.target, self.slot = link, list(job[1:]), target, 0
        values = array[...].astype(full)
        target[...] = tile[...] + jnp.sum(values * values)
        self.ask()

    def ask(self):
        link, held, slot, group = self.link, self.held, self.slot, self.groups.pop(0)
        n = size_of(link.sizes, group)
        held[slot] = self.target[...]
        self.pushes = [link.push(held.at[slot], held.at[slot + k], along(link.sizes, group, k)) for k in range(1, n)]

    def step(self, turn):
        pass

    def finish(self):
        while True:
            for push in self.pushes:
                push.wait()
            for k, _ in enumerate(self.pushes):
                self.target[...] += self.held[self.slot + 1 + k]
            self.slot += 1 + len(self.pushes)
            if not self.groups:
                return
            self.ask()


KINDS = {SWAP: Swap, STACK: Stack, SPREAD: Spread, COLLECT: Collect, TOTAL: Total}
EXTRAS = {COLLECT: 2, TOTAL: 1}


def bundle_kernel(jobs, sizes, *refs):
    refs = list(refs)
    take = lambda count: [refs.pop(0) for _ in range(count)]
    sources = [take(2 if job[0] in EXTRAS else 1) for job in jobs]
    targets = [take(1)[0] for job in jobs]
    extras = [take(EXTRAS.get(job[0], 0)) for job in jobs]
    link = Link(sizes, *refs)
    link.greet(partners_of(jobs, sizes))
    running = [KINDS[job[0]](link, job, *rest) for job, *rest in zip(jobs, sources, targets, extras)]
    most = max(size_of(sizes, job[-1]).bit_length() - 1 for job in jobs)
    for turn in range(most):
        for job, work in zip(jobs, running):
            if job[0] == COLLECT or turn:
                work.step(turn)
    for work in running:
        if not isinstance(work, Swap):
            work.finish()
    for work in running:
        if isinstance(work, Swap):
            work.finish()


def whole_in_vmem():
    return pl.BlockSpec(memory_space=pltpu.VMEM)


def talking(number, mib):
    return pltpu.CompilerParams(collective_id=number, has_side_effects=True, vmem_limit_bytes=mib * 2**20)


def bundle(number, micros, *jobs):
    sizes = axis_sizes()
    anywhere = pl.BlockSpec(memory_space=pl.ANY)
    flat, in_specs, out_specs, shapes, scratch, copies, held = [], [], [], [], [], 0, 0
    for *job, array in jobs:
        kind, n = job[0], size_of(sizes, job[-1])
        copies += KINDS[kind].copies(sizes, job, n)
        if kind == COLLECT:
            near, far = array
            flat += [near, far]
            in_specs += [whole_in_vmem(), anywhere]
            out_specs.append(whole_in_vmem())
            shapes.append(jax.ShapeDtypeStruct(near.shape[1:], full))
            scratch += [pltpu.VMEM(far.shape, low), pltpu.VMEM((n - 1,) + far.shape[1:], low)]
            held += 10 * near.size
            continue
        if kind == TOTAL:
            flat += array
            in_specs += [whole_in_vmem()] * 2
            out_specs.append(whole_in_vmem())
            shapes.append(jax.ShapeDtypeStruct(array[0].shape, full))
            scratch.append(pltpu.VMEM((KINDS[kind].copies(sizes, job, n),) + array[0].shape, full))
            held += 2 * array[1].size
            continue
        flat.append(array)
        in_specs.append(anywhere)
        out_specs.append(anywhere)
        shape = array.shape
        if kind == STACK:
            shape = (size_of(sizes, job[1]), n) + shape
        elif kind == SPREAD:
            shape = (2, n) + shape
        shapes.append(jax.ShapeDtypeStruct(shape, array.dtype))
    return pl.pallas_call(
        functools.partial(bundle_kernel, tuple(tuple(job[:-1]) for job in jobs), sizes),
        out_shape=shapes,
        in_specs=in_specs,
        out_specs=out_specs,
        scratch_shapes=scratch + [pltpu.SemaphoreType.DMA((copies,)), pltpu.SemaphoreType.DMA((copies,))],
        compiler_params=talking(number, 6 + held // 2**20),
        cost_estimate=pl.CostEstimate(flops=int(micros * 8e8), bytes_accessed=0, transcendentals=0),
    )(*flat)


def halves(products, group):
    n = lax.axis_size(group)
    half = products[0][0].shape[0] // 2

    def part(start):
        total = 0.0
        for left, right in products:
            total = total + rows_by_rows(left[start : start + half], right)
        return total.reshape(n, half // n, -1)

    return part(0), part(half).astype(low)


PLANE = (CONTEXT, TENSOR)


def fold_kernel(sizes, part_ref, sum_ref, inner, work, outer, send, recv):
    link = Link(sizes, send, recv)
    plane, shards = size_of(sizes, PLANE), size_of(sizes, SHARD)
    link.greet([along(sizes, group, k) for group in (PLANE, SHARD) for k in range(1, size_of(sizes, group))])
    s, c = link.index(SHARD), link.index((CONTEXT,))
    pushes = [
        link.push(part_ref.at[c ^ (k // sizes[TENSOR])], inner.at[k - 1], along(sizes, PLANE, k))
        for k in range(1, plane)
    ]
    work[...] = part_ref[c]
    for k, push in enumerate(pushes):
        push.wait()
        work[...] += inner[k]
    pushes = [link.push(work.at[s ^ k], outer.at[k - 1], along(sizes, SHARD, k)) for k in range(1, shards)]
    sum_ref[...] = work[s]
    for k, push in enumerate(pushes):
        push.wait()
        sum_ref[...] += outer[k]


def fold(part, number):
    sizes = axis_sizes()
    plane, shards = size_of(sizes, PLANE), size_of(sizes, SHARD)
    return pl.pallas_call(
        functools.partial(fold_kernel, sizes),
        out_shape=jax.ShapeDtypeStruct(part.shape[2:], full),
        in_specs=[whole_in_vmem()],
        out_specs=whole_in_vmem(),
        scratch_shapes=[
            pltpu.VMEM((plane - 1,) + part.shape[1:], full),
            pltpu.VMEM(part.shape[1:], full),
            pltpu.VMEM((shards - 1,) + part.shape[2:], full),
            pltpu.SemaphoreType.DMA((plane + shards,)),
            pltpu.SemaphoreType.DMA((plane + shards,)),
        ],
        compiler_params=talking(number, 8),
    )(part)


def adam_mlp_kernel(chunks, rates, factor_ref, *refs):
    parts, pair, down, outs = refs[: len(chunks)], refs[2:5], refs[5:8], refs[8:]
    count = parts[0].shape[0]
    block = down[0].shape[1] // count
    for part, (start, stop) in zip(parts, chunks):
        size = stop - start
        for owner in range(count):
            cols = slice(owner * block + start, owner * block + stop)
            for k in range(3):
                where = (slice(None), k, cols) if k < 2 else (slice(None), cols)
                states, results, rate = (pair, outs[:3], rates[0]) if k < 2 else (down, outs[3:], rates[1])
                grad = part[owner, :, k * size : (k + 1) * size].astype(full)
                values = adam_step(*(ref[where] for ref in states), grad, factor_ref[0], rate, weight_decay)
                for out, value in zip(results, (values[0], values[1], values[2])):
                    out[where] = value


def adam_mlp(parts, chunks, pair, down, factor, rates):
    rows = down[0].shape[0]
    step = 32 if rows % 32 == 0 else rows
    thick = pl.BlockSpec((step,) + pair[0].shape[1:], lambda i: (i, 0, 0))
    flat = pl.BlockSpec((step,) + down[0].shape[1:], lambda i: (i, 0))
    grads = [pl.BlockSpec((part.shape[0], step, part.shape[2]), lambda i: (0, i, 0)) for part in parts]
    shapes = [jax.ShapeDtypeStruct(array.shape, full) for array in (*pair, *down)]
    return pl.pallas_call(
        functools.partial(adam_mlp_kernel, chunks, rates),
        grid=(rows // step,),
        out_shape=shapes,
        in_specs=[pl.BlockSpec(memory_space=pltpu.SMEM)] + grads + [thick] * 3 + [flat] * 3,
        out_specs=[thick] * 3 + [flat] * 3,
        compiler_params=pltpu.CompilerParams(vmem_limit_bytes=28 * 2**20),
    )(factor.reshape(1), *parts, *pair, *down)


def weight_grads_kernel(count, dim, *refs):
    lefts, rights, out = refs[:count], refs[count:-1], refs[-1]
    start = 0
    for left, right in zip(lefts, rights):
        size = right.shape[1 - dim]
        out[:, start : start + size] = over(0, dim, left[...], right[...]).astype(low)
        start += size


def weight_grads(pairs, dim):
    tokens, width = pairs[0][0].shape
    cols = sum(right.shape[1 - dim] for _, right in pairs)
    step = 256
    return pl.pallas_call(
        functools.partial(weight_grads_kernel, len(pairs), dim),
        grid=(width // step,),
        out_shape=jax.ShapeDtypeStruct((width, cols), low),
        in_specs=[pl.BlockSpec((tokens, step), lambda i: (0, i))] * len(pairs)
        + [pl.BlockSpec(right.shape, lambda i: (0, 0)) for _, right in pairs],
        out_specs=pl.BlockSpec((step, cols), lambda i: (i, 0)),
        compiler_params=pltpu.CompilerParams(vmem_limit_bytes=48 * 2**20),
        cost_estimate=pl.CostEstimate(flops=2 * tokens * width * cols, bytes_accessed=0, transcendentals=0),
    )(*(left for left, _ in pairs), *(right for _, right in pairs))


def attend(query, key, value, allowed):
    scores = rows_by_rows(query, key) * HD ** (-0.5)
    scores = jnp.where(allowed, scores, masked_score)
    row_max = jnp.max(scores, axis=-1, keepdims=True)
    expanded = jnp.exp(scores - row_max)
    row_total = jnp.sum(expanded, axis=-1, keepdims=True)
    probs = (expanded / row_total).astype(low)
    return rows_by_cols(probs, value), row_max + jnp.log(row_total)


def attend_back(query, key, value, grad, log_total, allowed):
    scores = rows_by_rows(query, key) * HD ** (-0.5)
    scores = jnp.where(allowed, scores, masked_score)
    probs = jnp.exp(scores - log_total)
    grad_value = cols_by_cols(probs.astype(low), grad)
    grad_probs = rows_by_rows(grad, value)
    delta = jnp.sum(probs * grad_probs, axis=-1, keepdims=True)
    grad_scores = (probs * (grad_probs - delta)).astype(low)
    grad_query = rows_by_cols(grad_scores, key) * HD ** (-0.5)
    grad_key = cols_by_cols(grad_scores, query) * HD ** (-0.5)
    return grad_query, grad_key, grad_value


def body(
    hidden_in,
    out_grad,
    prefix_len,
    qkv_weight,
    qkv_m,
    qkv_v,
    out_weight,
    out_m,
    out_v,
    gate_up_weight,
    gate_up_m,
    gate_up_v,
    down_weight,
    down_m,
    down_v,
    gains,
    gains_m,
    gains_v,
):
    _, local_len, width = hidden_in.shape
    shards, contexts, tensors = (lax.axis_size(group) for group in (SHARD, CONTEXT, TENSOR))
    context, tensor = lax.axis_index(CONTEXT), lax.axis_index(TENSOR)
    group_size = lax.axis_size(MLP_GROUP)
    rows = qkv_weight.shape[0]
    group = H // KV
    head_cols = (group + 2) * HD
    own = local_len // tensors
    ff_block = down_weight.shape[1] // group_size
    ff_first = ff_block // 2 // 128 * 128 or ff_block // 2
    chunks = ((0, ff_first), (ff_first, ff_block))

    def to_blocks(weight, count):
        return jnp.moveaxis(weight.astype(low).reshape(rows, count, -1), 1, 0)

    def lay(blocks):
        return jnp.moveaxis(blocks, 0, 1).reshape(rows, -1).astype(full)

    (attn_part,) = bundle(
        0,
        16,
        (
            SWAP,
            (CONTEXT,),
            jnp.concatenate([to_blocks(qkv_weight, contexts), to_blocks(out_weight, contexts)], axis=2),
        ),
    )
    gain_values, attn_part = lax.optimization_barrier((gains.astype(low).astype(full), attn_part))
    (gain_blocks,) = bundle(9, 10, (STACK, SHARD, (CONTEXT,), gain_values))
    attn_full = lax.all_gather(attn_part.reshape(contexts * rows, -1), SHARD, axis=0, tiled=True)
    qkv_full, out_full = attn_full[:, :head_cols], attn_full[:, head_cols:]
    gain_rows = gain_blocks.reshape(shards * contexts, 2, rows).transpose(1, 0, 2).reshape(2, width)
    gain_attn, gain_mlp = gain_rows[0], gain_rows[1]
    inputs = lax.dynamic_slice_in_dim(hidden_in[0], tensor * own, own, 0).astype(full)
    grad_low = lax.dynamic_slice_in_dim(out_grad[0], tensor * own, own, 0)
    cotangent = grad_low.astype(full)
    scaled_one, factor_one = normalize(inputs)

    gate_up_blocks = gate_up_weight.astype(low).reshape(rows, 2, group_size, ff_block).transpose(2, 0, 1, 3)
    down_blocks = to_blocks(down_weight, group_size)

    def chunk_blocks(start, stop):
        pair = gate_up_blocks[:, :, :, start:stop]
        return jnp.concatenate([pair[:, :, 0], pair[:, :, 1], down_blocks[:, :, start:stop]], axis=2)

    def gather_mlp(part):
        return lax.all_gather(part.reshape(group_size * rows, -1), MLP_GATHER, axis=0, tiled=True)

    normed_one, part_one = bundle(
        1,
        60,
        (SPREAD, (CONTEXT,), (scaled_one * gain_attn).astype(low)),
        (SWAP, MLP_GROUP, chunk_blocks(*chunks[0])),
    )
    normed_one = normed_one.reshape(-1, width)
    mlp_full = [gather_mlp(part_one)]

    places = jnp.arange(contexts, dtype=jnp.int32) ^ context
    cores = jnp.arange(tensors, dtype=jnp.int32) ^ tensor
    positions = (
        places[None, :, None] * local_len
        + cores[:, None, None] * own
        + jnp.arange(own, dtype=jnp.int32)[None, None, :]
    ).reshape(-1)
    cosine, sine = rope_tables(positions)
    allowed = (positions[None, :] <= positions[:, None]) | (positions[None, :] < prefix_len[0])

    joined = rows_by_cols(normed_one, qkv_full)
    parts = [joined[:, i * HD : (i + 1) * HD] for i in range(group + 2)]
    queries = [rotate(part, cosine, sine).astype(low) for part in parts[:group]]
    key = rotate(parts[group], cosine, sine).astype(low)
    value = parts[group + 1].astype(low)
    mixed, log_total = zip(*[attend(query, key, value, allowed) for query in queries])
    attended = jnp.concatenate([part.astype(low) for part in mixed], axis=1)
    branch, part_two, grad_branch_mlp = bundle(
        2,
        80,
        (COLLECT, (CONTEXT,), halves([(attended, out_full)], (CONTEXT,))),
        (SWAP, MLP_GROUP, chunk_blocks(*chunks[1])),
        (SPREAD, MLP_GROUP, grad_low),
    )
    grad_branch_mlp = grad_branch_mlp.reshape(-1, width)
    mlp_full.append(gather_mlp(part_two))
    middle = inputs + branch
    scaled_two, factor_two = normalize(middle)
    (normed_two,) = bundle(3, 40, (SPREAD, MLP_GROUP, (scaled_two * gain_mlp).astype(low)))
    normed_two = normed_two.reshape(-1, width)

    sums, back_products, out_products = [], [], []
    for place, (start, stop) in enumerate(chunks):
        size = stop - start
        weights = mlp_full[place]
        pair_weights, down_weights = weights[:, : 2 * size], weights[:, 2 * size :]
        gate_up = rows_by_cols(normed_two, pair_weights)
        gate, up_part = gate_up[:, :size], gate_up[:, size:]
        sigmoid_gate = jax.nn.sigmoid(gate)
        activated = gate * sigmoid_gate
        hidden = (activated * up_part).astype(low)
        grad_hidden = rows_by_cols(grad_branch_mlp, down_weights)
        grad_gate = grad_hidden * up_part * sigmoid_gate * (1.0 + gate * (1.0 - sigmoid_gate))
        grad_up = grad_hidden * activated
        grad_rows = jnp.concatenate([grad_gate, grad_up], axis=1).astype(low)
        grads = weight_grads([(normed_two, grad_rows), (grad_branch_mlp, hidden)], 0)
        grad_rows, grads = lax.optimization_barrier((grad_rows, grads))
        if sums:
            grads, sums[0] = lax.optimization_barrier((grads, sums[0]))
        else:
            grads, mlp_full[1] = lax.optimization_barrier((grads, mlp_full[1]))
        sums.append(lax.psum_scatter(grads, MLP_GATHER, scatter_dimension=0, tiled=True))
        back_products.append((grad_rows, pair_weights))
        out_products.append((hidden, down_weights))

    (grad_normed_two,) = bundle(4, 40, (COLLECT, MLP_GROUP, halves(back_products, MLP_GROUP)))
    grad_gain_mlp = jnp.sum(grad_normed_two * scaled_two, axis=0)
    grad_middle = cotangent + norm_back(grad_normed_two * gain_mlp, scaled_two, factor_two)
    grad_middle, sums[0] = lax.optimization_barrier((grad_middle, sums[0]))
    grad_branch_attn, mlp_branch, parts_one = bundle(
        5,
        80,
        (SPREAD, (CONTEXT,), grad_middle.astype(low)),
        (COLLECT, MLP_GROUP, halves(out_products, MLP_GROUP)),
        (SWAP, MLP_GROUP, sums[0].reshape(group_size, rows, -1)),
    )
    out_own = (middle + mlp_branch).astype(low)
    grad_branch_attn = grad_branch_attn.reshape(-1, width)
    grad_attended = rows_by_cols(grad_branch_attn, out_full).astype(low)

    grad_queries = []
    grad_key = 0.0
    grad_value = 0.0
    for i in range(group):
        grad_query, key_part, value_part = attend_back(
            queries[i], key, value, grad_attended[:, i * HD : (i + 1) * HD], log_total[i], allowed
        )
        grad_queries.append(unrotate(grad_query, cosine, sine))
        grad_key = grad_key + key_part
        grad_value = grad_value + value_part
    grad_joined = jnp.concatenate(
        grad_queries + [unrotate(grad_key, cosine, sine), grad_value], axis=1
    ).astype(low)
    grad_attn = weight_grads([(normed_one, grad_joined.T), (grad_branch_attn, attended.T)], 1)
    grad_joined, grad_attn = lax.optimization_barrier((grad_joined, grad_attn))
    grad_attn, sum_two = lax.optimization_barrier((grad_attn, sums[1]))
    attn_sum = lax.psum_scatter(grad_attn, SHARD, scatter_dimension=0, tiled=True)
    grad_normed_one, parts_two = bundle(
        6,
        55,
        (COLLECT, (CONTEXT,), halves([(grad_joined, qkv_full)], (CONTEXT,))),
        (SWAP, MLP_GROUP, sum_two.reshape(group_size, rows, -1)),
    )
    grad_gain_attn = jnp.sum(grad_normed_one * scaled_one, axis=0)
    grad_inputs = grad_middle + norm_back(grad_normed_one * gain_attn, scaled_one, factor_one)
    grad_own = grad_inputs.astype(low)

    def both_cores(values):
        other = lax.ppermute(values, TENSOR, [(0, 1), (1, 0)])
        return jnp.where(tensor == 0, jnp.concatenate([values, other]), jnp.concatenate([other, values]))[None]

    hidden_out = both_cores(out_own)
    hidden_grad = both_cores(grad_own)
    gain_part = jnp.stack([grad_gain_attn, grad_gain_mlp]).reshape(2, shards, contexts, rows)
    owned_gains = fold(gain_part.transpose(2, 1, 0, 3), 7)

    squares = jnp.sum(owned_gains * owned_gains) / tensors
    for owned in (sums[0], sum_two):
        owned = owned.astype(full)
        squares = squares + jnp.sum(owned * owned)
    attn_sum, squares, hidden_out, hidden_grad = lax.optimization_barrier(
        (attn_sum, squares, hidden_out, hidden_grad)
    )
    total, attn_parts = bundle(
        8,
        20,
        (TOTAL, PLANE, SHARD, (jnp.full((8, 128), squares, full), attn_sum)),
        (SWAP, (CONTEXT,), attn_sum.reshape(contexts, rows, -1)),
    )
    grad_norm = jnp.sqrt(total[0, 0])
    owned_qkv = lay(attn_parts[:, :, :head_cols])
    owned_out = lay(attn_parts[:, :, head_cols:])
    factor = jnp.minimum(1.0, clip_limit / grad_norm)

    qkv_out = adam_step(qkv_weight, qkv_m, qkv_v, owned_qkv, factor, 2.0 * (D / 2) ** (-0.5), weight_decay)
    out_out = adam_step(
        out_weight, out_m, out_v, owned_out, factor, 2.0 * (H * HD / 16) ** (-0.5), weight_decay
    )
    mlp_out = adam_mlp(
        (parts_one, parts_two),
        chunks,
        (gate_up_weight, gate_up_m, gate_up_v),
        (down_weight, down_m, down_v),
        factor,
        (2.0 * D ** (-0.5), 2.0 * FF ** (-0.5)),
    )
    gains_out = adam_step(gains, gains_m, gains_v, owned_gains, factor, 0.8, 0.0)
    return (hidden_out, hidden_grad, grad_norm, *qkv_out, *out_out, *mlp_out, *gains_out)


def solution(mesh):
    shards, contexts, tensors = mesh.devices.shape
    fine = Mesh(mesh.devices.reshape(shards // 2, 2, contexts, tensors), AXES)
    tokens = P(SHARD, CONTEXT, None)
    rows = (HIGH, LOW, CONTEXT)
    flat = P(rows, TENSOR)
    paired = P(rows, None, TENSOR)
    gains = P(None, rows)
    states = (flat,) * 6 + (paired,) * 3 + (flat,) * 3 + (gains,) * 3
    return jax.shard_map(
        body,
        mesh=fine,
        in_specs=(tokens, tokens, P(SHARD)) + states,
        out_specs=(tokens, tokens, P()) + states,
        check_vma=False,
    )
```

```python
import functools

import jax
import jax.numpy as jnp
from jax import lax
from jax.experimental import pallas as pl
from jax.experimental.pallas import tpu as pltpu
from jax.sharding import Mesh
from jax.sharding import PartitionSpec as P

D = 2560
H = 32
KV = 8
HD = 80
FF = 7168
STEP = 8


norm_epsilon = 1e-05
rope_theta = 1000000.0
masked_score = -1e30
clip_limit = 1.0
beta_first = 0.9
beta_second = 0.95
adam_epsilon = 1e-08
weight_decay = 0.1

HIGH, LOW, CONTEXT, TENSOR = "high", "low", "context", "tensor"
SHARD = (HIGH, LOW)
AXES = (HIGH, LOW, CONTEXT, TENSOR)
SWAP, STACK, SPREAD, COLLECT, TOTAL = "swap", "stack", "spread", "collect", "total"
MLP_GROUP = (CONTEXT,)
MLP_GATHER = (HIGH, LOW)
MESH = pl.DeviceIdType.MESH
low = jnp.bfloat16
full = jnp.float32


def rope_tables(positions):
    half = HD // 2
    exponent = jnp.arange(half, dtype=full) * (2.0 / HD)
    frequency = rope_theta ** (-exponent)
    angles = positions.astype(full)[:, None] * frequency[None, :]
    angles = jnp.concatenate([angles, angles], axis=-1)
    return (jnp.cos(angles), jnp.sin(angles))


def rotate(values, cosine, sine):
    half = values.shape[-1] // 2
    turned = jnp.concatenate([-values[..., half:], values[..., :half]], axis=-1)
    return values * cosine + turned * sine


def unrotate(values, cosine, sine):
    half = values.shape[-1] // 2
    turned = jnp.concatenate([-values[..., half:], values[..., :half]], axis=-1)
    return values * cosine - turned * sine


def normalize(values):
    factor = lax.rsqrt(jnp.mean(values * values, axis=-1, keepdims=True) + norm_epsilon)
    return (values * factor, factor)


def norm_back(grad_scaled, scaled, factor):
    return factor * (grad_scaled - scaled * jnp.mean(grad_scaled * scaled, axis=-1, keepdims=True))


def adam_step(weight, first, second, grad, factor, rate, decay):
    grad = grad * factor
    first_new = beta_first * first + (1.0 - beta_first) * grad
    second_new = beta_second * second + (1.0 - beta_second) * grad * grad
    first_scale, second_scale = 1.0 / (1.0 - beta_first**STEP), 1.0 / (1.0 - beta_second**STEP)
    corrected = first_new * first_scale / (jnp.sqrt(second_new * second_scale) + adam_epsilon)
    return (first_new, second_new, weight - rate * (corrected + decay * weight))


def over(left_dim, right_dim, left, right):
    return lax.dot_general(left, right, (((left_dim,), (right_dim,)), ((), ())), preferred_element_type=full)


rows_by_cols = functools.partial(over, 1, 0)
rows_by_rows = functools.partial(over, 1, 1)
cols_by_cols = functools.partial(over, 0, 0)


class Link:
    def __init__(self, sizes, send, recv):
        self.sizes, self.send, self.recv, self.used = sizes, send, recv, 0
        self.place = tuple(lax.axis_index(axis) for axis in AXES)

    def device(self, offset):
        return {axis: here ^ by for axis, here, by in zip(AXES, self.place, offset)}

    def index(self, group):
        index = 0
        for axis, here in zip(AXES, self.place):
            if axis in group:
                index = index * self.sizes[axis] + here
        return index

    def greet(self, partners):
        barrier = pltpu.get_barrier_semaphore()
        for offset in partners:
            pl.semaphore_signal(barrier, inc=1, device_id=self.device(offset), device_id_type=MESH)
        pl.semaphore_wait(barrier, len(partners))

    def push(self, src, dst, offset):
        copy = pltpu.make_async_remote_copy(
            src_ref=src,
            dst_ref=dst,
            send_sem=self.send.at[self.used],
            recv_sem=self.recv.at[self.used],
            device_id=self.device(offset),
            device_id_type=MESH,
        )
        self.used += 1
        copy.start()
        return copy

    def keep(self, src, dst):
        copy = pltpu.make_async_copy(src, dst, self.send.at[self.used])
        self.used += 1
        copy.start()
        return copy


MATE = (0, 0, 0, 1)


def axis_sizes():
    return {axis: lax.axis_size(axis) for axis in AXES}


def size_of(sizes, group):
    size = 1
    for axis in group:
        size *= sizes[axis]
    return size


def along(sizes, group, k):
    offset = []
    for axis in reversed(AXES):
        by = 0
        if axis in group:
            k, by = divmod(k, sizes[axis])
        offset.append(by)
    return tuple(reversed(offset))


def partners_of(jobs, sizes):
    found = set()
    for job in jobs:
        for group in job[1:]:
            n = size_of(sizes, group)
            steps = [1 << i for i in range(n.bit_length() - 1)] if job[0] in (SPREAD, COLLECT) else range(1, n)
            found |= {along(sizes, group, k) for k in steps}
        if job[0] in (SPREAD, COLLECT):
            found.add(MATE)
    return sorted(found)


def lanes(width, count):
    tiles, start, runs = width // 128, 0, []
    for i in range(count):
        size = 128 * ((tiles + count - 1 - i) // count)
        runs.append((start, size))
        start += size
    return runs


def turns(n, width):
    bits = [1 << i for i in range(n.bit_length() - 1)]
    return [(pl.ds(*run), bits[i:] + bits[:i]) for i, run in enumerate(lanes(width, len(bits)))]


class Swap:
    copies = staticmethod(lambda sizes, job, n: n)

    def __init__(self, link, job, sources, target, extras):
        (src,), group = sources, job[-1]
        me = link.index(group)
        self.ends = [
            link.push(src.at[me ^ k], target.at[me], along(link.sizes, group, k))
            for k in range(1, size_of(link.sizes, group))
        ]
        self.ends.append(link.keep(src.at[me], target.at[me]))

    def step(self, turn):
        pass

    def finish(self):
        for end in self.ends:
            end.wait()


class Stack:
    copies = staticmethod(lambda sizes, job, n: n + size_of(sizes, job[1]))

    def __init__(self, link, job, sources, target, extras):
        (src,), (_, outer, inner) = sources, job
        slot = target.at[link.index(outer), link.index(inner)]
        self.pieces = [link.push(src, slot, along(link.sizes, inner, k)) for k in range(1, size_of(link.sizes, inner))]
        self.pieces.append(link.keep(src, slot))
        self.link, self.outer, self.target = link, outer, target

    def step(self, turn):
        pass

    def finish(self):
        for piece in self.pieces:
            piece.wait()
        link, row = self.link, self.target.at[self.link.index(self.outer)]
        ends = [
            link.push(row, row, along(link.sizes, self.outer, k)) for k in range(1, size_of(link.sizes, self.outer))
        ]
        for end in ends:
            end.wait()


class Spread:
    copies = staticmethod(lambda sizes, job, n: 2 + 2 * (n - 1) * (n.bit_length() - 1))

    def __init__(self, link, job, sources, target, extras):
        (self.src,), self.group = sources, job[-1]
        self.link, self.target = link, target
        self.routes = turns(size_of(link.sizes, self.group), self.src.shape[1])
        self.held = [[0] for _ in self.routes]
        self.flying = [[] for _ in self.routes]
        self.sent, self.ends = [], []
        self.step(0)
        self.ends.append(link.push(self.src, target.at[1, 0], MATE))
        self.ends.append(link.keep(self.src, target.at[0, 0]))

    def land(self, i):
        run = self.routes[i][0]
        for k, copy in self.flying[i]:
            copy.wait_recv()
            self.held[i].append(k)
            self.ends.append(self.link.push(self.target.at[0, k, :, run], self.target.at[1, k, :, run], MATE))
        self.flying[i] = []

    def step(self, turn):
        for i, (run, bits) in enumerate(self.routes):
            if turn >= len(bits):
                continue
            arrived = self.flying[i]
            for _, copy in arrived:
                copy.wait_recv()
            bit = bits[turn]
            offset = along(self.link.sizes, self.group, bit)
            held = self.held[i] + [k for k, _ in arrived]
            flying = []
            for k in held:
                src = self.src.at[:, run] if k == 0 else self.target.at[0, k, :, run]
                copy = self.link.push(src, self.target.at[0, k ^ bit, :, run], offset)
                flying.append((k ^ bit, copy))
                self.sent.append(copy)
            for k, _ in arrived:
                here, there = self.target.at[0, k, :, run], self.target.at[1, k, :, run]
                self.ends.append(self.link.push(here, there, MATE))
            self.held[i], self.flying[i] = held, flying

    def finish(self):
        for i, _ in enumerate(self.routes):
            self.land(i)
        for copy in self.sent:
            copy.wait_send()
        for end in self.ends:
            end.wait()


class Collect:
    copies = staticmethod(lambda sizes, job, n: n + (n - 1) * (n.bit_length() - 1))

    def __init__(self, link, job, sources, target, extras):
        (self.near, self.far), self.group = sources, job[-1]
        (self.mates, self.got), self.link, self.target = extras, link, target
        n = size_of(link.sizes, self.group)
        self.routes = turns(n, self.near.shape[2])
        self.left = [list(range(n)) for _ in self.routes]
        self.adds = [{k: [] for k in range(n)} for _ in self.routes]
        self.places = [0 for _ in self.routes]
        self.sent = []
        self.crossed = set()
        self.crossing = {k: link.push(self.far.at[k], self.mates.at[k], MATE) for k in reversed(range(n))}

    def value(self, i, k):
        run = self.routes[i][0]
        if k not in self.crossed:
            self.crossing[k].wait_recv()
            self.crossed.add(k)
        total = self.near[k, :, run] + self.mates[k, :, run].astype(full)
        for place, copy in self.adds[i][k]:
            copy.wait_recv()
            total = total + self.got[place, :, run].astype(full)
        return total

    def step(self, turn):
        for i, (run, bits) in enumerate(self.routes):
            if turn >= len(bits):
                continue
            bit = bits[turn]
            offset = along(self.link.sizes, self.group, bit)
            for k in [k for k in self.left[i] if k & bit]:
                self.mates[k, :, run] = self.value(i, k).astype(low)
                place = self.places[i]
                copy = self.link.push(self.mates.at[k, :, run], self.got.at[place, :, run], offset)
                self.adds[i][k ^ bit].append((place, copy))
                self.sent.append(copy)
                self.places[i] += 1
            self.left[i] = [k for k in self.left[i] if not k & bit]

    def finish(self):
        for i, (run, _) in enumerate(self.routes):
            self.target[:, run] = self.value(i, 0)
        for copy in self.sent + list(self.crossing.values()):
            copy.wait_send()


class Total:
    copies = staticmethod(lambda sizes, job, n: sum(size_of(sizes, group) for group in job[1:]))

    def __init__(self, link, job, sources, target, extras):
        (tile, array), (self.held,) = sources, extras
        self.link, self.groups, self.target, self.slot = link, list(job[1:]), target, 0
        values = array[...].astype(full)
        target[...] = tile[...] + jnp.sum(values * values)
        self.ask()

    def ask(self):
        link, held, slot, group = self.link, self.held, self.slot, self.groups.pop(0)
        n = size_of(link.sizes, group)
        held[slot] = self.target[...]
        self.pushes = [link.push(held.at[slot], held.at[slot + k], along(link.sizes, group, k)) for k in range(1, n)]

    def step(self, turn):
        pass

    def finish(self):
        while True:
            for push in self.pushes:
                push.wait()
            for k, _ in enumerate(self.pushes):
                self.target[...] += self.held[self.slot + 1 + k]
            self.slot += 1 + len(self.pushes)
            if not self.groups:
                return
            self.ask()


KINDS = {SWAP: Swap, STACK: Stack, SPREAD: Spread, COLLECT: Collect, TOTAL: Total}
EXTRAS = {COLLECT: 2, TOTAL: 1}


def bundle_kernel(jobs, sizes, *refs):
    refs = list(refs)
    take = lambda count: [refs.pop(0) for _ in range(count)]
    sources = [take(2 if job[0] in EXTRAS else 1) for job in jobs]
    targets = [take(1)[0] for job in jobs]
    extras = [take(EXTRAS.get(job[0], 0)) for job in jobs]
    link = Link(sizes, *refs)
    link.greet(partners_of(jobs, sizes))
    running = [KINDS[job[0]](link, job, *rest) for job, *rest in zip(jobs, sources, targets, extras)]
    most = max(size_of(sizes, job[-1]).bit_length() - 1 for job in jobs)
    for turn in range(most):
        for job, work in zip(jobs, running):
            if job[0] == COLLECT or turn:
                work.step(turn)
    for work in running:
        if not isinstance(work, Swap):
            work.finish()
    for work in running:
        if isinstance(work, Swap):
            work.finish()


def whole_in_vmem():
    return pl.BlockSpec(memory_space=pltpu.VMEM)


def talking(number, mib):
    return pltpu.CompilerParams(collective_id=number, has_side_effects=True, vmem_limit_bytes=mib * 2**20)


def bundle(number, micros, *jobs):
    sizes = axis_sizes()
    anywhere = pl.BlockSpec(memory_space=pl.ANY)
    flat, in_specs, out_specs, shapes, scratch, copies, held = [], [], [], [], [], 0, 0
    for *job, array in jobs:
        kind, n = job[0], size_of(sizes, job[-1])
        copies += KINDS[kind].copies(sizes, job, n)
        if kind == COLLECT:
            near, far = array
            flat += [near, far]
            in_specs += [whole_in_vmem(), anywhere]
            out_specs.append(whole_in_vmem())
            shapes.append(jax.ShapeDtypeStruct(near.shape[1:], full))
            scratch += [pltpu.VMEM(far.shape, low), pltpu.VMEM((n - 1,) + far.shape[1:], low)]
            held += 10 * near.size
            continue
        if kind == TOTAL:
            flat += array
            in_specs += [whole_in_vmem()] * 2
            out_specs.append(whole_in_vmem())
            shapes.append(jax.ShapeDtypeStruct(array[0].shape, full))
            scratch.append(pltpu.VMEM((KINDS[kind].copies(sizes, job, n),) + array[0].shape, full))
            held += 2 * array[1].size
            continue
        flat.append(array)
        in_specs.append(anywhere)
        out_specs.append(anywhere)
        shape = array.shape
        if kind == STACK:
            shape = (size_of(sizes, job[1]), n) + shape
        elif kind == SPREAD:
            shape = (2, n) + shape
        shapes.append(jax.ShapeDtypeStruct(shape, array.dtype))
    return pl.pallas_call(
        functools.partial(bundle_kernel, tuple(tuple(job[:-1]) for job in jobs), sizes),
        out_shape=shapes,
        in_specs=in_specs,
        out_specs=out_specs,
        scratch_shapes=scratch + [pltpu.SemaphoreType.DMA((copies,)), pltpu.SemaphoreType.DMA((copies,))],
        compiler_params=talking(number, 6 + held // 2**20),
        cost_estimate=pl.CostEstimate(flops=int(micros * 8e8), bytes_accessed=0, transcendentals=0),
    )(*flat)


def halves(products, group):
    n = lax.axis_size(group)
    half = products[0][0].shape[0] // 2

    def part(start):
        total = 0.0
        for left, right in products:
            total = total + rows_by_rows(left[start : start + half], right)
        return total.reshape(n, half // n, -1)

    return part(0), part(half).astype(low)


PLANE = (CONTEXT, TENSOR)


def fold_kernel(sizes, part_ref, sum_ref, inner, work, outer, send, recv):
    link = Link(sizes, send, recv)
    plane, shards = size_of(sizes, PLANE), size_of(sizes, SHARD)
    link.greet([along(sizes, group, k) for group in (PLANE, SHARD) for k in range(1, size_of(sizes, group))])
    s, c = link.index(SHARD), link.index((CONTEXT,))
    pushes = [
        link.push(part_ref.at[c ^ (k // sizes[TENSOR])], inner.at[k - 1], along(sizes, PLANE, k))
        for k in range(1, plane)
    ]
    work[...] = part_ref[c]
    for k, push in enumerate(pushes):
        push.wait()
        work[...] += inner[k]
    pushes = [link.push(work.at[s ^ k], outer.at[k - 1], along(sizes, SHARD, k)) for k in range(1, shards)]
    sum_ref[...] = work[s]
    for k, push in enumerate(pushes):
        push.wait()
        sum_ref[...] += outer[k]


def fold(part, number):
    sizes = axis_sizes()
    plane, shards = size_of(sizes, PLANE), size_of(sizes, SHARD)
    return pl.pallas_call(
        functools.partial(fold_kernel, sizes),
        out_shape=jax.ShapeDtypeStruct(part.shape[2:], full),
        in_specs=[whole_in_vmem()],
        out_specs=whole_in_vmem(),
        scratch_shapes=[
            pltpu.VMEM((plane - 1,) + part.shape[1:], full),
            pltpu.VMEM(part.shape[1:], full),
            pltpu.VMEM((shards - 1,) + part.shape[2:], full),
            pltpu.SemaphoreType.DMA((plane + shards,)),
            pltpu.SemaphoreType.DMA((plane + shards,)),
        ],
        compiler_params=talking(number, 8),
    )(part)


def adam_kernel(chunks, head_cols, rates, factor_ref, *refs):
    count = len(chunks)
    parts, attn_part = refs[:count], refs[count]
    states, outs = refs[count + 1 : count + 13], refs[count + 13 : count + 25]
    grads = refs[count + 25 :]
    qkv, out, pair, down = ((states[i : i + 3], outs[i : i + 3], rates[i // 3]) for i in range(0, 12, 3))
    factor = factor_ref[0]

    def update(weight, where, grad):
        old, new, rate = weight
        first, second, fresh = adam_step(*(ref[where] for ref in old), grad, factor, rate, weight_decay)
        new[0][where], new[1][where], new[2][where] = first, second, fresh

    owners = attn_part.shape[0]
    for weight, grad, start in ((qkv, grads[0], 0), (out, grads[1], head_cols)):
        size = grad.shape[1] // owners
        for owner in range(owners):
            grad[:, owner * size : (owner + 1) * size] = attn_part[owner, :, start : start + size].astype(full)
        update(weight, slice(None), grad[...])
    owners = parts[0].shape[0]
    block = down[0][0].shape[1] // owners
    for part, (start, stop) in zip(parts, chunks):
        size = stop - start
        for owner in range(owners):
            cols = slice(owner * block + start, owner * block + stop)
            update(pair, (slice(None), 0, cols), part[owner, :, :size].astype(full))
            update(pair, (slice(None), 1, cols), part[owner, :, size : 2 * size].astype(full))
            update(down, (slice(None), cols), part[owner, :, 2 * size :].astype(full))


def adam_all(parts, chunks, attn_part, head_cols, weights, factor, rates):
    rows = weights[0].shape[0]
    step = 32 if rows % 32 == 0 else rows

    def state_block(array):
        rest = array.shape[1:]
        return pl.BlockSpec((step,) + rest, lambda i: (i,) + (0,) * len(rest))

    blocks = [state_block(array) for array in weights]
    grads = [pl.BlockSpec((part.shape[0], step, part.shape[2]), lambda i: (0, i, 0)) for part in (*parts, attn_part)]
    row_bytes = sum(array.size // rows for array in weights) * 16 + sum(p.shape[0] * p.shape[2] for p in parts) * 8
    return pl.pallas_call(
        functools.partial(adam_kernel, chunks, head_cols, rates),
        grid=(rows // step,),
        out_shape=[jax.ShapeDtypeStruct(array.shape, full) for array in weights],
        in_specs=[pl.BlockSpec(memory_space=pltpu.SMEM)] + grads + blocks,
        out_specs=blocks,
        scratch_shapes=[pltpu.VMEM((step, weights[i].shape[1]), full) for i in (0, 3)],
        compiler_params=pltpu.CompilerParams(vmem_limit_bytes=58 * 2**20),
    )(factor.reshape(1), *parts, attn_part, *weights)


def weight_grads_kernel(count, dim, *refs):
    lefts, rights, out = refs[:count], refs[count:-1], refs[-1]
    start = 0
    for left, right in zip(lefts, rights):
        size = right.shape[1 - dim]
        out[:, start : start + size] = over(0, dim, left[...], right[...]).astype(low)
        start += size


def weight_grads(pairs, dim):
    tokens, width = pairs[0][0].shape
    cols = sum(right.shape[1 - dim] for _, right in pairs)
    step = 256
    return pl.pallas_call(
        functools.partial(weight_grads_kernel, len(pairs), dim),
        grid=(width // step,),
        out_shape=jax.ShapeDtypeStruct((width, cols), low),
        in_specs=[pl.BlockSpec((tokens, step), lambda i: (0, i))] * len(pairs)
        + [pl.BlockSpec(right.shape, lambda i: (0, 0)) for _, right in pairs],
        out_specs=pl.BlockSpec((step, cols), lambda i: (i, 0)),
        compiler_params=pltpu.CompilerParams(vmem_limit_bytes=48 * 2**20),
        cost_estimate=pl.CostEstimate(flops=2 * tokens * width * cols, bytes_accessed=0, transcendentals=0),
    )(*(left for left, _ in pairs), *(right for _, right in pairs))


def attend(query, key, value, allowed):
    scores = rows_by_rows(query, key) * HD ** (-0.5)
    scores = jnp.where(allowed, scores, masked_score)
    row_max = jnp.max(scores, axis=-1, keepdims=True)
    expanded = jnp.exp(scores - row_max)
    row_total = jnp.sum(expanded, axis=-1, keepdims=True)
    probs = (expanded / row_total).astype(low)
    return rows_by_cols(probs, value), row_max + jnp.log(row_total)


def attend_back(query, key, value, grad, log_total, allowed):
    scores = rows_by_rows(query, key) * HD ** (-0.5)
    scores = jnp.where(allowed, scores, masked_score)
    probs = jnp.exp(scores - log_total)
    grad_value = cols_by_cols(probs.astype(low), grad)
    grad_probs = rows_by_rows(grad, value)
    delta = jnp.sum(probs * grad_probs, axis=-1, keepdims=True)
    grad_scores = (probs * (grad_probs - delta)).astype(low)
    grad_query = rows_by_cols(grad_scores, key) * HD ** (-0.5)
    grad_key = cols_by_cols(grad_scores, query) * HD ** (-0.5)
    return grad_query, grad_key, grad_value


def body(
    hidden_in,
    out_grad,
    prefix_len,
    qkv_weight,
    qkv_m,
    qkv_v,
    out_weight,
    out_m,
    out_v,
    gate_up_weight,
    gate_up_m,
    gate_up_v,
    down_weight,
    down_m,
    down_v,
    gains,
    gains_m,
    gains_v,
):
    _, local_len, width = hidden_in.shape
    shards, contexts, tensors = (lax.axis_size(group) for group in (SHARD, CONTEXT, TENSOR))
    context, tensor = lax.axis_index(CONTEXT), lax.axis_index(TENSOR)
    group_size = lax.axis_size(MLP_GROUP)
    rows = qkv_weight.shape[0]
    group = H // KV
    head_cols = (group + 2) * HD
    own = local_len // tensors
    ff_block = down_weight.shape[1] // group_size
    ff_first = ff_block // 2 // 128 * 128 or ff_block // 2
    chunks = ((0, ff_first), (ff_first, ff_block))

    def to_blocks(weight, count):
        return jnp.moveaxis(weight.astype(low).reshape(rows, count, -1), 1, 0)

    (attn_part,) = bundle(
        0,
        16,
        (
            SWAP,
            (CONTEXT,),
            jnp.concatenate([to_blocks(qkv_weight, contexts), to_blocks(out_weight, contexts)], axis=2),
        ),
    )
    gain_values, attn_part = lax.optimization_barrier((gains.astype(low).astype(full), attn_part))
    (gain_blocks,) = bundle(9, 10, (STACK, SHARD, (CONTEXT,), gain_values))
    attn_full = lax.all_gather(attn_part.reshape(contexts * rows, -1), SHARD, axis=0, tiled=True)
    qkv_full, out_full = attn_full[:, :head_cols], attn_full[:, head_cols:]
    gain_rows = gain_blocks.reshape(shards * contexts, 2, rows).transpose(1, 0, 2).reshape(2, width)
    gain_attn, gain_mlp = gain_rows[0], gain_rows[1]
    inputs = lax.dynamic_slice_in_dim(hidden_in[0], tensor * own, own, 0).astype(full)
    grad_low = lax.dynamic_slice_in_dim(out_grad[0], tensor * own, own, 0)
    cotangent = grad_low.astype(full)
    scaled_one, factor_one = normalize(inputs)

    gate_up_blocks = gate_up_weight.astype(low).reshape(rows, 2, group_size, ff_block).transpose(2, 0, 1, 3)
    down_blocks = to_blocks(down_weight, group_size)

    def chunk_blocks(start, stop):
        pair = gate_up_blocks[:, :, :, start:stop]
        return jnp.concatenate([pair[:, :, 0], pair[:, :, 1], down_blocks[:, :, start:stop]], axis=2)

    def gather_mlp(part):
        return lax.all_gather(part.reshape(group_size * rows, -1), MLP_GATHER, axis=0, tiled=True)

    normed_one, part_one = bundle(
        1,
        60,
        (SPREAD, (CONTEXT,), (scaled_one * gain_attn).astype(low)),
        (SWAP, MLP_GROUP, chunk_blocks(*chunks[0])),
    )
    normed_one = normed_one.reshape(-1, width)
    mlp_full = [gather_mlp(part_one)]

    places = jnp.arange(contexts, dtype=jnp.int32) ^ context
    cores = jnp.arange(tensors, dtype=jnp.int32) ^ tensor
    positions = (
        places[None, :, None] * local_len
        + cores[:, None, None] * own
        + jnp.arange(own, dtype=jnp.int32)[None, None, :]
    ).reshape(-1)
    cosine, sine = rope_tables(positions)
    allowed = (positions[None, :] <= positions[:, None]) | (positions[None, :] < prefix_len[0])

    joined = rows_by_cols(normed_one, qkv_full)
    parts = [joined[:, i * HD : (i + 1) * HD] for i in range(group + 2)]
    queries = [rotate(part, cosine, sine).astype(low) for part in parts[:group]]
    key = rotate(parts[group], cosine, sine).astype(low)
    value = parts[group + 1].astype(low)
    mixed, log_total = zip(*[attend(query, key, value, allowed) for query in queries])
    attended = jnp.concatenate([part.astype(low) for part in mixed], axis=1)
    branch, part_two, grad_branch_mlp = bundle(
        2,
        80,
        (COLLECT, (CONTEXT,), halves([(attended, out_full)], (CONTEXT,))),
        (SWAP, MLP_GROUP, chunk_blocks(*chunks[1])),
        (SPREAD, MLP_GROUP, grad_low),
    )
    grad_branch_mlp = grad_branch_mlp.reshape(-1, width)
    mlp_full.append(gather_mlp(part_two))
    middle = inputs + branch
    scaled_two, factor_two = normalize(middle)
    (normed_two,) = bundle(3, 40, (SPREAD, MLP_GROUP, (scaled_two * gain_mlp).astype(low)))
    normed_two = normed_two.reshape(-1, width)

    sums, back_products, out_products = [], [], []
    for place, (start, stop) in enumerate(chunks):
        size = stop - start
        weights = mlp_full[place]
        pair_weights, down_weights = weights[:, : 2 * size], weights[:, 2 * size :]
        gate_up = rows_by_cols(normed_two, pair_weights)
        gate, up_part = gate_up[:, :size], gate_up[:, size:]
        sigmoid_gate = jax.nn.sigmoid(gate)
        activated = gate * sigmoid_gate
        hidden = (activated * up_part).astype(low)
        grad_hidden = rows_by_cols(grad_branch_mlp, down_weights)
        grad_gate = grad_hidden * up_part * sigmoid_gate * (1.0 + gate * (1.0 - sigmoid_gate))
        grad_up = grad_hidden * activated
        grad_rows = jnp.concatenate([grad_gate, grad_up], axis=1).astype(low)
        grads = weight_grads([(normed_two, grad_rows), (grad_branch_mlp, hidden)], 0)
        grad_rows, grads = lax.optimization_barrier((grad_rows, grads))
        if sums:
            grads, sums[0] = lax.optimization_barrier((grads, sums[0]))
        else:
            grads, mlp_full[1] = lax.optimization_barrier((grads, mlp_full[1]))
        sums.append(lax.psum_scatter(grads, MLP_GATHER, scatter_dimension=0, tiled=True))
        back_products.append((grad_rows, pair_weights))
        out_products.append((hidden, down_weights))

    (grad_normed_two,) = bundle(4, 40, (COLLECT, MLP_GROUP, halves(back_products, MLP_GROUP)))
    grad_gain_mlp = jnp.sum(grad_normed_two * scaled_two, axis=0)
    grad_middle = cotangent + norm_back(grad_normed_two * gain_mlp, scaled_two, factor_two)
    grad_middle, sums[0] = lax.optimization_barrier((grad_middle, sums[0]))
    grad_branch_attn, mlp_branch, parts_one = bundle(
        5,
        80,
        (SPREAD, (CONTEXT,), grad_middle.astype(low)),
        (COLLECT, MLP_GROUP, halves(out_products, MLP_GROUP)),
        (SWAP, MLP_GROUP, sums[0].reshape(group_size, rows, -1)),
    )
    out_own = (middle + mlp_branch).astype(low)
    grad_branch_attn = grad_branch_attn.reshape(-1, width)
    grad_attended = rows_by_cols(grad_branch_attn, out_full).astype(low)

    grad_queries = []
    grad_key = 0.0
    grad_value = 0.0
    for i in range(group):
        grad_query, key_part, value_part = attend_back(
            queries[i], key, value, grad_attended[:, i * HD : (i + 1) * HD], log_total[i], allowed
        )
        grad_queries.append(unrotate(grad_query, cosine, sine))
        grad_key = grad_key + key_part
        grad_value = grad_value + value_part
    grad_joined = jnp.concatenate(
        grad_queries + [unrotate(grad_key, cosine, sine), grad_value], axis=1
    ).astype(low)
    grad_attn = weight_grads([(normed_one, grad_joined.T), (grad_branch_attn, attended.T)], 1)
    grad_joined, grad_attn = lax.optimization_barrier((grad_joined, grad_attn))
    grad_attn, sum_two = lax.optimization_barrier((grad_attn, sums[1]))
    attn_sum = lax.psum_scatter(grad_attn, SHARD, scatter_dimension=0, tiled=True)
    grad_normed_one, parts_two = bundle(
        6,
        55,
        (COLLECT, (CONTEXT,), halves([(grad_joined, qkv_full)], (CONTEXT,))),
        (SWAP, MLP_GROUP, sum_two.reshape(group_size, rows, -1)),
    )
    grad_gain_attn = jnp.sum(grad_normed_one * scaled_one, axis=0)
    grad_inputs = grad_middle + norm_back(grad_normed_one * gain_attn, scaled_one, factor_one)
    grad_own = grad_inputs.astype(low)

    def both_cores(values):
        other = lax.ppermute(values, TENSOR, [(0, 1), (1, 0)])
        return jnp.where(tensor == 0, jnp.concatenate([values, other]), jnp.concatenate([other, values]))[None]

    hidden_out = both_cores(out_own)
    hidden_grad = both_cores(grad_own)
    gain_part = jnp.stack([grad_gain_attn, grad_gain_mlp]).reshape(2, shards, contexts, rows)
    owned_gains = fold(gain_part.transpose(2, 1, 0, 3), 7)

    squares = jnp.sum(owned_gains * owned_gains) / tensors
    for owned in (sums[0], sum_two):
        owned = owned.astype(full)
        squares = squares + jnp.sum(owned * owned)
    attn_sum, squares, hidden_out, hidden_grad = lax.optimization_barrier(
        (attn_sum, squares, hidden_out, hidden_grad)
    )
    total, attn_parts = bundle(
        8,
        20,
        (TOTAL, PLANE, SHARD, (jnp.full((8, 128), squares, full), attn_sum)),
        (SWAP, (CONTEXT,), attn_sum.reshape(contexts, rows, -1)),
    )
    grad_norm = jnp.sqrt(total[0, 0])
    factor = jnp.minimum(1.0, clip_limit / grad_norm)

    matrices = adam_all(
        (parts_one, parts_two),
        chunks,
        attn_parts,
        head_cols,
        (
            *(qkv_weight, qkv_m, qkv_v),
            *(out_weight, out_m, out_v),
            *(gate_up_weight, gate_up_m, gate_up_v),
            *(down_weight, down_m, down_v),
        ),
        factor,
        (2.0 * (D / 2) ** (-0.5), 2.0 * (H * HD / 16) ** (-0.5), 2.0 * D ** (-0.5), 2.0 * FF ** (-0.5)),
    )
    gains_out = adam_step(gains, gains_m, gains_v, owned_gains, factor, 0.8, 0.0)
    return (hidden_out, hidden_grad, grad_norm, *matrices, *gains_out)


def solution(mesh):
    shards, contexts, tensors = mesh.devices.shape
    fine = Mesh(mesh.devices.reshape(shards // 2, 2, contexts, tensors), AXES)
    tokens = P(SHARD, CONTEXT, None)
    rows = (HIGH, LOW, CONTEXT)
    flat = P(rows, TENSOR)
    paired = P(rows, None, TENSOR)
    gains = P(None, rows)
    states = (flat,) * 6 + (paired,) * 3 + (flat,) * 3 + (gains,) * 3
    return jax.shard_map(
        body,
        mesh=fine,
        in_specs=(tokens, tokens, P(SHARD)) + states,
        out_specs=(tokens, tokens, P()) + states,
        check_vma=False,
    )
```

```python
import functools

import jax
import jax.numpy as jnp
from jax import lax
from jax.experimental import pallas as pl
from jax.experimental.pallas import tpu as pltpu
from jax.sharding import Mesh
from jax.sharding import PartitionSpec as P

D = 2560
H = 32
KV = 8
HD = 80
FF = 7168
STEP = 8


norm_epsilon = 1e-05
rope_theta = 1000000.0
masked_score = -1e30
clip_limit = 1.0
beta_first = 0.9
beta_second = 0.95
adam_epsilon = 1e-08
weight_decay = 0.1

HIGH, LOW, CONTEXT, TENSOR = "high", "low", "context", "tensor"
SHARD = (HIGH, LOW)
AXES = (HIGH, LOW, CONTEXT, TENSOR)
SWAP, STACK, SPREAD, COLLECT, TOTAL = "swap", "stack", "spread", "collect", "total"
MLP_GROUP = (CONTEXT,)
MLP_GATHER = (HIGH, LOW)
MESH = pl.DeviceIdType.MESH
low = jnp.bfloat16
full = jnp.float32


def rope_tables(positions):
    half = HD // 2
    exponent = jnp.arange(half, dtype=full) * (2.0 / HD)
    frequency = rope_theta ** (-exponent)
    angles = positions.astype(full)[:, None] * frequency[None, :]
    angles = jnp.concatenate([angles, angles], axis=-1)
    return (jnp.cos(angles), jnp.sin(angles))


def rotate(values, cosine, sine):
    half = values.shape[-1] // 2
    turned = jnp.concatenate([-values[..., half:], values[..., :half]], axis=-1)
    return values * cosine + turned * sine


def unrotate(values, cosine, sine):
    half = values.shape[-1] // 2
    turned = jnp.concatenate([-values[..., half:], values[..., :half]], axis=-1)
    return values * cosine - turned * sine


def normalize(values):
    factor = lax.rsqrt(jnp.mean(values * values, axis=-1, keepdims=True) + norm_epsilon)
    return (values * factor, factor)


def norm_back(grad_scaled, scaled, factor):
    return factor * (grad_scaled - scaled * jnp.mean(grad_scaled * scaled, axis=-1, keepdims=True))


def adam_step(weight, first, second, grad, factor, rate, decay):
    grad = grad * factor
    first_new = beta_first * first + (1.0 - beta_first) * grad
    second_new = beta_second * second + (1.0 - beta_second) * grad * grad
    first_scale, second_scale = 1.0 / (1.0 - beta_first**STEP), 1.0 / (1.0 - beta_second**STEP)
    corrected = first_new * first_scale / (jnp.sqrt(second_new * second_scale) + adam_epsilon)
    return (first_new, second_new, weight - rate * (corrected + decay * weight))


def over(left_dim, right_dim, left, right):
    return lax.dot_general(left, right, (((left_dim,), (right_dim,)), ((), ())), preferred_element_type=full)


rows_by_cols = functools.partial(over, 1, 0)
rows_by_rows = functools.partial(over, 1, 1)
cols_by_cols = functools.partial(over, 0, 0)


class Link:
    def __init__(self, sizes, send, recv):
        self.sizes, self.send, self.recv, self.used = sizes, send, recv, 0
        self.place = tuple(lax.axis_index(axis) for axis in AXES)

    def device(self, offset):
        return {axis: here ^ by for axis, here, by in zip(AXES, self.place, offset)}

    def index(self, group):
        index = 0
        for axis, here in zip(AXES, self.place):
            if axis in group:
                index = index * self.sizes[axis] + here
        return index

    def greet(self, partners):
        barrier = pltpu.get_barrier_semaphore()
        for offset in partners:
            pl.semaphore_signal(barrier, inc=1, device_id=self.device(offset), device_id_type=MESH)
        pl.semaphore_wait(barrier, len(partners))

    def push(self, src, dst, offset):
        copy = pltpu.make_async_remote_copy(
            src_ref=src,
            dst_ref=dst,
            send_sem=self.send.at[self.used],
            recv_sem=self.recv.at[self.used],
            device_id=self.device(offset),
            device_id_type=MESH,
        )
        self.used += 1
        copy.start()
        return copy

    def keep(self, src, dst):
        copy = pltpu.make_async_copy(src, dst, self.send.at[self.used])
        self.used += 1
        copy.start()
        return copy


MATE = (0, 0, 0, 1)


def axis_sizes():
    return {axis: lax.axis_size(axis) for axis in AXES}


def size_of(sizes, group):
    size = 1
    for axis in group:
        size *= sizes[axis]
    return size


def along(sizes, group, k):
    offset = []
    for axis in reversed(AXES):
        by = 0
        if axis in group:
            k, by = divmod(k, sizes[axis])
        offset.append(by)
    return tuple(reversed(offset))


def partners_of(jobs, sizes):
    found = set()
    for job in jobs:
        for group in job[1:]:
            n = size_of(sizes, group)
            steps = [1 << i for i in range(n.bit_length() - 1)] if job[0] in (SPREAD, COLLECT) else range(1, n)
            found |= {along(sizes, group, k) for k in steps}
        if job[0] in (SPREAD, COLLECT):
            found.add(MATE)
    return sorted(found)


def lanes(width, count):
    tiles, start, runs = width // 128, 0, []
    for i in range(count):
        size = 128 * ((tiles + count - 1 - i) // count)
        runs.append((start, size))
        start += size
    return runs


def turns(n, width):
    bits = [1 << i for i in range(n.bit_length() - 1)]
    return [(pl.ds(*run), bits[i:] + bits[:i]) for i, run in enumerate(lanes(width, len(bits)))]


class Swap:
    copies = staticmethod(lambda sizes, job, n: n)

    def __init__(self, link, job, sources, target, extras):
        (src,), group = sources, job[-1]
        me = link.index(group)
        self.ends = [
            link.push(src.at[me ^ k], target.at[me], along(link.sizes, group, k))
            for k in range(1, size_of(link.sizes, group))
        ]
        self.ends.append(link.keep(src.at[me], target.at[me]))

    def step(self, turn):
        pass

    def finish(self):
        for end in self.ends:
            end.wait()


class Stack:
    copies = staticmethod(lambda sizes, job, n: n + size_of(sizes, job[1]))

    def __init__(self, link, job, sources, target, extras):
        (src,), (_, outer, inner) = sources, job
        slot = target.at[link.index(outer), link.index(inner)]
        self.pieces = [link.push(src, slot, along(link.sizes, inner, k)) for k in range(1, size_of(link.sizes, inner))]
        self.pieces.append(link.keep(src, slot))
        self.link, self.outer, self.target = link, outer, target

    def step(self, turn):
        pass

    def finish(self):
        for piece in self.pieces:
            piece.wait()
        link, row = self.link, self.target.at[self.link.index(self.outer)]
        ends = [
            link.push(row, row, along(link.sizes, self.outer, k)) for k in range(1, size_of(link.sizes, self.outer))
        ]
        for end in ends:
            end.wait()


class Spread:
    copies = staticmethod(lambda sizes, job, n: 2 + 2 * (n - 1) * (n.bit_length() - 1))

    def __init__(self, link, job, sources, target, extras):
        (self.src,), self.group = sources, job[-1]
        self.link, self.target = link, target
        self.routes = turns(size_of(link.sizes, self.group), self.src.shape[1])
        self.held = [[0] for _ in self.routes]
        self.flying = [[] for _ in self.routes]
        self.sent, self.ends = [], []
        self.step(0)
        self.ends.append(link.push(self.src, target.at[1, 0], MATE))
        self.ends.append(link.keep(self.src, target.at[0, 0]))

    def land(self, i):
        run = self.routes[i][0]
        for k, copy in self.flying[i]:
            copy.wait_recv()
            self.held[i].append(k)
            self.ends.append(self.link.push(self.target.at[0, k, :, run], self.target.at[1, k, :, run], MATE))
        self.flying[i] = []

    def step(self, turn):
        for i, (run, bits) in enumerate(self.routes):
            if turn >= len(bits):
                continue
            arrived = self.flying[i]
            for _, copy in arrived:
                copy.wait_recv()
            bit = bits[turn]
            offset = along(self.link.sizes, self.group, bit)
            held = self.held[i] + [k for k, _ in arrived]
            flying = []
            for k in held:
                src = self.src.at[:, run] if k == 0 else self.target.at[0, k, :, run]
                copy = self.link.push(src, self.target.at[0, k ^ bit, :, run], offset)
                flying.append((k ^ bit, copy))
                self.sent.append(copy)
            for k, _ in arrived:
                here, there = self.target.at[0, k, :, run], self.target.at[1, k, :, run]
                self.ends.append(self.link.push(here, there, MATE))
            self.held[i], self.flying[i] = held, flying

    def finish(self):
        for i, _ in enumerate(self.routes):
            self.land(i)
        for copy in self.sent:
            copy.wait_send()
        for end in self.ends:
            end.wait()


class Collect:
    copies = staticmethod(lambda sizes, job, n: n + (n - 1) * (n.bit_length() - 1))

    def __init__(self, link, job, sources, target, extras):
        (self.near, self.far), self.group = sources, job[-1]
        (self.mates, self.got), self.link, self.target = extras, link, target
        n = size_of(link.sizes, self.group)
        self.routes = turns(n, self.near.shape[2])
        self.left = [list(range(n)) for _ in self.routes]
        self.adds = [{k: [] for k in range(n)} for _ in self.routes]
        self.places = [0 for _ in self.routes]
        self.sent = []
        self.crossed = set()
        self.crossing = {k: link.push(self.far.at[k], self.mates.at[k], MATE) for k in reversed(range(n))}

    def value(self, i, k):
        run = self.routes[i][0]
        if k not in self.crossed:
            self.crossing[k].wait_recv()
            self.crossed.add(k)
        total = self.near[k, :, run] + self.mates[k, :, run].astype(full)
        for place, copy in self.adds[i][k]:
            copy.wait_recv()
            total = total + self.got[place, :, run].astype(full)
        return total

    def step(self, turn):
        for i, (run, bits) in enumerate(self.routes):
            if turn >= len(bits):
                continue
            bit = bits[turn]
            offset = along(self.link.sizes, self.group, bit)
            for k in [k for k in self.left[i] if k & bit]:
                self.mates[k, :, run] = self.value(i, k).astype(self.mates.dtype)
                place = self.places[i]
                copy = self.link.push(self.mates.at[k, :, run], self.got.at[place, :, run], offset)
                self.adds[i][k ^ bit].append((place, copy))
                self.sent.append(copy)
                self.places[i] += 1
            self.left[i] = [k for k in self.left[i] if not k & bit]

    def finish(self):
        for i, (run, _) in enumerate(self.routes):
            self.target[:, run] = self.value(i, 0)
        for copy in self.sent + list(self.crossing.values()):
            copy.wait_send()


class Total:
    copies = staticmethod(lambda sizes, job, n: sum(size_of(sizes, group) for group in job[1:]))

    def __init__(self, link, job, sources, target, extras):
        (tile, array), (self.held,) = sources, extras
        self.link, self.groups, self.target, self.slot = link, list(job[1:]), target, 0
        values = array[...].astype(full)
        target[...] = tile[...] + jnp.sum(values * values)
        self.ask()

    def ask(self):
        link, held, slot, group = self.link, self.held, self.slot, self.groups.pop(0)
        n = size_of(link.sizes, group)
        held[slot] = self.target[...]
        self.pushes = [link.push(held.at[slot], held.at[slot + k], along(link.sizes, group, k)) for k in range(1, n)]

    def step(self, turn):
        pass

    def finish(self):
        while True:
            for push in self.pushes:
                push.wait()
            for k, _ in enumerate(self.pushes):
                self.target[...] += self.held[self.slot + 1 + k]
            self.slot += 1 + len(self.pushes)
            if not self.groups:
                return
            self.ask()


KINDS = {SWAP: Swap, STACK: Stack, SPREAD: Spread, COLLECT: Collect, TOTAL: Total}
EXTRAS = {COLLECT: 2, TOTAL: 1}


def bundle_kernel(jobs, sizes, *refs):
    refs = list(refs)
    take = lambda count: [refs.pop(0) for _ in range(count)]
    sources = [take(2 if job[0] in EXTRAS else 1) for job in jobs]
    targets = [take(1)[0] for job in jobs]
    extras = [take(EXTRAS.get(job[0], 0)) for job in jobs]
    link = Link(sizes, *refs)
    link.greet(partners_of(jobs, sizes))
    running = [KINDS[job[0]](link, job, *rest) for job, *rest in zip(jobs, sources, targets, extras)]
    most = max(size_of(sizes, job[-1]).bit_length() - 1 for job in jobs)
    for turn in range(most):
        for job, work in zip(jobs, running):
            if job[0] == COLLECT or turn:
                work.step(turn)
    for work in running:
        if not isinstance(work, Swap):
            work.finish()
    for work in running:
        if isinstance(work, Swap):
            work.finish()


def whole_in_vmem():
    return pl.BlockSpec(memory_space=pltpu.VMEM)


def talking(number, mib):
    return pltpu.CompilerParams(collective_id=number, has_side_effects=True, vmem_limit_bytes=mib * 2**20)


def bundle(number, micros, *jobs):
    sizes = axis_sizes()
    anywhere = pl.BlockSpec(memory_space=pl.ANY)
    flat, in_specs, out_specs, shapes, scratch, copies, held = [], [], [], [], [], 0, 0
    for *job, array in jobs:
        kind, n = job[0], size_of(sizes, job[-1])
        copies += KINDS[kind].copies(sizes, job, n)
        if kind == COLLECT:
            near, far = array
            flat += [near, far]
            in_specs += [whole_in_vmem(), anywhere]
            out_specs.append(whole_in_vmem())
            shapes.append(jax.ShapeDtypeStruct(near.shape[1:], full))
            scratch += [pltpu.VMEM(far.shape, far.dtype), pltpu.VMEM((n - 1,) + far.shape[1:], far.dtype)]
            held += (6 + 2 * far.dtype.itemsize) * near.size
            continue
        if kind == TOTAL:
            flat += array
            in_specs += [whole_in_vmem()] * 2
            out_specs.append(whole_in_vmem())
            shapes.append(jax.ShapeDtypeStruct(array[0].shape, full))
            scratch.append(pltpu.VMEM((KINDS[kind].copies(sizes, job, n),) + array[0].shape, full))
            held += 2 * array[1].size
            continue
        flat.append(array)
        in_specs.append(anywhere)
        out_specs.append(anywhere)
        shape = array.shape
        if kind == STACK:
            shape = (size_of(sizes, job[1]), n) + shape
        elif kind == SPREAD:
            shape = (2, n) + shape
        shapes.append(jax.ShapeDtypeStruct(shape, array.dtype))
    return pl.pallas_call(
        functools.partial(bundle_kernel, tuple(tuple(job[:-1]) for job in jobs), sizes),
        out_shape=shapes,
        in_specs=in_specs,
        out_specs=out_specs,
        scratch_shapes=scratch + [pltpu.SemaphoreType.DMA((copies,)), pltpu.SemaphoreType.DMA((copies,))],
        compiler_params=talking(number, 6 + held // 2**20),
        cost_estimate=pl.CostEstimate(flops=int(micros * 6e8), bytes_accessed=0, transcendentals=0),
    )(*flat)


def halves(left, right, group):
    n = lax.axis_size(group)
    half = left.shape[0] // 2
    return [rows_by_rows(left[start : start + half], right).reshape(n, half // n, -1) for start in (0, half)]


PLANE = (CONTEXT, TENSOR)


def fold_kernel(sizes, part_ref, sum_ref, inner, work, outer, send, recv):
    link = Link(sizes, send, recv)
    plane, shards = size_of(sizes, PLANE), size_of(sizes, SHARD)
    link.greet([along(sizes, group, k) for group in (PLANE, SHARD) for k in range(1, size_of(sizes, group))])
    s, c = link.index(SHARD), link.index((CONTEXT,))
    pushes = [
        link.push(part_ref.at[c ^ (k // sizes[TENSOR])], inner.at[k - 1], along(sizes, PLANE, k))
        for k in range(1, plane)
    ]
    work[...] = part_ref[c]
    for k, push in enumerate(pushes):
        push.wait()
        work[...] += inner[k]
    pushes = [link.push(work.at[s ^ k], outer.at[k - 1], along(sizes, SHARD, k)) for k in range(1, shards)]
    sum_ref[...] = work[s]
    for k, push in enumerate(pushes):
        push.wait()
        sum_ref[...] += outer[k]


def fold(part, number):
    sizes = axis_sizes()
    plane, shards = size_of(sizes, PLANE), size_of(sizes, SHARD)
    return pl.pallas_call(
        functools.partial(fold_kernel, sizes),
        out_shape=jax.ShapeDtypeStruct(part.shape[2:], full),
        in_specs=[whole_in_vmem()],
        out_specs=whole_in_vmem(),
        scratch_shapes=[
            pltpu.VMEM((plane - 1,) + part.shape[1:], full),
            pltpu.VMEM(part.shape[1:], full),
            pltpu.VMEM((shards - 1,) + part.shape[2:], full),
            pltpu.SemaphoreType.DMA((plane + shards,)),
            pltpu.SemaphoreType.DMA((plane + shards,)),
        ],
        compiler_params=talking(number, 8),
    )(part)


def adam_kernel(chunks, head_cols, rates, factor_ref, *refs):
    count = len(chunks)
    parts, attn_part = refs[:count], refs[count]
    states, outs = refs[count + 1 : count + 13], refs[count + 13 : count + 25]
    grads = refs[count + 25 :]
    qkv, out, pair, down = ((states[i : i + 3], outs[i : i + 3], rates[i // 3]) for i in range(0, 12, 3))
    factor = factor_ref[0]

    def update(weight, where, grad):
        old, new, rate = weight
        first, second, fresh = adam_step(*(ref[where] for ref in old), grad, factor, rate, weight_decay)
        new[0][where], new[1][where], new[2][where] = first, second, fresh

    owners = attn_part.shape[0]
    for weight, grad, start in ((qkv, grads[0], 0), (out, grads[1], head_cols)):
        size = grad.shape[1] // owners
        for owner in range(owners):
            grad[:, owner * size : (owner + 1) * size] = attn_part[owner, :, start : start + size].astype(full)
        update(weight, slice(None), grad[...])
    owners = parts[0].shape[0]
    block = down[0][0].shape[1] // owners
    for part, (start, stop) in zip(parts, chunks):
        size = stop - start
        for owner in range(owners):
            cols = slice(owner * block + start, owner * block + stop)
            update(pair, (slice(None), 0, cols), part[owner, :, :size].astype(full))
            update(pair, (slice(None), 1, cols), part[owner, :, size : 2 * size].astype(full))
            update(down, (slice(None), cols), part[owner, :, 2 * size :].astype(full))


def adam_all(parts, chunks, attn_part, head_cols, weights, factor, rates):
    rows = weights[0].shape[0]
    step = 32 if rows % 32 == 0 else rows

    def state_block(array):
        rest = array.shape[1:]
        return pl.BlockSpec((step,) + rest, lambda i: (i,) + (0,) * len(rest))

    blocks = [state_block(array) for array in weights]
    grads = [pl.BlockSpec((part.shape[0], step, part.shape[2]), lambda i: (0, i, 0)) for part in (*parts, attn_part)]
    row_bytes = sum(array.size // rows for array in weights) * 16 + sum(p.shape[0] * p.shape[2] for p in parts) * 8
    return pl.pallas_call(
        functools.partial(adam_kernel, chunks, head_cols, rates),
        grid=(rows // step,),
        out_shape=[jax.ShapeDtypeStruct(array.shape, full) for array in weights],
        in_specs=[pl.BlockSpec(memory_space=pltpu.SMEM)] + grads + blocks,
        out_specs=blocks,
        scratch_shapes=[pltpu.VMEM((step, weights[i].shape[1]), full) for i in (0, 3)],
        compiler_params=pltpu.CompilerParams(vmem_limit_bytes=58 * 2**20),
    )(factor.reshape(1), *parts, attn_part, *weights)


def weight_grads_kernel(count, dim, *refs):
    lefts, rights, out = refs[:count], refs[count:-1], refs[-1]
    start = 0
    for left, right in zip(lefts, rights):
        size = right.shape[1 - dim]
        out[:, start : start + size] = over(0, dim, left[...], right[...]).astype(low)
        start += size


def weight_grads(pairs, dim):
    tokens, width = pairs[0][0].shape
    cols = sum(right.shape[1 - dim] for _, right in pairs)
    step = 256
    return pl.pallas_call(
        functools.partial(weight_grads_kernel, len(pairs), dim),
        grid=(width // step,),
        out_shape=jax.ShapeDtypeStruct((width, cols), low),
        in_specs=[pl.BlockSpec((tokens, step), lambda i: (0, i))] * len(pairs)
        + [pl.BlockSpec(right.shape, lambda i: (0, 0)) for _, right in pairs],
        out_specs=pl.BlockSpec((step, cols), lambda i: (i, 0)),
        compiler_params=pltpu.CompilerParams(vmem_limit_bytes=48 * 2**20),
        cost_estimate=pl.CostEstimate(flops=2 * tokens * width * cols, bytes_accessed=0, transcendentals=0),
    )(*(left for left, _ in pairs), *(right for _, right in pairs))


def attend(query, key, value, allowed):
    scores = rows_by_rows(query, key) * HD ** (-0.5)
    scores = jnp.where(allowed, scores, masked_score)
    row_max = jnp.max(scores, axis=-1, keepdims=True)
    expanded = jnp.exp(scores - row_max)
    row_total = jnp.sum(expanded, axis=-1, keepdims=True)
    probs = (expanded / row_total).astype(low)
    return rows_by_cols(probs, value), row_max + jnp.log(row_total)


def attend_back(query, key, value, grad, log_total, allowed):
    scores = rows_by_rows(query, key) * HD ** (-0.5)
    scores = jnp.where(allowed, scores, masked_score)
    probs = jnp.exp(scores - log_total)
    grad_value = cols_by_cols(probs.astype(low), grad)
    grad_probs = rows_by_rows(grad, value)
    delta = jnp.sum(probs * grad_probs, axis=-1, keepdims=True)
    grad_scores = (probs * (grad_probs - delta)).astype(low)
    grad_query = rows_by_cols(grad_scores, key) * HD ** (-0.5)
    grad_key = cols_by_cols(grad_scores, query) * HD ** (-0.5)
    return grad_query, grad_key, grad_value


def body(
    hidden_in,
    out_grad,
    prefix_len,
    qkv_weight,
    qkv_m,
    qkv_v,
    out_weight,
    out_m,
    out_v,
    gate_up_weight,
    gate_up_m,
    gate_up_v,
    down_weight,
    down_m,
    down_v,
    gains,
    gains_m,
    gains_v,
):
    _, local_len, width = hidden_in.shape
    shards, contexts, tensors = (lax.axis_size(group) for group in (SHARD, CONTEXT, TENSOR))
    context, tensor = lax.axis_index(CONTEXT), lax.axis_index(TENSOR)
    group_size = lax.axis_size(MLP_GROUP)
    rows = qkv_weight.shape[0]
    group = H // KV
    head_cols = (group + 2) * HD
    own = local_len // tensors
    ff_block = down_weight.shape[1] // group_size
    ff_first = ff_block // 2 // 128 * 128 or ff_block // 2
    chunks = ((0, ff_first), (ff_first, ff_block))

    def to_blocks(weight, count):
        return jnp.moveaxis(weight.astype(low).reshape(rows, count, -1), 1, 0)

    (attn_part,) = bundle(
        0,
        16,
        (
            SWAP,
            (CONTEXT,),
            jnp.concatenate([to_blocks(qkv_weight, contexts), to_blocks(out_weight, contexts)], axis=2),
        ),
    )
    gain_values, attn_part = lax.optimization_barrier((gains.astype(low).astype(full), attn_part))
    (gain_blocks,) = bundle(9, 10, (STACK, SHARD, (CONTEXT,), gain_values))
    attn_full = lax.all_gather(attn_part.reshape(contexts * rows, -1), SHARD, axis=0, tiled=True)
    qkv_full, out_full = attn_full[:, :head_cols], attn_full[:, head_cols:]
    gain_rows = gain_blocks.reshape(shards * contexts, 2, rows).transpose(1, 0, 2).reshape(2, width)
    gain_attn, gain_mlp = gain_rows[0], gain_rows[1]
    inputs = lax.dynamic_slice_in_dim(hidden_in[0], tensor * own, own, 0).astype(full)
    grad_low = lax.dynamic_slice_in_dim(out_grad[0], tensor * own, own, 0)
    cotangent = grad_low.astype(full)
    scaled_one, factor_one = normalize(inputs)

    gate_up_blocks = gate_up_weight.astype(low).reshape(rows, 2, group_size, ff_block).transpose(2, 0, 1, 3)
    down_blocks = to_blocks(down_weight, group_size)

    def chunk_blocks(start, stop):
        pair = gate_up_blocks[:, :, :, start:stop]
        return jnp.concatenate([pair[:, :, 0], pair[:, :, 1], down_blocks[:, :, start:stop]], axis=2)

    def gather_mlp(part):
        return lax.all_gather(part.reshape(group_size * rows, -1), MLP_GATHER, axis=0, tiled=True)

    normed_one, part_one, part_two = bundle(
        1,
        75,
        (SPREAD, (CONTEXT,), (scaled_one * gain_attn).astype(low)),
        (SWAP, MLP_GROUP, chunk_blocks(*chunks[0])),
        (SWAP, MLP_GROUP, chunk_blocks(*chunks[1])),
    )
    normed_one = normed_one.reshape(-1, width)
    mlp_full = [gather_mlp(part_one)]

    places = jnp.arange(contexts, dtype=jnp.int32) ^ context
    cores = jnp.arange(tensors, dtype=jnp.int32) ^ tensor
    positions = (
        places[None, :, None] * local_len
        + cores[:, None, None] * own
        + jnp.arange(own, dtype=jnp.int32)[None, None, :]
    ).reshape(-1)
    cosine, sine = rope_tables(positions)
    allowed = (positions[None, :] <= positions[:, None]) | (positions[None, :] < prefix_len[0])

    joined = rows_by_cols(normed_one, qkv_full)
    parts = [joined[:, i * HD : (i + 1) * HD] for i in range(group + 2)]
    queries = [rotate(part, cosine, sine).astype(low) for part in parts[:group]]
    key = rotate(parts[group], cosine, sine).astype(low)
    value = parts[group + 1].astype(low)
    mixed, log_total = zip(*[attend(query, key, value, allowed) for query in queries])
    attended = jnp.concatenate([part.astype(low) for part in mixed], axis=1)
    branch, grad_branch_mlp = bundle(
        2,
        75,
        (COLLECT, (CONTEXT,), halves(attended, out_full, (CONTEXT,))),
        (SPREAD, MLP_GROUP, grad_low),
    )
    part_two, branch = lax.optimization_barrier((part_two, branch))
    grad_branch_mlp = grad_branch_mlp.reshape(-1, width)
    mlp_full.append(gather_mlp(part_two))
    middle = inputs + branch
    scaled_two, factor_two = normalize(middle)
    (normed_two,) = bundle(3, 40, (SPREAD, MLP_GROUP, (scaled_two * gain_mlp).astype(low)))
    normed_two = normed_two.reshape(-1, width)

    sums, back_sums, out_sums = [], [0.0, 0.0], [0.0, 0.0]
    for place, (start, stop) in enumerate(chunks):
        size = stop - start
        weights = mlp_full[place]
        pair_weights, down_weights = weights[:, : 2 * size], weights[:, 2 * size :]
        gate_up = rows_by_cols(normed_two, pair_weights)
        gate, up_part = gate_up[:, :size], gate_up[:, size:]
        sigmoid_gate = jax.nn.sigmoid(gate)
        activated = gate * sigmoid_gate
        hidden = (activated * up_part).astype(low)
        grad_hidden = rows_by_cols(grad_branch_mlp, down_weights)
        grad_gate = grad_hidden * up_part * sigmoid_gate * (1.0 + gate * (1.0 - sigmoid_gate))
        grad_up = grad_hidden * activated
        grad_rows = jnp.concatenate([grad_gate, grad_up], axis=1).astype(low)
        grads = weight_grads([(normed_two, grad_rows), (grad_branch_mlp, hidden)], 0)
        grad_rows, grads = lax.optimization_barrier((grad_rows, grads))
        if sums:
            grads, sums[0] = lax.optimization_barrier((grads, sums[0]))
        back_sums = [a + b for a, b in zip(back_sums, halves(grad_rows, pair_weights, MLP_GROUP))]
        out_sums = [a + b for a, b in zip(out_sums, halves(hidden, down_weights, MLP_GROUP))]
        if not sums:
            grads, back_sums, out_sums, mlp_full[1] = lax.optimization_barrier(
                (grads, back_sums, out_sums, mlp_full[1])
            )
        sums.append(lax.psum_scatter(grads, MLP_GATHER, scatter_dimension=0, tiled=True))

    (grad_normed_two,) = bundle(4, 60, (COLLECT, MLP_GROUP, back_sums))
    grad_gain_mlp = jnp.sum(grad_normed_two * scaled_two, axis=0)
    grad_middle = cotangent + norm_back(grad_normed_two * gain_mlp, scaled_two, factor_two)
    grad_middle, sums[0] = lax.optimization_barrier((grad_middle, sums[0]))
    grad_branch_attn, mlp_branch, parts_one = bundle(
        5,
        80,
        (SPREAD, (CONTEXT,), grad_middle.astype(low)),
        (COLLECT, MLP_GROUP, (out_sums[0], out_sums[1].astype(low))),
        (SWAP, MLP_GROUP, sums[0].reshape(group_size, rows, -1)),
    )
    out_own = (middle + mlp_branch).astype(low)
    grad_branch_attn = grad_branch_attn.reshape(-1, width)
    grad_attended = rows_by_cols(grad_branch_attn, out_full).astype(low)

    grad_queries = []
    grad_key = 0.0
    grad_value = 0.0
    for i in range(group):
        grad_query, key_part, value_part = attend_back(
            queries[i], key, value, grad_attended[:, i * HD : (i + 1) * HD], log_total[i], allowed
        )
        grad_queries.append(unrotate(grad_query, cosine, sine))
        grad_key = grad_key + key_part
        grad_value = grad_value + value_part
    grad_joined = jnp.concatenate(
        grad_queries + [unrotate(grad_key, cosine, sine), grad_value], axis=1
    ).astype(low)
    grad_attn = weight_grads([(normed_one, grad_joined.T), (grad_branch_attn, attended.T)], 1)
    grad_joined, grad_attn = lax.optimization_barrier((grad_joined, grad_attn))
    grad_attn, sum_two = lax.optimization_barrier((grad_attn, sums[1]))
    attn_sum = lax.psum_scatter(grad_attn, SHARD, scatter_dimension=0, tiled=True)
    joined_near, joined_far = halves(grad_joined, qkv_full, (CONTEXT,))
    grad_normed_one, parts_two = bundle(
        6,
        55,
        (COLLECT, (CONTEXT,), (joined_near, joined_far.astype(low))),
        (SWAP, MLP_GROUP, sum_two.reshape(group_size, rows, -1)),
    )
    grad_gain_attn = jnp.sum(grad_normed_one * scaled_one, axis=0)
    grad_inputs = grad_middle + norm_back(grad_normed_one * gain_attn, scaled_one, factor_one)
    grad_own = grad_inputs.astype(low)

    def both_cores(values):
        other = lax.ppermute(values, TENSOR, [(0, 1), (1, 0)])
        return jnp.where(tensor == 0, jnp.concatenate([values, other]), jnp.concatenate([other, values]))[None]

    hidden_out = both_cores(out_own)
    hidden_grad = both_cores(grad_own)
    gain_part = jnp.stack([grad_gain_attn, grad_gain_mlp]).reshape(2, shards, contexts, rows)
    owned_gains = fold(gain_part.transpose(2, 1, 0, 3), 7)

    squares = jnp.sum(owned_gains * owned_gains) / tensors
    for owned in (sums[0], sum_two):
        owned = owned.astype(full)
        squares = squares + jnp.sum(owned * owned)
    attn_sum, squares, hidden_out, hidden_grad = lax.optimization_barrier(
        (attn_sum, squares, hidden_out, hidden_grad)
    )
    total, attn_parts = bundle(
        8,
        20,
        (TOTAL, PLANE, SHARD, (jnp.full((8, 128), squares, full), attn_sum)),
        (SWAP, (CONTEXT,), attn_sum.reshape(contexts, rows, -1)),
    )
    grad_norm = jnp.sqrt(total[0, 0])
    factor = jnp.minimum(1.0, clip_limit / grad_norm)

    matrices = adam_all(
        (parts_one, parts_two),
        chunks,
        attn_parts,
        head_cols,
        (
            *(qkv_weight, qkv_m, qkv_v),
            *(out_weight, out_m, out_v),
            *(gate_up_weight, gate_up_m, gate_up_v),
            *(down_weight, down_m, down_v),
        ),
        factor,
        (2.0 * (D / 2) ** (-0.5), 2.0 * (H * HD / 16) ** (-0.5), 2.0 * D ** (-0.5), 2.0 * FF ** (-0.5)),
    )
    gains_out = adam_step(gains, gains_m, gains_v, owned_gains, factor, 0.8, 0.0)
    return (hidden_out, hidden_grad, grad_norm, *matrices, *gains_out)


def solution(mesh):
    shards, contexts, tensors = mesh.devices.shape
    fine = Mesh(mesh.devices.reshape(shards // 2, 2, contexts, tensors), AXES)
    tokens = P(SHARD, CONTEXT, None)
    rows = (HIGH, LOW, CONTEXT)
    flat = P(rows, TENSOR)
    paired = P(rows, None, TENSOR)
    gains = P(None, rows)
    states = (flat,) * 6 + (paired,) * 3 + (flat,) * 3 + (gains,) * 3
    return jax.shard_map(
        body,
        mesh=fine,
        in_specs=(tokens, tokens, P(SHARD)) + states,
        out_specs=(tokens, tokens, P()) + states,
        check_vma=False,
    )
```

```python
import functools

import jax
import jax.numpy as jnp
from jax import lax
from jax.experimental import pallas as pl
from jax.experimental.pallas import tpu as pltpu
from jax.sharding import Mesh
from jax.sharding import PartitionSpec as P

D = 2560
H = 32
KV = 8
HD = 80
FF = 7168
STEP = 8


norm_epsilon = 1e-05
rope_theta = 1000000.0
masked_score = -1e30
clip_limit = 1.0
beta_first = 0.9
beta_second = 0.95
adam_epsilon = 1e-08
weight_decay = 0.1

HIGH, LOW, CONTEXT, TENSOR = "high", "low", "context", "tensor"
SHARD = (HIGH, LOW)
AXES = (HIGH, LOW, CONTEXT, TENSOR)
SWAP, STACK, SPREAD, COLLECT, TOTAL = "swap", "stack", "spread", "collect", "total"
MLP_GROUP = (CONTEXT,)
MLP_GATHER = (HIGH, LOW)
MESH = pl.DeviceIdType.MESH
low = jnp.bfloat16
full = jnp.float32


def rope_tables(positions):
    half = HD // 2
    exponent = jnp.arange(half, dtype=full) * (2.0 / HD)
    frequency = rope_theta ** (-exponent)
    angles = positions.astype(full)[:, None] * frequency[None, :]
    angles = jnp.concatenate([angles, angles], axis=-1)
    return (jnp.cos(angles), jnp.sin(angles))


def rotate(values, cosine, sine):
    half = values.shape[-1] // 2
    turned = jnp.concatenate([-values[..., half:], values[..., :half]], axis=-1)
    return values * cosine + turned * sine


def unrotate(values, cosine, sine):
    half = values.shape[-1] // 2
    turned = jnp.concatenate([-values[..., half:], values[..., :half]], axis=-1)
    return values * cosine - turned * sine


def normalize(values):
    factor = lax.rsqrt(jnp.mean(values * values, axis=-1, keepdims=True) + norm_epsilon)
    return (values * factor, factor)


def norm_back(grad_scaled, scaled, factor):
    return factor * (grad_scaled - scaled * jnp.mean(grad_scaled * scaled, axis=-1, keepdims=True))


def adam_step(weight, first, second, grad, factor, rate, decay):
    grad = grad * factor
    first_new = beta_first * first + (1.0 - beta_first) * grad
    second_new = beta_second * second + (1.0 - beta_second) * grad * grad
    first_scale, second_scale = 1.0 / (1.0 - beta_first**STEP), 1.0 / (1.0 - beta_second**STEP)
    corrected = first_new * first_scale / (jnp.sqrt(second_new * second_scale) + adam_epsilon)
    return (first_new, second_new, weight - rate * (corrected + decay * weight))


def over(left_dim, right_dim, left, right):
    return lax.dot_general(left, right, (((left_dim,), (right_dim,)), ((), ())), preferred_element_type=full)


rows_by_cols = functools.partial(over, 1, 0)
rows_by_rows = functools.partial(over, 1, 1)
cols_by_cols = functools.partial(over, 0, 0)


class Link:
    def __init__(self, sizes, send, recv):
        self.sizes, self.send, self.recv, self.used = sizes, send, recv, 0
        self.place = tuple(lax.axis_index(axis) for axis in AXES)

    def device(self, offset):
        return {axis: here ^ by for axis, here, by in zip(AXES, self.place, offset)}

    def index(self, group):
        index = 0
        for axis, here in zip(AXES, self.place):
            if axis in group:
                index = index * self.sizes[axis] + here
        return index

    def greet(self, partners):
        barrier = pltpu.get_barrier_semaphore()
        for offset in partners:
            pl.semaphore_signal(barrier, inc=1, device_id=self.device(offset), device_id_type=MESH)
        pl.semaphore_wait(barrier, len(partners))

    def push(self, src, dst, offset):
        copy = pltpu.make_async_remote_copy(
            src_ref=src,
            dst_ref=dst,
            send_sem=self.send.at[self.used],
            recv_sem=self.recv.at[self.used],
            device_id=self.device(offset),
            device_id_type=MESH,
        )
        self.used += 1
        copy.start()
        return copy

    def keep(self, src, dst):
        copy = pltpu.make_async_copy(src, dst, self.send.at[self.used])
        self.used += 1
        copy.start()
        return copy


MATE = (0, 0, 0, 1)


def axis_sizes():
    return {axis: lax.axis_size(axis) for axis in AXES}


def size_of(sizes, group):
    size = 1
    for axis in group:
        size *= sizes[axis]
    return size


def along(sizes, group, k):
    offset = []
    for axis in reversed(AXES):
        by = 0
        if axis in group:
            k, by = divmod(k, sizes[axis])
        offset.append(by)
    return tuple(reversed(offset))


def partners_of(jobs, sizes):
    found = set()
    for job in jobs:
        for group in job[1:]:
            n = size_of(sizes, group)
            steps = [1 << i for i in range(n.bit_length() - 1)] if job[0] in (SPREAD, COLLECT) else range(1, n)
            found |= {along(sizes, group, k) for k in steps}
        if job[0] in (SPREAD, COLLECT):
            found.add(MATE)
    return sorted(found)


def lanes(width, count):
    tiles, start, runs = width // 128, 0, []
    for i in range(count):
        size = 128 * ((tiles + count - 1 - i) // count)
        runs.append((start, size))
        start += size
    return runs


def turns(n, width):
    bits = [1 << i for i in range(n.bit_length() - 1)]
    return [(pl.ds(*run), bits[i:] + bits[:i]) for i, run in enumerate(lanes(width, len(bits)))]


class Swap:
    copies = staticmethod(lambda sizes, job, n: n)

    def __init__(self, link, job, sources, target, extras):
        (src,), group = sources, job[-1]
        me = link.index(group)
        self.ends = [
            link.push(src.at[me ^ k], target.at[me], along(link.sizes, group, k))
            for k in range(1, size_of(link.sizes, group))
        ]
        self.ends.append(link.keep(src.at[me], target.at[me]))

    def step(self, turn):
        pass

    def finish(self):
        for end in self.ends:
            end.wait()


class Stack:
    copies = staticmethod(lambda sizes, job, n: n + size_of(sizes, job[1]))

    def __init__(self, link, job, sources, target, extras):
        (src,), (_, outer, inner) = sources, job
        slot = target.at[link.index(outer), link.index(inner)]
        self.pieces = [link.push(src, slot, along(link.sizes, inner, k)) for k in range(1, size_of(link.sizes, inner))]
        self.pieces.append(link.keep(src, slot))
        self.link, self.outer, self.target = link, outer, target

    def step(self, turn):
        pass

    def finish(self):
        for piece in self.pieces:
            piece.wait()
        link, row = self.link, self.target.at[self.link.index(self.outer)]
        ends = [
            link.push(row, row, along(link.sizes, self.outer, k)) for k in range(1, size_of(link.sizes, self.outer))
        ]
        for end in ends:
            end.wait()


class Spread:
    copies = staticmethod(lambda sizes, job, n: 2 + 2 * (n - 1) * (n.bit_length() - 1))

    def __init__(self, link, job, sources, target, extras):
        (self.src,), self.group = sources, job[-1]
        self.link, self.target = link, target
        self.routes = turns(size_of(link.sizes, self.group), self.src.shape[1])
        self.held = [[0] for _ in self.routes]
        self.flying = [[] for _ in self.routes]
        self.sent, self.ends = [], []
        self.step(0)
        self.ends.append(link.push(self.src, target.at[1, 0], MATE))
        self.ends.append(link.keep(self.src, target.at[0, 0]))

    def land(self, i):
        run = self.routes[i][0]
        for k, copy in self.flying[i]:
            copy.wait_recv()
            self.held[i].append(k)
            self.ends.append(self.link.push(self.target.at[0, k, :, run], self.target.at[1, k, :, run], MATE))
        self.flying[i] = []

    def step(self, turn):
        for i, (run, bits) in enumerate(self.routes):
            if turn >= len(bits):
                continue
            arrived = self.flying[i]
            for _, copy in arrived:
                copy.wait_recv()
            bit = bits[turn]
            offset = along(self.link.sizes, self.group, bit)
            held = self.held[i] + [k for k, _ in arrived]
            flying = []
            for k in held:
                src = self.src.at[:, run] if k == 0 else self.target.at[0, k, :, run]
                copy = self.link.push(src, self.target.at[0, k ^ bit, :, run], offset)
                flying.append((k ^ bit, copy))
                self.sent.append(copy)
            for k, _ in arrived:
                here, there = self.target.at[0, k, :, run], self.target.at[1, k, :, run]
                self.ends.append(self.link.push(here, there, MATE))
            self.held[i], self.flying[i] = held, flying

    def finish(self):
        for i, _ in enumerate(self.routes):
            self.land(i)
        for copy in self.sent:
            copy.wait_send()
        for end in self.ends:
            end.wait()


class Collect:
    copies = staticmethod(lambda sizes, job, n: n + (n - 1) * (n.bit_length() - 1))

    def __init__(self, link, job, sources, target, extras):
        (self.near, self.far), self.group = sources, job[-1]
        (self.mates, self.got), self.link, self.target = extras, link, target
        n = size_of(link.sizes, self.group)
        self.routes = turns(n, self.near.shape[2])
        self.left = [list(range(n)) for _ in self.routes]
        self.adds = [{k: [] for k in range(n)} for _ in self.routes]
        self.places = [0 for _ in self.routes]
        self.sent = []
        self.crossed = set()
        self.crossing = {k: link.push(self.far.at[k], self.mates.at[k], MATE) for k in reversed(range(n))}

    def value(self, i, k):
        run = self.routes[i][0]
        if k not in self.crossed:
            self.crossing[k].wait_recv()
            self.crossed.add(k)
        total = self.near[k, :, run] + self.mates[k, :, run].astype(full)
        for place, copy in self.adds[i][k]:
            copy.wait_recv()
            total = total + self.got[place, :, run].astype(full)
        return total

    def step(self, turn):
        for i, (run, bits) in enumerate(self.routes):
            if turn >= len(bits):
                continue
            bit = bits[turn]
            offset = along(self.link.sizes, self.group, bit)
            for k in [k for k in self.left[i] if k & bit]:
                self.mates[k, :, run] = self.value(i, k).astype(low)
                place = self.places[i]
                copy = self.link.push(self.mates.at[k, :, run], self.got.at[place, :, run], offset)
                self.adds[i][k ^ bit].append((place, copy))
                self.sent.append(copy)
                self.places[i] += 1
            self.left[i] = [k for k in self.left[i] if not k & bit]

    def finish(self):
        for i, (run, _) in enumerate(self.routes):
            self.target[:, run] = self.value(i, 0)
        for copy in self.sent + list(self.crossing.values()):
            copy.wait_send()


class Total:
    copies = staticmethod(lambda sizes, job, n: sum(size_of(sizes, group) for group in job[1:]))

    def __init__(self, link, job, sources, target, extras):
        (tile, array), (self.held,) = sources, extras
        self.link, self.groups, self.target, self.slot = link, list(job[1:]), target, 0
        values = array[...].astype(full)
        target[...] = tile[...] + jnp.sum(values * values)
        self.ask()

    def ask(self):
        link, held, slot, group = self.link, self.held, self.slot, self.groups.pop(0)
        n = size_of(link.sizes, group)
        held[slot] = self.target[...]
        self.pushes = [link.push(held.at[slot], held.at[slot + k], along(link.sizes, group, k)) for k in range(1, n)]

    def step(self, turn):
        pass

    def finish(self):
        while True:
            for push in self.pushes:
                push.wait()
            for k, _ in enumerate(self.pushes):
                self.target[...] += self.held[self.slot + 1 + k]
            self.slot += 1 + len(self.pushes)
            if not self.groups:
                return
            self.ask()


KINDS = {SWAP: Swap, STACK: Stack, SPREAD: Spread, COLLECT: Collect, TOTAL: Total}
EXTRAS = {COLLECT: 2, TOTAL: 1}


def bundle_kernel(jobs, sizes, *refs):
    refs = list(refs)
    take = lambda count: [refs.pop(0) for _ in range(count)]
    sources = [take(2 if job[0] in EXTRAS else 1) for job in jobs]
    targets = [take(1)[0] for job in jobs]
    extras = [take(EXTRAS.get(job[0], 0)) for job in jobs]
    link = Link(sizes, *refs)
    link.greet(partners_of(jobs, sizes))
    running = [KINDS[job[0]](link, job, *rest) for job, *rest in zip(jobs, sources, targets, extras)]
    most = max(size_of(sizes, job[-1]).bit_length() - 1 for job in jobs)
    for turn in range(most):
        for job, work in zip(jobs, running):
            if job[0] == COLLECT or turn:
                work.step(turn)
    for work in running:
        if not isinstance(work, Swap):
            work.finish()
    for work in running:
        if isinstance(work, Swap):
            work.finish()


def whole_in_vmem():
    return pl.BlockSpec(memory_space=pltpu.VMEM)


def talking(number, mib):
    return pltpu.CompilerParams(collective_id=number, has_side_effects=True, vmem_limit_bytes=mib * 2**20)


def bundle(number, micros, *jobs):
    sizes = axis_sizes()
    anywhere = pl.BlockSpec(memory_space=pl.ANY)
    flat, in_specs, out_specs, shapes, scratch, copies, held = [], [], [], [], [], 0, 0
    for *job, array in jobs:
        kind, n = job[0], size_of(sizes, job[-1])
        copies += KINDS[kind].copies(sizes, job, n)
        if kind == COLLECT:
            near, far = array
            flat += [near, far]
            in_specs += [whole_in_vmem(), anywhere]
            out_specs.append(whole_in_vmem())
            shapes.append(jax.ShapeDtypeStruct(near.shape[1:], full))
            scratch += [pltpu.VMEM(far.shape, low), pltpu.VMEM((n - 1,) + far.shape[1:], low)]
            held += 10 * near.size
            continue
        if kind == TOTAL:
            flat += array
            in_specs += [whole_in_vmem()] * 2
            out_specs.append(whole_in_vmem())
            shapes.append(jax.ShapeDtypeStruct(array[0].shape, full))
            scratch.append(pltpu.VMEM((KINDS[kind].copies(sizes, job, n),) + array[0].shape, full))
            held += 2 * array[1].size
            continue
        flat.append(array)
        in_specs.append(anywhere)
        out_specs.append(anywhere)
        shape = array.shape
        if kind == STACK:
            shape = (size_of(sizes, job[1]), n) + shape
        elif kind == SPREAD:
            shape = (2, n) + shape
        shapes.append(jax.ShapeDtypeStruct(shape, array.dtype))
    return pl.pallas_call(
        functools.partial(bundle_kernel, tuple(tuple(job[:-1]) for job in jobs), sizes),
        out_shape=shapes,
        in_specs=in_specs,
        out_specs=out_specs,
        scratch_shapes=scratch + [pltpu.SemaphoreType.DMA((copies,)), pltpu.SemaphoreType.DMA((copies,))],
        compiler_params=talking(number, 6 + held // 2**20),
        cost_estimate=pl.CostEstimate(flops=int(micros * 8e8), bytes_accessed=0, transcendentals=0),
    )(*flat)


def halves(products, group):
    n = lax.axis_size(group)
    half = products[0][0].shape[0] // 2

    def part(start):
        total = 0.0
        for left, right in products:
            total = total + rows_by_rows(left[start : start + half], right)
        return total.reshape(n, half // n, -1)

    return part(0), part(half).astype(low)


PLANE = (CONTEXT, TENSOR)


def fold_kernel(sizes, part_ref, sum_ref, inner, work, outer, send, recv):
    link = Link(sizes, send, recv)
    plane, shards = size_of(sizes, PLANE), size_of(sizes, SHARD)
    link.greet([along(sizes, group, k) for group in (PLANE, SHARD) for k in range(1, size_of(sizes, group))])
    s, c = link.index(SHARD), link.index((CONTEXT,))
    pushes = [
        link.push(part_ref.at[c ^ (k // sizes[TENSOR])], inner.at[k - 1], along(sizes, PLANE, k))
        for k in range(1, plane)
    ]
    work[...] = part_ref[c]
    for k, push in enumerate(pushes):
        push.wait()
        work[...] += inner[k]
    pushes = [link.push(work.at[s ^ k], outer.at[k - 1], along(sizes, SHARD, k)) for k in range(1, shards)]
    sum_ref[...] = work[s]
    for k, push in enumerate(pushes):
        push.wait()
        sum_ref[...] += outer[k]


def fold(part, number):
    sizes = axis_sizes()
    plane, shards = size_of(sizes, PLANE), size_of(sizes, SHARD)
    return pl.pallas_call(
        functools.partial(fold_kernel, sizes),
        out_shape=jax.ShapeDtypeStruct(part.shape[2:], full),
        in_specs=[whole_in_vmem()],
        out_specs=whole_in_vmem(),
        scratch_shapes=[
            pltpu.VMEM((plane - 1,) + part.shape[1:], full),
            pltpu.VMEM(part.shape[1:], full),
            pltpu.VMEM((shards - 1,) + part.shape[2:], full),
            pltpu.SemaphoreType.DMA((plane + shards,)),
            pltpu.SemaphoreType.DMA((plane + shards,)),
        ],
        compiler_params=talking(number, 8),
    )(part)


def adam_kernel(chunks, head_cols, rates, factor_ref, *refs):
    count = len(chunks)
    parts, attn_part = refs[:count], refs[count]
    states, outs = refs[count + 1 : count + 13], refs[count + 13 : count + 25]
    grads = refs[count + 25 :]
    qkv, out, pair, down = ((states[i : i + 3], outs[i : i + 3], rates[i // 3]) for i in range(0, 12, 3))
    factor = factor_ref[0]

    def update(weight, where, grad):
        old, new, rate = weight
        first, second, fresh = adam_step(*(ref[where] for ref in old), grad, factor, rate, weight_decay)
        new[0][where], new[1][where], new[2][where] = first, second, fresh

    owners = attn_part.shape[0]
    for weight, grad, start in ((qkv, grads[0], 0), (out, grads[1], head_cols)):
        size = grad.shape[1] // owners
        for owner in range(owners):
            grad[:, owner * size : (owner + 1) * size] = attn_part[owner, :, start : start + size].astype(full)
        update(weight, slice(None), grad[...])
    owners = parts[0].shape[0]
    block = down[0][0].shape[1] // owners
    for part, (start, stop) in zip(parts, chunks):
        size = stop - start
        for owner in range(owners):
            cols = slice(owner * block + start, owner * block + stop)
            update(pair, (slice(None), 0, cols), part[owner, :, :size].astype(full))
            update(pair, (slice(None), 1, cols), part[owner, :, size : 2 * size].astype(full))
            update(down, (slice(None), cols), part[owner, :, 2 * size :].astype(full))


def adam_all(parts, chunks, attn_part, head_cols, weights, factor, rates):
    rows = weights[0].shape[0]
    step = 32 if rows % 32 == 0 else rows

    def state_block(array):
        rest = array.shape[1:]
        return pl.BlockSpec((step,) + rest, lambda i: (i,) + (0,) * len(rest))

    blocks = [state_block(array) for array in weights]
    grads = [pl.BlockSpec((part.shape[0], step, part.shape[2]), lambda i: (0, i, 0)) for part in (*parts, attn_part)]
    row_bytes = sum(array.size // rows for array in weights) * 16 + sum(p.shape[0] * p.shape[2] for p in parts) * 8
    return pl.pallas_call(
        functools.partial(adam_kernel, chunks, head_cols, rates),
        grid=(rows // step,),
        out_shape=[jax.ShapeDtypeStruct(array.shape, full) for array in weights],
        in_specs=[pl.BlockSpec(memory_space=pltpu.SMEM)] + grads + blocks,
        out_specs=blocks,
        scratch_shapes=[pltpu.VMEM((step, weights[i].shape[1]), full) for i in (0, 3)],
        compiler_params=pltpu.CompilerParams(vmem_limit_bytes=58 * 2**20),
    )(factor.reshape(1), *parts, attn_part, *weights)


def weight_grads_kernel(count, dim, *refs):
    lefts, rights, out = refs[:count], refs[count:-1], refs[-1]
    start = 0
    for left, right in zip(lefts, rights):
        size = right.shape[1 - dim]
        out[:, start : start + size] = over(0, dim, left[...], right[...]).astype(low)
        start += size


def weight_grads(pairs, dim):
    tokens, width = pairs[0][0].shape
    cols = sum(right.shape[1 - dim] for _, right in pairs)
    step = 256
    return pl.pallas_call(
        functools.partial(weight_grads_kernel, len(pairs), dim),
        grid=(width // step,),
        out_shape=jax.ShapeDtypeStruct((width, cols), low),
        in_specs=[pl.BlockSpec((tokens, step), lambda i: (0, i))] * len(pairs)
        + [pl.BlockSpec(right.shape, lambda i: (0, 0)) for _, right in pairs],
        out_specs=pl.BlockSpec((step, cols), lambda i: (i, 0)),
        compiler_params=pltpu.CompilerParams(vmem_limit_bytes=48 * 2**20),
        cost_estimate=pl.CostEstimate(flops=2 * tokens * width * cols, bytes_accessed=0, transcendentals=0),
    )(*(left for left, _ in pairs), *(right for _, right in pairs))


def attend(query, key, value, allowed):
    scores = rows_by_rows(query, key) * HD ** (-0.5)
    scores = jnp.where(allowed, scores, masked_score)
    row_max = jnp.max(scores, axis=-1, keepdims=True)
    expanded = jnp.exp(scores - row_max)
    row_total = jnp.sum(expanded, axis=-1, keepdims=True)
    probs = (expanded / row_total).astype(low)
    return rows_by_cols(probs, value), row_max + jnp.log(row_total)


def attend_back(query, key, value, grad, log_total, allowed):
    scores = rows_by_rows(query, key) * HD ** (-0.5)
    scores = jnp.where(allowed, scores, masked_score)
    probs = jnp.exp(scores - log_total)
    grad_value = cols_by_cols(probs.astype(low), grad)
    grad_probs = rows_by_rows(grad, value)
    delta = jnp.sum(probs * grad_probs, axis=-1, keepdims=True)
    grad_scores = (probs * (grad_probs - delta)).astype(low)
    grad_query = rows_by_cols(grad_scores, key) * HD ** (-0.5)
    grad_key = cols_by_cols(grad_scores, query) * HD ** (-0.5)
    return grad_query, grad_key, grad_value


def body(
    hidden_in,
    out_grad,
    prefix_len,
    qkv_weight,
    qkv_m,
    qkv_v,
    out_weight,
    out_m,
    out_v,
    gate_up_weight,
    gate_up_m,
    gate_up_v,
    down_weight,
    down_m,
    down_v,
    gains,
    gains_m,
    gains_v,
):
    _, local_len, width = hidden_in.shape
    shards, contexts, tensors = (lax.axis_size(group) for group in (SHARD, CONTEXT, TENSOR))
    context, tensor = lax.axis_index(CONTEXT), lax.axis_index(TENSOR)
    group_size = lax.axis_size(MLP_GROUP)
    rows = qkv_weight.shape[0]
    group = H // KV
    head_cols = (group + 2) * HD
    own = local_len // tensors
    ff_block = down_weight.shape[1] // group_size
    ff_first = ff_block // 2 // 128 * 128 or ff_block // 2
    chunks = ((0, ff_first), (ff_first, ff_block))

    def to_blocks(weight, count):
        return jnp.moveaxis(weight.astype(low).reshape(rows, count, -1), 1, 0)

    (attn_part,) = bundle(
        0,
        16,
        (
            SWAP,
            (CONTEXT,),
            jnp.concatenate([to_blocks(qkv_weight, contexts), to_blocks(out_weight, contexts)], axis=2),
        ),
    )
    gain_values, attn_part = lax.optimization_barrier((lax.reduce_precision(gains, 8, 7), attn_part))
    (gain_blocks,) = bundle(9, 10, (STACK, SHARD, (CONTEXT,), gain_values))
    attn_full = lax.all_gather(attn_part.reshape(contexts * rows, -1), SHARD, axis=0, tiled=True)
    qkv_full, out_full = attn_full[:, :head_cols], attn_full[:, head_cols:]
    gain_rows = gain_blocks.reshape(shards * contexts, 2, rows).transpose(1, 0, 2).reshape(2, width)
    gain_attn, gain_mlp = gain_rows[0], gain_rows[1]
    inputs = lax.dynamic_slice_in_dim(hidden_in[0], tensor * own, own, 0).astype(full)
    grad_low = lax.dynamic_slice_in_dim(out_grad[0], tensor * own, own, 0)
    cotangent = grad_low.astype(full)
    scaled_one, factor_one = normalize(inputs)

    gate_up_blocks = gate_up_weight.astype(low).reshape(rows, 2, group_size, ff_block).transpose(2, 0, 1, 3)
    down_blocks = to_blocks(down_weight, group_size)

    def chunk_blocks(start, stop):
        pair = gate_up_blocks[:, :, :, start:stop]
        return jnp.concatenate([pair[:, :, 0], pair[:, :, 1], down_blocks[:, :, start:stop]], axis=2)

    def gather_mlp(part):
        return lax.all_gather(part.reshape(group_size * rows, -1), MLP_GATHER, axis=0, tiled=True)

    normed_one, part_one = bundle(
        1,
        60,
        (SPREAD, (CONTEXT,), (scaled_one * gain_attn).astype(low)),
        (SWAP, MLP_GROUP, chunk_blocks(*chunks[0])),
    )
    normed_one = normed_one.reshape(-1, width)
    mlp_full = [gather_mlp(part_one)]

    places = jnp.arange(contexts, dtype=jnp.int32) ^ context
    cores = jnp.arange(tensors, dtype=jnp.int32) ^ tensor
    positions = (
        places[None, :, None] * local_len
        + cores[:, None, None] * own
        + jnp.arange(own, dtype=jnp.int32)[None, None, :]
    ).reshape(-1)
    cosine, sine = rope_tables(positions)
    allowed = (positions[None, :] <= positions[:, None]) | (positions[None, :] < prefix_len[0])

    joined = rows_by_cols(normed_one, qkv_full)
    parts = [joined[:, i * HD : (i + 1) * HD] for i in range(group + 2)]
    queries = [rotate(part, cosine, sine).astype(low) for part in parts[:group]]
    key = rotate(parts[group], cosine, sine).astype(low)
    value = parts[group + 1].astype(low)
    mixed, log_total = zip(*[attend(query, key, value, allowed) for query in queries])
    attended = jnp.concatenate([part.astype(low) for part in mixed], axis=1)
    branch, part_two, grad_branch_mlp = bundle(
        2,
        80,
        (COLLECT, (CONTEXT,), halves([(attended, out_full)], (CONTEXT,))),
        (SWAP, MLP_GROUP, chunk_blocks(*chunks[1])),
        (SPREAD, MLP_GROUP, grad_low),
    )
    grad_branch_mlp = grad_branch_mlp.reshape(-1, width)
    mlp_full.append(gather_mlp(part_two))
    middle = inputs + branch
    scaled_two, factor_two = normalize(middle)
    (normed_two,) = bundle(3, 40, (SPREAD, MLP_GROUP, (scaled_two * gain_mlp).astype(low)))
    normed_two = normed_two.reshape(-1, width)

    sums, back_products, out_products = [], [], []
    for place, (start, stop) in enumerate(chunks):
        size = stop - start
        weights = mlp_full[place]
        pair_weights, down_weights = weights[:, : 2 * size], weights[:, 2 * size :]
        gate_up = rows_by_cols(normed_two, pair_weights)
        gate, up_part = gate_up[:, :size], gate_up[:, size:]
        sigmoid_gate = jax.nn.sigmoid(gate)
        activated = gate * sigmoid_gate
        hidden = (activated * up_part).astype(low)
        grad_hidden = rows_by_cols(grad_branch_mlp, down_weights)
        grad_gate = grad_hidden * up_part * sigmoid_gate * (1.0 + gate * (1.0 - sigmoid_gate))
        grad_up = grad_hidden * activated
        grad_rows = jnp.concatenate([grad_gate, grad_up], axis=1).astype(low)
        grads = weight_grads([(normed_two, grad_rows), (grad_branch_mlp, hidden)], 0)
        grad_rows, grads = lax.optimization_barrier((grad_rows, grads))
        if sums:
            grads, sums[0] = lax.optimization_barrier((grads, sums[0]))
        else:
            grads, mlp_full[1] = lax.optimization_barrier((grads, mlp_full[1]))
        sums.append(lax.psum_scatter(grads, MLP_GATHER, scatter_dimension=0, tiled=True))
        back_products.append((grad_rows, pair_weights))
        out_products.append((hidden, down_weights))

    (grad_normed_two,) = bundle(4, 40, (COLLECT, MLP_GROUP, halves(back_products, MLP_GROUP)))
    grad_gain_mlp = jnp.sum(grad_normed_two * scaled_two, axis=0)
    grad_middle = cotangent + norm_back(grad_normed_two * gain_mlp, scaled_two, factor_two)
    grad_middle, sums[0] = lax.optimization_barrier((grad_middle, sums[0]))
    grad_branch_attn, mlp_branch, parts_one = bundle(
        5,
        80,
        (SPREAD, (CONTEXT,), grad_middle.astype(low)),
        (COLLECT, MLP_GROUP, halves(out_products, MLP_GROUP)),
        (SWAP, MLP_GROUP, sums[0].reshape(group_size, rows, -1)),
    )
    out_own = (middle + mlp_branch).astype(low)
    grad_branch_attn = grad_branch_attn.reshape(-1, width)
    grad_attended = rows_by_cols(grad_branch_attn, out_full).astype(low)

    grad_queries = []
    grad_key = 0.0
    grad_value = 0.0
    for i in range(group):
        grad_query, key_part, value_part = attend_back(
            queries[i], key, value, grad_attended[:, i * HD : (i + 1) * HD], log_total[i], allowed
        )
        grad_queries.append(unrotate(grad_query, cosine, sine))
        grad_key = grad_key + key_part
        grad_value = grad_value + value_part
    grad_joined = jnp.concatenate(
        grad_queries + [unrotate(grad_key, cosine, sine), grad_value], axis=1
    ).astype(low)
    grad_attn = weight_grads([(normed_one, grad_joined.T), (grad_branch_attn, attended.T)], 1)
    grad_joined, grad_attn = lax.optimization_barrier((grad_joined, grad_attn))
    grad_attn, sum_two = lax.optimization_barrier((grad_attn, sums[1]))
    attn_sum = lax.psum_scatter(grad_attn, SHARD, scatter_dimension=0, tiled=True)
    grad_normed_one, parts_two = bundle(
        6,
        55,
        (COLLECT, (CONTEXT,), halves([(grad_joined, qkv_full)], (CONTEXT,))),
        (SWAP, MLP_GROUP, sum_two.reshape(group_size, rows, -1)),
    )
    grad_gain_attn = jnp.sum(grad_normed_one * scaled_one, axis=0)
    grad_inputs = grad_middle + norm_back(grad_normed_one * gain_attn, scaled_one, factor_one)
    grad_own = grad_inputs.astype(low)

    def both_cores(values):
        other = lax.ppermute(values, TENSOR, [(0, 1), (1, 0)])
        return jnp.where(tensor == 0, jnp.concatenate([values, other]), jnp.concatenate([other, values]))[None]

    hidden_out = both_cores(out_own)
    hidden_grad = both_cores(grad_own)
    gain_part = jnp.stack([grad_gain_attn, grad_gain_mlp]).reshape(2, shards, contexts, rows)
    owned_gains = fold(gain_part.transpose(2, 1, 0, 3), 7)

    squares = jnp.sum(owned_gains * owned_gains) / tensors
    for owned in (sums[0], sum_two):
        owned = owned.astype(full)
        squares = squares + jnp.sum(owned * owned)
    attn_sum, squares, hidden_out, hidden_grad = lax.optimization_barrier(
        (attn_sum, squares, hidden_out, hidden_grad)
    )
    total, attn_parts = bundle(
        8,
        20,
        (TOTAL, PLANE, SHARD, (jnp.full((8, 128), squares, full), attn_sum)),
        (SWAP, (CONTEXT,), attn_sum.reshape(contexts, rows, -1)),
    )
    grad_norm = jnp.sqrt(total[0, 0])
    factor = jnp.minimum(1.0, clip_limit / grad_norm)

    matrices = adam_all(
        (parts_one, parts_two),
        chunks,
        attn_parts,
        head_cols,
        (
            *(qkv_weight, qkv_m, qkv_v),
            *(out_weight, out_m, out_v),
            *(gate_up_weight, gate_up_m, gate_up_v),
            *(down_weight, down_m, down_v),
        ),
        factor,
        (2.0 * (D / 2) ** (-0.5), 2.0 * (H * HD / 16) ** (-0.5), 2.0 * D ** (-0.5), 2.0 * FF ** (-0.5)),
    )
    gains_out = adam_step(gains, gains_m, gains_v, owned_gains, factor, 0.8, 0.0)
    return (hidden_out, hidden_grad, grad_norm, *matrices, *gains_out)


def solution(mesh):
    shards, contexts, tensors = mesh.devices.shape
    fine = Mesh(mesh.devices.reshape(shards // 2, 2, contexts, tensors), AXES)
    tokens = P(SHARD, CONTEXT, None)
    rows = (HIGH, LOW, CONTEXT)
    flat = P(rows, TENSOR)
    paired = P(rows, None, TENSOR)
    gains = P(None, rows)
    states = (flat,) * 6 + (paired,) * 3 + (flat,) * 3 + (gains,) * 3
    return jax.shard_map(
        body,
        mesh=fine,
        in_specs=(tokens, tokens, P(SHARD)) + states,
        out_specs=(tokens, tokens, P()) + states,
        check_vma=False,
    )
```

```python
import functools

import jax
import jax.numpy as jnp
from jax import lax
from jax.experimental import pallas as pl
from jax.experimental.pallas import tpu as pltpu
from jax.sharding import Mesh
from jax.sharding import PartitionSpec as P

D = 2560
H = 32
KV = 8
HD = 80
FF = 7168
STEP = 8


norm_epsilon = 1e-05
rope_theta = 1000000.0
masked_score = -1e30
clip_limit = 1.0
beta_first = 0.9
beta_second = 0.95
adam_epsilon = 1e-08
weight_decay = 0.1

HIGH, LOW, CONTEXT, TENSOR = "high", "low", "context", "tensor"
SHARD = (HIGH, LOW)
AXES = (HIGH, LOW, CONTEXT, TENSOR)
SWAP, STACK, SPREAD, COLLECT, TOTAL = "swap", "stack", "spread", "collect", "total"
MLP_GROUP = (CONTEXT,)
MLP_GATHER = (HIGH, LOW)
MESH = pl.DeviceIdType.MESH
low = jnp.bfloat16
full = jnp.float32


def rope_tables(positions):
    half = HD // 2
    exponent = jnp.arange(half, dtype=full) * (2.0 / HD)
    frequency = rope_theta ** (-exponent)
    angles = positions.astype(full)[:, None] * frequency[None, :]
    angles = jnp.concatenate([angles, angles], axis=-1)
    return (jnp.cos(angles), jnp.sin(angles))


def rotate(values, cosine, sine):
    half = values.shape[-1] // 2
    turned = jnp.concatenate([-values[..., half:], values[..., :half]], axis=-1)
    return values * cosine + turned * sine


def unrotate(values, cosine, sine):
    half = values.shape[-1] // 2
    turned = jnp.concatenate([-values[..., half:], values[..., :half]], axis=-1)
    return values * cosine - turned * sine


def normalize(values):
    factor = lax.rsqrt(jnp.mean(values * values, axis=-1, keepdims=True) + norm_epsilon)
    return (values * factor, factor)


def norm_back(grad_scaled, scaled, factor):
    return factor * (grad_scaled - scaled * jnp.mean(grad_scaled * scaled, axis=-1, keepdims=True))


def adam_step(weight, first, second, grad, factor, rate, decay):
    grad = grad * factor
    first_new = beta_first * first + (1.0 - beta_first) * grad
    second_new = beta_second * second + (1.0 - beta_second) * grad * grad
    first_scale, second_scale = 1.0 / (1.0 - beta_first**STEP), 1.0 / (1.0 - beta_second**STEP)
    corrected = first_new * first_scale / (jnp.sqrt(second_new * second_scale) + adam_epsilon)
    return (first_new, second_new, weight - rate * (corrected + decay * weight))


def over(left_dim, right_dim, left, right):
    return lax.dot_general(left, right, (((left_dim,), (right_dim,)), ((), ())), preferred_element_type=full)


rows_by_cols = functools.partial(over, 1, 0)
rows_by_rows = functools.partial(over, 1, 1)
cols_by_cols = functools.partial(over, 0, 0)


class Link:
    def __init__(self, sizes, send, recv):
        self.sizes, self.send, self.recv, self.used = sizes, send, recv, 0
        self.place = tuple(lax.axis_index(axis) for axis in AXES)

    def device(self, offset):
        return {axis: here ^ by for axis, here, by in zip(AXES, self.place, offset)}

    def index(self, group):
        index = 0
        for axis, here in zip(AXES, self.place):
            if axis in group:
                index = index * self.sizes[axis] + here
        return index

    def greet(self, partners):
        barrier = pltpu.get_barrier_semaphore()
        for offset in partners:
            pl.semaphore_signal(barrier, inc=1, device_id=self.device(offset), device_id_type=MESH)
        pl.semaphore_wait(barrier, len(partners))

    def push(self, src, dst, offset):
        copy = pltpu.make_async_remote_copy(
            src_ref=src,
            dst_ref=dst,
            send_sem=self.send.at[self.used],
            recv_sem=self.recv.at[self.used],
            device_id=self.device(offset),
            device_id_type=MESH,
        )
        self.used += 1
        copy.start()
        return copy

    def keep(self, src, dst):
        copy = pltpu.make_async_copy(src, dst, self.send.at[self.used])
        self.used += 1
        copy.start()
        return copy


MATE = (0, 0, 0, 1)


def axis_sizes():
    return {axis: lax.axis_size(axis) for axis in AXES}


def size_of(sizes, group):
    size = 1
    for axis in group:
        size *= sizes[axis]
    return size


def along(sizes, group, k):
    offset = []
    for axis in reversed(AXES):
        by = 0
        if axis in group:
            k, by = divmod(k, sizes[axis])
        offset.append(by)
    return tuple(reversed(offset))


def partners_of(jobs, sizes):
    found = set()
    for job in jobs:
        for group in job[1:]:
            n = size_of(sizes, group)
            steps = [1 << i for i in range(n.bit_length() - 1)] if job[0] in (SPREAD, COLLECT) else range(1, n)
            found |= {along(sizes, group, k) for k in steps}
        if job[0] in (SPREAD, COLLECT):
            found.add(MATE)
    return sorted(found)


def lanes(width, count):
    tiles, start, runs = width // 128, 0, []
    for i in range(count):
        size = 128 * ((tiles + count - 1 - i) // count)
        runs.append((start, size))
        start += size
    return runs


def turns(n, width):
    bits = [1 << i for i in range(n.bit_length() - 1)]
    return [(pl.ds(*run), bits[i:] + bits[:i]) for i, run in enumerate(lanes(width, len(bits)))]


class Swap:
    copies = staticmethod(lambda sizes, job, n: n)

    def __init__(self, link, job, sources, target, extras):
        (src,), group = sources, job[-1]
        me = link.index(group)
        self.ends = [
            link.push(src.at[me ^ k], target.at[me], along(link.sizes, group, k))
            for k in range(1, size_of(link.sizes, group))
        ]
        self.ends.append(link.keep(src.at[me], target.at[me]))

    def step(self, turn):
        pass

    def finish(self):
        for end in self.ends:
            end.wait()


class Stack:
    copies = staticmethod(lambda sizes, job, n: n + size_of(sizes, job[1]))

    def __init__(self, link, job, sources, target, extras):
        (src,), (_, outer, inner) = sources, job
        slot = target.at[link.index(outer), link.index(inner)]
        self.pieces = [link.push(src, slot, along(link.sizes, inner, k)) for k in range(1, size_of(link.sizes, inner))]
        self.pieces.append(link.keep(src, slot))
        self.link, self.outer, self.target = link, outer, target

    def step(self, turn):
        pass

    def finish(self):
        for piece in self.pieces:
            piece.wait()
        link, row = self.link, self.target.at[self.link.index(self.outer)]
        ends = [
            link.push(row, row, along(link.sizes, self.outer, k)) for k in range(1, size_of(link.sizes, self.outer))
        ]
        for end in ends:
            end.wait()


class Spread:
    copies = staticmethod(lambda sizes, job, n: 2 + 2 * (n - 1) * (n.bit_length() - 1))

    def __init__(self, link, job, sources, target, extras):
        (self.src,), self.group = sources, job[-1]
        self.link, self.target = link, target
        self.routes = turns(size_of(link.sizes, self.group), self.src.shape[1])
        self.held = [[0] for _ in self.routes]
        self.flying = [[] for _ in self.routes]
        self.sent, self.ends = [], []
        self.step(0)
        self.ends.append(link.push(self.src, target.at[1, 0], MATE))
        self.ends.append(link.keep(self.src, target.at[0, 0]))

    def land(self, i):
        run = self.routes[i][0]
        for k, copy in self.flying[i]:
            copy.wait_recv()
            self.held[i].append(k)
            self.ends.append(self.link.push(self.target.at[0, k, :, run], self.target.at[1, k, :, run], MATE))
        self.flying[i] = []

    def step(self, turn):
        for i, (run, bits) in enumerate(self.routes):
            if turn >= len(bits):
                continue
            arrived = self.flying[i]
            for _, copy in arrived:
                copy.wait_recv()
            bit = bits[turn]
            offset = along(self.link.sizes, self.group, bit)
            held = self.held[i] + [k for k, _ in arrived]
            flying = []
            for k in held:
                src = self.src.at[:, run] if k == 0 else self.target.at[0, k, :, run]
                copy = self.link.push(src, self.target.at[0, k ^ bit, :, run], offset)
                flying.append((k ^ bit, copy))
                self.sent.append(copy)
            for k, _ in arrived:
                here, there = self.target.at[0, k, :, run], self.target.at[1, k, :, run]
                self.ends.append(self.link.push(here, there, MATE))
            self.held[i], self.flying[i] = held, flying

    def finish(self):
        for i, _ in enumerate(self.routes):
            self.land(i)
        for copy in self.sent:
            copy.wait_send()
        for end in self.ends:
            end.wait()


class Collect:
    copies = staticmethod(lambda sizes, job, n: n + (n - 1) * (n.bit_length() - 1))

    def __init__(self, link, job, sources, target, extras):
        (self.near, self.far), self.group = sources, job[-1]
        (self.mates, self.got), self.link, self.target = extras, link, target
        n = size_of(link.sizes, self.group)
        self.routes = turns(n, self.near.shape[2])
        self.left = [list(range(n)) for _ in self.routes]
        self.adds = [{k: [] for k in range(n)} for _ in self.routes]
        self.places = [0 for _ in self.routes]
        self.sent = []
        self.crossed = set()
        self.crossing = {k: link.push(self.far.at[k], self.mates.at[k], MATE) for k in reversed(range(n))}

    def value(self, i, k):
        run = self.routes[i][0]
        if k not in self.crossed:
            self.crossing[k].wait_recv()
            self.crossed.add(k)
        total = self.near[k, :, run] + self.mates[k, :, run].astype(full)
        for place, copy in self.adds[i][k]:
            copy.wait_recv()
            total = total + self.got[place, :, run].astype(full)
        return total

    def step(self, turn):
        for i, (run, bits) in enumerate(self.routes):
            if turn >= len(bits):
                continue
            bit = bits[turn]
            offset = along(self.link.sizes, self.group, bit)
            for k in [k for k in self.left[i] if k & bit]:
                self.mates[k, :, run] = self.value(i, k).astype(low)
                place = self.places[i]
                copy = self.link.push(self.mates.at[k, :, run], self.got.at[place, :, run], offset)
                self.adds[i][k ^ bit].append((place, copy))
                self.sent.append(copy)
                self.places[i] += 1
            self.left[i] = [k for k in self.left[i] if not k & bit]

    def finish(self):
        for i, (run, _) in enumerate(self.routes):
            self.target[:, run] = self.value(i, 0)
        for copy in self.sent + list(self.crossing.values()):
            copy.wait_send()


class Total:
    copies = staticmethod(lambda sizes, job, n: sum(size_of(sizes, group) for group in job[1:]))

    def __init__(self, link, job, sources, target, extras):
        (tile, array), (self.held,) = sources, extras
        self.link, self.groups, self.target, self.slot = link, list(job[1:]), target, 0
        values = array[...].astype(full)
        target[...] = tile[...] + jnp.sum(values * values)
        self.ask()

    def ask(self):
        link, held, slot, group = self.link, self.held, self.slot, self.groups.pop(0)
        n = size_of(link.sizes, group)
        held[slot] = self.target[...]
        self.pushes = [link.push(held.at[slot], held.at[slot + k], along(link.sizes, group, k)) for k in range(1, n)]

    def step(self, turn):
        pass

    def finish(self):
        while True:
            for push in self.pushes:
                push.wait()
            for k, _ in enumerate(self.pushes):
                self.target[...] += self.held[self.slot + 1 + k]
            self.slot += 1 + len(self.pushes)
            if not self.groups:
                return
            self.ask()


KINDS = {SWAP: Swap, STACK: Stack, SPREAD: Spread, COLLECT: Collect, TOTAL: Total}
EXTRAS = {COLLECT: 2, TOTAL: 1}


def bundle_kernel(jobs, sizes, *refs):
    refs = list(refs)
    take = lambda count: [refs.pop(0) for _ in range(count)]
    sources = [take(2 if job[0] in EXTRAS else 1) for job in jobs]
    targets = [take(1)[0] for job in jobs]
    extras = [take(EXTRAS.get(job[0], 0)) for job in jobs]
    link = Link(sizes, *refs)
    link.greet(partners_of(jobs, sizes))
    running = [KINDS[job[0]](link, job, *rest) for job, *rest in zip(jobs, sources, targets, extras)]
    most = max(size_of(sizes, job[-1]).bit_length() - 1 for job in jobs)
    for turn in range(most):
        for job, work in zip(jobs, running):
            if job[0] == COLLECT or turn:
                work.step(turn)
    for work in running:
        if not isinstance(work, Swap):
            work.finish()
    for work in running:
        if isinstance(work, Swap):
            work.finish()


def whole_in_vmem():
    return pl.BlockSpec(memory_space=pltpu.VMEM)


def talking(number, mib):
    return pltpu.CompilerParams(collective_id=number, has_side_effects=True, vmem_limit_bytes=mib * 2**20)


def bundle(number, micros, *jobs):
    sizes = axis_sizes()
    anywhere = pl.BlockSpec(memory_space=pl.ANY)
    flat, in_specs, out_specs, shapes, scratch, copies, held = [], [], [], [], [], 0, 0
    for *job, array in jobs:
        kind, n = job[0], size_of(sizes, job[-1])
        copies += KINDS[kind].copies(sizes, job, n)
        if kind == COLLECT:
            near, far = array
            flat += [near, far]
            in_specs += [whole_in_vmem(), anywhere]
            out_specs.append(whole_in_vmem())
            shapes.append(jax.ShapeDtypeStruct(near.shape[1:], full))
            scratch += [pltpu.VMEM(far.shape, low), pltpu.VMEM((n - 1,) + far.shape[1:], low)]
            held += 10 * near.size
            continue
        if kind == TOTAL:
            flat += array
            in_specs += [whole_in_vmem()] * 2
            out_specs.append(whole_in_vmem())
            shapes.append(jax.ShapeDtypeStruct(array[0].shape, full))
            scratch.append(pltpu.VMEM((KINDS[kind].copies(sizes, job, n),) + array[0].shape, full))
            held += 2 * array[1].size
            continue
        flat.append(array)
        in_specs.append(anywhere)
        out_specs.append(anywhere)
        shape = array.shape
        if kind == STACK:
            shape = (size_of(sizes, job[1]), n) + shape
        elif kind == SPREAD:
            shape = (2, n) + shape
        shapes.append(jax.ShapeDtypeStruct(shape, array.dtype))
    return pl.pallas_call(
        functools.partial(bundle_kernel, tuple(tuple(job[:-1]) for job in jobs), sizes),
        out_shape=shapes,
        in_specs=in_specs,
        out_specs=out_specs,
        scratch_shapes=scratch + [pltpu.SemaphoreType.DMA((copies,)), pltpu.SemaphoreType.DMA((copies,))],
        compiler_params=talking(number, 6 + held // 2**20),
        cost_estimate=pl.CostEstimate(flops=int(micros * 8e8), bytes_accessed=0, transcendentals=0),
    )(*flat)


def halves(products, group):
    n = lax.axis_size(group)
    half = products[0][0].shape[0] // 2

    def part(start):
        total = 0.0
        for left, right in products:
            total = total + rows_by_rows(left[start : start + half], right)
        return total.reshape(n, half // n, -1)

    return part(0), part(half).astype(low)


PLANE = (CONTEXT, TENSOR)


def fold_kernel(sizes, part_ref, sum_ref, inner, work, outer, send, recv):
    link = Link(sizes, send, recv)
    plane, shards = size_of(sizes, PLANE), size_of(sizes, SHARD)
    link.greet([along(sizes, group, k) for group in (PLANE, SHARD) for k in range(1, size_of(sizes, group))])
    s, c = link.index(SHARD), link.index((CONTEXT,))
    pushes = [
        link.push(part_ref.at[c ^ (k // sizes[TENSOR])], inner.at[k - 1], along(sizes, PLANE, k))
        for k in range(1, plane)
    ]
    work[...] = part_ref[c]
    for k, push in enumerate(pushes):
        push.wait()
        work[...] += inner[k]
    pushes = [link.push(work.at[s ^ k], outer.at[k - 1], along(sizes, SHARD, k)) for k in range(1, shards)]
    sum_ref[...] = work[s]
    for k, push in enumerate(pushes):
        push.wait()
        sum_ref[...] += outer[k]


def fold(part, number):
    sizes = axis_sizes()
    plane, shards = size_of(sizes, PLANE), size_of(sizes, SHARD)
    return pl.pallas_call(
        functools.partial(fold_kernel, sizes),
        out_shape=jax.ShapeDtypeStruct(part.shape[2:], full),
        in_specs=[whole_in_vmem()],
        out_specs=whole_in_vmem(),
        scratch_shapes=[
            pltpu.VMEM((plane - 1,) + part.shape[1:], full),
            pltpu.VMEM(part.shape[1:], full),
            pltpu.VMEM((shards - 1,) + part.shape[2:], full),
            pltpu.SemaphoreType.DMA((plane + shards,)),
            pltpu.SemaphoreType.DMA((plane + shards,)),
        ],
        compiler_params=talking(number, 8),
    )(part)


def adam_mlp_kernel(chunks, rates, factor_ref, *refs):
    parts, pair, down, outs = refs[: len(chunks)], refs[2:5], refs[5:8], refs[8:]
    count = parts[0].shape[0]
    block = down[0].shape[1] // count
    for part, (start, stop) in zip(parts, chunks):
        size = stop - start
        for owner in range(count):
            cols = slice(owner * block + start, owner * block + stop)
            for k in range(3):
                where = (slice(None), k, cols) if k < 2 else (slice(None), cols)
                states, results, rate = (pair, outs[:3], rates[0]) if k < 2 else (down, outs[3:], rates[1])
                grad = part[owner, :, k * size : (k + 1) * size].astype(full)
                values = adam_step(*(ref[where] for ref in states), grad, factor_ref[0], rate, weight_decay)
                for out, value in zip(results, (values[0], values[1], values[2])):
                    out[where] = value


def adam_mlp(parts, chunks, pair, down, factor, rates):
    rows = down[0].shape[0]
    step = 32 if rows % 32 == 0 else rows
    thick = pl.BlockSpec((step,) + pair[0].shape[1:], lambda i: (i, 0, 0))
    flat = pl.BlockSpec((step,) + down[0].shape[1:], lambda i: (i, 0))
    grads = [pl.BlockSpec((part.shape[0], step, part.shape[2]), lambda i: (0, i, 0)) for part in parts]
    shapes = [jax.ShapeDtypeStruct(array.shape, full) for array in (*pair, *down)]
    return pl.pallas_call(
        functools.partial(adam_mlp_kernel, chunks, rates),
        grid=(rows // step,),
        out_shape=shapes,
        in_specs=[pl.BlockSpec(memory_space=pltpu.SMEM)] + grads + [thick] * 3 + [flat] * 3,
        out_specs=[thick] * 3 + [flat] * 3,
        compiler_params=pltpu.CompilerParams(vmem_limit_bytes=58 * 2**20),
    )(factor.reshape(1), *parts, *pair, *down)


def adam_attn_kernel(head_cols, rates, factor_ref, part, *refs):
    states, outs, grads = refs[:6], refs[6:12], refs[12:]
    owners = part.shape[0]
    for i, start in ((0, 0), (1, head_cols)):
        grad = grads[i]
        size = grad.shape[1] // owners
        for owner in range(owners):
            grad[:, owner * size : (owner + 1) * size] = part[owner, :, start : start + size].astype(full)
        old, new = states[3 * i : 3 * i + 3], outs[3 * i : 3 * i + 3]
        values = adam_step(*(ref[...] for ref in old), grad[...], factor_ref[0], rates[i], weight_decay)
        for out, value in zip(new, values):
            out[...] = value


def adam_attn(part, head_cols, weights, factor, rates):
    rows = weights[0].shape[0]
    step = 32 if rows % 32 == 0 else rows
    blocks = [pl.BlockSpec((step, array.shape[1]), lambda i: (i, 0)) for array in weights]
    grad = pl.BlockSpec((part.shape[0], step, part.shape[2]), lambda i: (0, i, 0))
    return pl.pallas_call(
        functools.partial(adam_attn_kernel, head_cols, rates),
        grid=(rows // step,),
        out_shape=[jax.ShapeDtypeStruct(array.shape, full) for array in weights],
        in_specs=[pl.BlockSpec(memory_space=pltpu.SMEM), grad] + blocks,
        out_specs=blocks,
        scratch_shapes=[pltpu.VMEM((step, weights[i].shape[1]), full) for i in (0, 3)],
        compiler_params=pltpu.CompilerParams(vmem_limit_bytes=58 * 2**20),
    )(factor.reshape(1), part, *weights)


def swap_later(blocks, axis):
    me, size = lax.axis_index(axis), lax.axis_size(axis)

    def block(values, j):
        return lax.dynamic_index_in_dim(values, j, 0, keepdims=False)

    kept = [block(blocks, me)]
    for k in range(1, size):
        kept.append(lax.ppermute(block(blocks, me ^ k), axis, [(i, i ^ k) for i in range(size)]))
    kept = jnp.stack(kept)
    return jnp.stack([block(kept, me ^ j) for j in range(size)])


def weight_grads_kernel(count, dim, *refs):
    lefts, rights, out = refs[:count], refs[count:-1], refs[-1]
    start = 0
    for left, right in zip(lefts, rights):
        size = right.shape[1 - dim]
        out[:, start : start + size] = over(0, dim, left[...], right[...]).astype(low)
        start += size


def weight_grads(pairs, dim):
    tokens, width = pairs[0][0].shape
    cols = sum(right.shape[1 - dim] for _, right in pairs)
    step = 256
    return pl.pallas_call(
        functools.partial(weight_grads_kernel, len(pairs), dim),
        grid=(width // step,),
        out_shape=jax.ShapeDtypeStruct((width, cols), low),
        in_specs=[pl.BlockSpec((tokens, step), lambda i: (0, i))] * len(pairs)
        + [pl.BlockSpec(right.shape, lambda i: (0, 0)) for _, right in pairs],
        out_specs=pl.BlockSpec((step, cols), lambda i: (i, 0)),
        compiler_params=pltpu.CompilerParams(vmem_limit_bytes=48 * 2**20),
        cost_estimate=pl.CostEstimate(flops=2 * tokens * width * cols, bytes_accessed=0, transcendentals=0),
    )(*(left for left, _ in pairs), *(right for _, right in pairs))


def attend(query, key, value, allowed):
    scores = rows_by_rows(query, key) * HD ** (-0.5)
    scores = jnp.where(allowed, scores, masked_score)
    row_max = jnp.max(scores, axis=-1, keepdims=True)
    expanded = jnp.exp(scores - row_max)
    row_total = jnp.sum(expanded, axis=-1, keepdims=True)
    probs = (expanded / row_total).astype(low)
    return rows_by_cols(probs, value), row_max + jnp.log(row_total)


def attend_back(query, key, value, grad, log_total, allowed):
    scores = rows_by_rows(query, key) * HD ** (-0.5)
    scores = jnp.where(allowed, scores, masked_score)
    probs = jnp.exp(scores - log_total)
    grad_value = cols_by_cols(probs.astype(low), grad)
    grad_probs = rows_by_rows(grad, value)
    delta = jnp.sum(probs * grad_probs, axis=-1, keepdims=True)
    grad_scores = (probs * (grad_probs - delta)).astype(low)
    grad_query = rows_by_cols(grad_scores, key) * HD ** (-0.5)
    grad_key = cols_by_cols(grad_scores, query) * HD ** (-0.5)
    return grad_query, grad_key, grad_value


def body(
    hidden_in,
    out_grad,
    prefix_len,
    qkv_weight,
    qkv_m,
    qkv_v,
    out_weight,
    out_m,
    out_v,
    gate_up_weight,
    gate_up_m,
    gate_up_v,
    down_weight,
    down_m,
    down_v,
    gains,
    gains_m,
    gains_v,
):
    _, local_len, width = hidden_in.shape
    shards, contexts, tensors = (lax.axis_size(group) for group in (SHARD, CONTEXT, TENSOR))
    context, tensor = lax.axis_index(CONTEXT), lax.axis_index(TENSOR)
    group_size = lax.axis_size(MLP_GROUP)
    rows = qkv_weight.shape[0]
    group = H // KV
    head_cols = (group + 2) * HD
    own = local_len // tensors
    ff_block = down_weight.shape[1] // group_size
    ff_first = ff_block // 2 // 128 * 128 or ff_block // 2
    chunks = ((0, ff_first), (ff_first, ff_block))

    def to_blocks(weight, count):
        return jnp.moveaxis(weight.astype(low).reshape(rows, count, -1), 1, 0)

    (attn_part,) = bundle(
        0,
        16,
        (
            SWAP,
            (CONTEXT,),
            jnp.concatenate([to_blocks(qkv_weight, contexts), to_blocks(out_weight, contexts)], axis=2),
        ),
    )
    gain_values, attn_part = lax.optimization_barrier((lax.reduce_precision(gains, 8, 7), attn_part))
    (gain_blocks,) = bundle(9, 10, (STACK, SHARD, (CONTEXT,), gain_values))
    attn_full = lax.all_gather(attn_part.reshape(contexts * rows, -1), SHARD, axis=0, tiled=True)
    qkv_full, out_full = attn_full[:, :head_cols], attn_full[:, head_cols:]
    gain_rows = gain_blocks.reshape(shards * contexts, 2, rows).transpose(1, 0, 2).reshape(2, width)
    gain_attn, gain_mlp = gain_rows[0], gain_rows[1]
    inputs = lax.dynamic_slice_in_dim(hidden_in[0], tensor * own, own, 0).astype(full)
    grad_low = lax.dynamic_slice_in_dim(out_grad[0], tensor * own, own, 0)
    cotangent = grad_low.astype(full)
    scaled_one, factor_one = normalize(inputs)

    gate_up_blocks = gate_up_weight.astype(low).reshape(rows, 2, group_size, ff_block).transpose(2, 0, 1, 3)
    down_blocks = to_blocks(down_weight, group_size)

    def chunk_blocks(start, stop):
        pair = gate_up_blocks[:, :, :, start:stop]
        return jnp.concatenate([pair[:, :, 0], pair[:, :, 1], down_blocks[:, :, start:stop]], axis=2)

    def gather_mlp(part):
        return lax.all_gather(part.reshape(group_size * rows, -1), MLP_GATHER, axis=0, tiled=True)

    normed_one, part_one = bundle(
        1,
        60,
        (SPREAD, (CONTEXT,), (scaled_one * gain_attn).astype(low)),
        (SWAP, MLP_GROUP, chunk_blocks(*chunks[0])),
    )
    normed_one = normed_one.reshape(-1, width)
    mlp_full = [gather_mlp(part_one)]

    places = jnp.arange(contexts, dtype=jnp.int32) ^ context
    cores = jnp.arange(tensors, dtype=jnp.int32) ^ tensor
    positions = (
        places[None, :, None] * local_len
        + cores[:, None, None] * own
        + jnp.arange(own, dtype=jnp.int32)[None, None, :]
    ).reshape(-1)
    cosine, sine = rope_tables(positions)
    allowed = (positions[None, :] <= positions[:, None]) | (positions[None, :] < prefix_len[0])

    joined = rows_by_cols(normed_one, qkv_full)
    parts = [joined[:, i * HD : (i + 1) * HD] for i in range(group + 2)]
    queries = [rotate(part, cosine, sine).astype(low) for part in parts[:group]]
    key = rotate(parts[group], cosine, sine).astype(low)
    value = parts[group + 1].astype(low)
    mixed, log_total = zip(*[attend(query, key, value, allowed) for query in queries])
    attended = jnp.concatenate([part.astype(low) for part in mixed], axis=1)
    branch, part_two, grad_branch_mlp = bundle(
        2,
        80,
        (COLLECT, (CONTEXT,), halves([(attended, out_full)], (CONTEXT,))),
        (SWAP, MLP_GROUP, chunk_blocks(*chunks[1])),
        (SPREAD, MLP_GROUP, grad_low),
    )
    grad_branch_mlp = grad_branch_mlp.reshape(-1, width)
    mlp_full.append(gather_mlp(part_two))
    middle = inputs + branch
    scaled_two, factor_two = normalize(middle)
    (normed_two,) = bundle(3, 40, (SPREAD, MLP_GROUP, (scaled_two * gain_mlp).astype(low)))
    normed_two = normed_two.reshape(-1, width)

    sums, back_products, out_products = [], [], []
    for place, (start, stop) in enumerate(chunks):
        size = stop - start
        weights = mlp_full[place]
        pair_weights, down_weights = weights[:, : 2 * size], weights[:, 2 * size :]
        gate_up = rows_by_cols(normed_two, pair_weights)
        gate, up_part = gate_up[:, :size], gate_up[:, size:]
        sigmoid_gate = jax.nn.sigmoid(gate)
        activated = gate * sigmoid_gate
        hidden = (activated * up_part).astype(low)
        grad_hidden = rows_by_cols(grad_branch_mlp, down_weights)
        grad_gate = grad_hidden * up_part * sigmoid_gate * (1.0 + gate * (1.0 - sigmoid_gate))
        grad_up = grad_hidden * activated
        grad_rows = jnp.concatenate([grad_gate, grad_up], axis=1).astype(low)
        grads = weight_grads([(normed_two, grad_rows), (grad_branch_mlp, hidden)], 0)
        grad_rows, grads = lax.optimization_barrier((grad_rows, grads))
        if sums:
            grads, sums[0] = lax.optimization_barrier((grads, sums[0]))
        else:
            grads, mlp_full[1] = lax.optimization_barrier((grads, mlp_full[1]))
        sums.append(lax.psum_scatter(grads, MLP_GATHER, scatter_dimension=0, tiled=True))
        back_products.append((grad_rows, pair_weights))
        out_products.append((hidden, down_weights))

    (grad_normed_two,) = bundle(4, 40, (COLLECT, MLP_GROUP, halves(back_products, MLP_GROUP)))
    grad_gain_mlp = jnp.sum(grad_normed_two * scaled_two, axis=0)
    grad_middle = cotangent + norm_back(grad_normed_two * gain_mlp, scaled_two, factor_two)
    grad_middle, sums[0] = lax.optimization_barrier((grad_middle, sums[0]))
    grad_branch_attn, mlp_branch, parts_one = bundle(
        5,
        80,
        (SPREAD, (CONTEXT,), grad_middle.astype(low)),
        (COLLECT, MLP_GROUP, halves(out_products, MLP_GROUP)),
        (SWAP, MLP_GROUP, sums[0].reshape(group_size, rows, -1)),
    )
    out_own = (middle + mlp_branch).astype(low)
    grad_branch_attn = grad_branch_attn.reshape(-1, width)
    grad_attended = rows_by_cols(grad_branch_attn, out_full).astype(low)

    grad_queries = []
    grad_key = 0.0
    grad_value = 0.0
    for i in range(group):
        grad_query, key_part, value_part = attend_back(
            queries[i], key, value, grad_attended[:, i * HD : (i + 1) * HD], log_total[i], allowed
        )
        grad_queries.append(unrotate(grad_query, cosine, sine))
        grad_key = grad_key + key_part
        grad_value = grad_value + value_part
    grad_joined = jnp.concatenate(
        grad_queries + [unrotate(grad_key, cosine, sine), grad_value], axis=1
    ).astype(low)
    grad_attn = weight_grads([(normed_one, grad_joined.T), (grad_branch_attn, attended.T)], 1)
    grad_joined, grad_attn = lax.optimization_barrier((grad_joined, grad_attn))
    grad_attn, sum_two = lax.optimization_barrier((grad_attn, sums[1]))
    attn_sum = lax.psum_scatter(grad_attn, SHARD, scatter_dimension=0, tiled=True)
    grad_normed_one, parts_two = bundle(
        6,
        55,
        (COLLECT, (CONTEXT,), halves([(grad_joined, qkv_full)], (CONTEXT,))),
        (SWAP, MLP_GROUP, sum_two.reshape(group_size, rows, -1)),
    )
    grad_gain_attn = jnp.sum(grad_normed_one * scaled_one, axis=0)
    grad_inputs = grad_middle + norm_back(grad_normed_one * gain_attn, scaled_one, factor_one)
    grad_own = grad_inputs.astype(low)

    def both_cores(values):
        other = lax.ppermute(values, TENSOR, [(0, 1), (1, 0)])
        return jnp.where(tensor == 0, jnp.concatenate([values, other]), jnp.concatenate([other, values]))[None]

    hidden_out = both_cores(out_own)
    hidden_grad = both_cores(grad_own)
    gain_part = jnp.stack([grad_gain_attn, grad_gain_mlp]).reshape(2, shards, contexts, rows)
    owned_gains = fold(gain_part.transpose(2, 1, 0, 3), 7)

    squares = jnp.sum(owned_gains * owned_gains) / tensors
    for owned in (sums[0], sum_two):
        owned = owned.astype(full)
        squares = squares + jnp.sum(owned * owned)
    attn_sum, squares, hidden_out, hidden_grad = lax.optimization_barrier(
        (attn_sum, squares, hidden_out, hidden_grad)
    )
    (total,) = bundle(8, 10, (TOTAL, PLANE, SHARD, (jnp.full((8, 128), squares, full), attn_sum)))
    attn_sum, total = lax.optimization_barrier((attn_sum, total))
    attn_parts = swap_later(attn_sum.reshape(contexts, rows, -1), CONTEXT)
    grad_norm = jnp.sqrt(total[0, 0])
    factor = jnp.minimum(1.0, clip_limit / grad_norm)

    mlp_out = adam_mlp(
        (parts_one, parts_two),
        chunks,
        (gate_up_weight, gate_up_m, gate_up_v),
        (down_weight, down_m, down_v),
        factor,
        (2.0 * D ** (-0.5), 2.0 * FF ** (-0.5)),
    )
    attn_parts, first_out = lax.optimization_barrier((attn_parts, mlp_out[-1]))
    attn_out = adam_attn(
        attn_parts,
        head_cols,
        (qkv_weight, qkv_m, qkv_v, out_weight, out_m, out_v),
        factor,
        (2.0 * (D / 2) ** (-0.5), 2.0 * (H * HD / 16) ** (-0.5)),
    )
    gains_out = adam_step(gains, gains_m, gains_v, owned_gains, factor, 0.8, 0.0)
    return (hidden_out, hidden_grad, grad_norm, *attn_out, *mlp_out[:-1], first_out, *gains_out)


def solution(mesh):
    shards, contexts, tensors = mesh.devices.shape
    fine = Mesh(mesh.devices.reshape(shards // 2, 2, contexts, tensors), AXES)
    tokens = P(SHARD, CONTEXT, None)
    rows = (HIGH, LOW, CONTEXT)
    flat = P(rows, TENSOR)
    paired = P(rows, None, TENSOR)
    gains = P(None, rows)
    states = (flat,) * 6 + (paired,) * 3 + (flat,) * 3 + (gains,) * 3
    return jax.shard_map(
        body,
        mesh=fine,
        in_specs=(tokens, tokens, P(SHARD)) + states,
        out_specs=(tokens, tokens, P()) + states,
        check_vma=False,
    )
```
